128 devices in a mesh: graphs: 32 (over x, z, y_hi), heads: 4 (over y_lo, core).
Axes of the slice: x: 4, y: 4 (y_hi: 2, y_lo: 2; y = y_hi * 2 + y_lo), z: 4, core: 2. Of those that a mesh axis runs over, the one named last changes fastest.
Arguments:
- nodes: bfloat16 [1024, 100, 300], P(('graphs', 'heads')), may hold values from -6 to 6
- edge_table: bfloat16 [512, 300], replicated, may hold values from -6 to 6
- edge_index: int32 [1024, 100], P(('graphs', 'heads')), may hold values from 0 to 511
- star_sizes: int32 [1024], P('graphs'), may hold values from 2 to 100, as said below
- leaf_drop: int32 [1024, 100], P('graphs'), may hold values 0 or 1
- missing: int32 [1024, 100], P(('graphs', 'heads')), may hold values 0 or 1
- w_query: bfloat16 [2, 300, 300], P(None, None, 'heads'), may hold values from -0.375 to 0.375
- w_key: bfloat16 [2, 300, 300], P(None, None, 'heads'), may hold values from -0.375 to 0.375
- w_value: bfloat16 [2, 300, 300], P(None, None, 'heads'), may hold values from -0.375 to 0.375
- w_out: bfloat16 [2, 300, 300], replicated, may hold values from -0.5 to 0.5
- b_out: float32 [2, 300], replicated, may hold values from -1.8 to 1.8
- ln1_gain: float32 [2, 300], replicated, may hold values from 0.5 to 1.5
- ln1_bias: float32 [2, 300], replicated, may hold values from -1.8 to 1.8
- w_ff1: bfloat16 [2, 300, 1200], replicated, may hold values from -0.375 to 0.375
- b_ff1: float32 [2, 1200], replicated, may hold values from -1.8 to 1.8
- w_ff2: bfloat16 [2, 1200, 300], replicated, may hold values from -0.25 to 0.25
- b_ff2: float32 [2, 300], replicated, may hold values from -1.8 to 1.8
- ln2_gain: float32 [2, 300], replicated, may hold values from 0.5 to 1.5
- ln2_bias: float32 [2, 300], replicated, may hold values from -1.8 to 1.8
- w_edge: bfloat16 [2, 300, 300], replicated, may hold values from -0.375 to 0.375
- b_edge: float32 [2, 300], replicated, may hold values from -1.8 to 1.8
- d_nodes_out: bfloat16 [1024, 100, 300], P(('graphs', 'heads')), may hold values from -6 to 6
- d_edges_out: bfloat16 [1024, 100, 300], P(('graphs', 'heads')), may hold values from -6 to 6
Outputs:
- nodes_out: bfloat16 [1024, 100, 300], P(('graphs', 'heads'))
- edges_out: bfloat16 [1024, 100, 300], P(('graphs', 'heads'))
- grad_nodes: float32 [1024, 100, 300], P(('graphs', 'heads'))
- grad_edge_table: float32 [512, 300], replicated
- grad_w_query: float32 [2, 300, 300], P(None, None, 'heads')
- grad_w_key: float32 [2, 300, 300], P(None, None, 'heads')
- grad_w_value: float32 [2, 300, 300], P(None, None, 'heads')
- grad_w_out: float32 [2, 300, 300], replicated
- grad_b_out: float32 [2, 300], replicated
- grad_ln1_gain: float32 [2, 300], replicated
- grad_ln1_bias: float32 [2, 300], replicated
- grad_w_ff1: float32 [2, 300, 1200], replicated
- grad_b_ff1: float32 [2, 1200], replicated
- grad_w_ff2: float32 [2, 1200, 300], replicated
- grad_b_ff2: float32 [2, 300], replicated
- grad_ln2_gain: float32 [2, 300], replicated
- grad_ln2_bias: float32 [2, 300], replicated
- grad_w_edge: float32 [2, 300, 300], replicated
- grad_b_edge: float32 [2, 300], replicated
The draws below stay inside these ranges and needn't reach their ends.
Inputs may be any that keep to these rules, and one draw needn't show every extreme that they name: `star_sizes`: the used slots of a star are the center and its leaves; some star uses all 100.
All inputs are finite; a program needn't handle non-finite values. No bound on the sum of `leaf_drop` or of `missing` on one device may be relied on, other than what follows from the above.
Results may differ from the reference program's by a relative error of at most 0.033.
Values may be sent and summed in bfloat16 or wider, within the bound.
No kernel may reach another device: no remote copies, remote signals or barrier semaphores. Data moves between devices by JAX's collectives and lax.ppermute only.
A program may use at most 192 MiB of HBM per device.

```python
import math
import jax
import jax.numpy as jnp
from jax import lax

D = 300
NH = 12
HD = 25
FF = 1200
SLOTS = 100
NCOL = 512
LAYERS = 2
STARS = 1024


def draw_star_sizes(key, part):
    key = jax.random.fold_in(key, 11)
    first, second = jax.random.split(key)
    sizes = jax.random.randint(first, (STARS,), 2, SLOTS + 1)
    chosen = jax.random.randint(second, (), 0, STARS)
    return jnp.where(jnp.arange(STARS) == chosen, SLOTS, sizes).astype(jnp.int32)


def plant(values, rng, low, high):
    longest = values.shape.index(max(values.shape))
    spots = []
    for shift in (0, 1):
        where = [jax.random.randint(jax.random.fold_in(rng, axis), (), 0, length) for axis, length in enumerate(values.shape)]
        where[longest] = (where[longest] + shift) % values.shape[longest]
        spots.append(tuple(where))
    return values.at[spots[0]].set(low).at[spots[1]].set(high)


def block_levels(rng, shape, shards, least, largest):
    factor_of = 1.0
    for position, parts in shards:
        draws = jax.random.uniform(jax.random.fold_in(jax.random.fold_in(rng, 6), position), (parts,), jnp.float32, least / len(shards), largest / len(shards))
        factor_of = factor_of * jnp.repeat(jnp.exp(draws), shape[position] // parts).reshape((-1,) + (1,) * (len(shape) - 1 - position))
    return factor_of


def scatter_about(rng, extent, deviation, limit, cuts=(), kind=jnp.bfloat16):
    entries = jax.random.normal(rng, extent, jnp.float32) * deviation
    if len(cuts) > 0:
        entries = block_levels(rng, extent, cuts, -0.22, 0.18) * entries
    return jnp.clip(entries, min=-limit, max=limit).astype(kind)


def setup_inputs(seed: int = 0) -> dict:
    streams_of = jax.random.split(jax.random.key(seed), 24)
    return {
        "nodes": scatter_about(streams_of[0], (STARS, SLOTS, D), 1.0, 6.0, ((0, 128),)),
        "edge_table": scatter_about(streams_of[1], (NCOL, D), 1.0, 6.0),
        "edge_index": plant(jax.random.randint(streams_of[2], (STARS, SLOTS), 0, NCOL), jax.random.fold_in(streams_of[2], 1), 0, NCOL - 1).astype(jnp.int32),
        "star_sizes": draw_star_sizes(jax.random.fold_in(streams_of[23], 71), 0),
        "leaf_drop": plant((jax.random.randint(streams_of[4], (STARS, SLOTS), 0, 6) < 1).astype(jnp.int32), jax.random.fold_in(streams_of[4], 1), 0, 1),
        "missing": plant((jax.random.randint(streams_of[5], (STARS, SLOTS), 0, 8) < 1).astype(jnp.int32), jax.random.fold_in(streams_of[5], 1), 0, 1),
        "w_query": scatter_about(streams_of[6], (LAYERS, D, D), D ** -0.5, 0.375, ((2, 4),)),
        "w_key": scatter_about(streams_of[7], (LAYERS, D, D), D ** -0.5, 0.375, ((2, 4),)),
        "w_value": scatter_about(streams_of[8], (LAYERS, D, D), D ** -0.5, 0.375, ((2, 4),)),
        "w_out": scatter_about(streams_of[9], (LAYERS, D, D), (D // 2) ** -0.5, 0.5),
        "b_out": scatter_about(streams_of[10], (LAYERS, D), 0.3, 1.8, (), jnp.float32),
        "ln1_gain": jnp.clip(1.0 + 0.1 * jax.random.normal(streams_of[11], (LAYERS, D), jnp.float32), 0.5, 1.5),
        "ln1_bias": scatter_about(streams_of[12], (LAYERS, D), 0.3, 1.8, (), jnp.float32),
        "w_ff1": scatter_about(streams_of[13], (LAYERS, D, FF), D ** -0.5, 0.375),
        "b_ff1": scatter_about(streams_of[14], (LAYERS, FF), 0.3, 1.8, (), jnp.float32),
        "w_ff2": scatter_about(streams_of[15], (LAYERS, FF, D), (FF // 2) ** -0.5, 0.25),
        "b_ff2": scatter_about(streams_of[16], (LAYERS, D), 0.3, 1.8, (), jnp.float32),
        "ln2_gain": jnp.clip(1.0 + 0.1 * jax.random.normal(streams_of[17], (LAYERS, D), jnp.float32), 0.5, 1.5),
        "ln2_bias": scatter_about(streams_of[18], (LAYERS, D), 0.3, 1.8, (), jnp.float32),
        "w_edge": scatter_about(streams_of[19], (LAYERS, D, D), D ** -0.5, 0.375),
        "b_edge": scatter_about(streams_of[20], (LAYERS, D), 0.3, 1.8, (), jnp.float32),
        "d_nodes_out": scatter_about(streams_of[21], (STARS, SLOTS, D), 1.0, 6.0, ((0, 128),)),
        "d_edges_out": scatter_about(streams_of[22], (STARS, SLOTS, D), 1.0, 6.0, ((0, 128),)),
    }


@jax.custom_vjp
def low(v):
    return lax.optimization_barrier(v.astype(jnp.bfloat16)).astype(jnp.float32)

@jax.custom_vjp
def low_back(v):
    return v

def low_keep(v):
    return (low(v), None)

def low_pass(kept, grad):
    return (grad,)

def back_keep(v):
    return (v, None)

def back_low(kept, grad):
    return (low(grad),)
low.defvjp(low_keep, low_pass)
low_back.defvjp(back_keep, back_low)

def matmul(left, right):
    return jnp.einsum('...i,ij->...j', left, right, precision=lax.Precision.HIGHEST)

def norm_rows(hidden, gain, bias):
    center = hidden - lax.optimization_barrier(jnp.mean(hidden, -1, keepdims=True))
    spread = lax.optimization_barrier(jnp.mean(center * center, -1, keepdims=True))
    return center * lax.rsqrt(spread + 1e-05) * gain + bias

def attend(queries, key_mod, value_mod, key_ok):
    scale = 1.0 / math.sqrt(HD)
    highest = lax.Precision.HIGHEST
    scores = jnp.einsum('bhe,bjhe->bhj', queries[:, 0], key_mod, precision=highest) * scale
    scores = jnp.where(key_ok[:, None, :], scores, -1e+30)
    top = lax.optimization_barrier(jnp.max(scores, -1, keepdims=True))
    expo = jnp.exp(scores - top)
    probs = expo / lax.optimization_barrier(jnp.sum(expo, -1, keepdims=True))
    center = jnp.einsum('bhj,bjhe->bhe', low(probs), value_mod, precision=highest)
    toward = lax.optimization_barrier(jnp.sum(queries * key_mod[:, 0:1], -1)) * scale
    itself = lax.optimization_barrier(jnp.sum(queries * key_mod, -1)) * scale
    upper = jnp.maximum(toward, itself)
    ex_center = jnp.exp(toward - upper)
    ex_self = jnp.exp(itself - upper)
    total = ex_center + ex_self
    leaf = low(ex_center / total)[..., None] * value_mod[:, 0:1] + low(ex_self / total)[..., None] * value_mod
    slot_ids = jnp.arange(SLOTS)
    return jnp.where(slot_ids[None, :, None, None] == 0, center[:, None], leaf)

def one_layer(state_x, state_e, weights, key_ok, valid):
    wq, wk, wv, wo, bo, gone, bone, wfa, bfa, wfb, bfb, gtwo, btwo, wedge, bedge = weights
    count = state_x.shape[0]
    nodes_low = low(state_x)
    edges_low = low(state_e)
    edges_att = low_back(edges_low)
    queries = low(low_back(matmul(nodes_low, wq)))
    key_mod = low(low_back(matmul(nodes_low, wk)) * edges_att)
    value_mod = low(low_back(matmul(nodes_low, wv)) * edges_att)
    shape = (count, SLOTS, NH, HD)
    attended = attend(queries.reshape(shape), key_mod.reshape(shape), value_mod.reshape(shape), key_ok)
    out_low = low(low_back(attended.reshape(count, SLOTS, D)))
    attn = low_back(matmul(out_low, wo) + bo)
    normed = norm_rows(state_x + attn, gone, bone)
    pre_act = low_back(matmul(low(normed), wfa) + bfa)
    ff_out = low_back(matmul(low(jax.nn.gelu(pre_act, approximate=False)), wfb) + bfb)
    result = norm_rows(normed + ff_out, gtwo, btwo) * valid[..., None]
    new_edges = low_back(matmul(edges_low, wedge) + bedge)
    return (result, new_edges)

def reference(nodes, edge_table, edge_index, star_sizes, leaf_drop, missing, w_query, w_key, w_value, w_out, b_out, ln1_gain, ln1_bias, w_ff1, b_ff1, w_ff2, b_ff2, ln2_gain, ln2_bias, w_edge, b_edge, d_nodes_out, d_edges_out):
    slot_ids = jnp.arange(SLOTS)
    inside = slot_ids[None, :] < star_sizes[:, None]
    valid = inside.astype(jnp.float32)
    key_ok = inside & ((slot_ids[None, :] == 0) | (leaf_drop == 0))
    present = ((slot_ids[None, :] == 0) | (missing == 0)).astype(jnp.float32)[..., None]
    params = tuple((t.astype(jnp.float32) for t in (nodes, edge_table, w_query, w_key, w_value, w_out, b_out, ln1_gain, ln1_bias, w_ff1, b_ff1, w_ff2, b_ff2, ln2_gain, ln2_bias, w_edge, b_edge)))

    def forward(nodes_f, table_f, *stacked):
        state_x = nodes_f * present
        state_e = low_back(jnp.take(table_f, edge_index, axis=0))
        for layer_no in range(LAYERS):
            weights = tuple((t[layer_no] for t in stacked))
            state_x, state_e = one_layer(state_x, state_e, weights, key_ok, valid)
        return (state_x, state_e)
    outputs, pullback = jax.vjp(forward, *params)
    grads = pullback((d_nodes_out.astype(jnp.float32), d_edges_out.astype(jnp.float32)))
    return (outputs[0].astype(jnp.bfloat16), outputs[1].astype(jnp.bfloat16), grads[0], grads[1], grads[2], grads[3], grads[4], grads[5], grads[6], grads[7], grads[8], grads[9], grads[10], grads[11], grads[12], grads[13], grads[14], grads[15], grads[16])
```

```python
import functools
import math

import jax
import jax.numpy as jnp
from jax import lax
from jax.experimental import pallas as pl
from jax.experimental.pallas import tpu as pltpu
from jax.sharding import Mesh, PartitionSpec as P

D = 300
DP = 384
FF = 1200
HD = 25
SLOTS = 100
STARS = 8
ROWS = STARS * SLOTS
HL = 128
NCOL = 512
SCALE = 1.0 / math.sqrt(HD)
CHUNK = 400
CHUNKS = ROWS // CHUNK
STRIP = 304
ROWS_L1 = 10240
ROWS_F0 = 6144
ROWS_T0 = 6144
F32 = jnp.float32
BF16 = jnp.bfloat16
MIB = 1 << 20


def mm(left, right):
    return lax.dot_general(left, right, (((1,), (0,)), ((), ())), preferred_element_type=F32)


def mm_nt(left, right):
    return lax.dot_general(left, right, (((1,), (1,)), ((), ())), preferred_element_type=F32)


def mm_tn(left, right):
    return lax.dot_general(left, right, (((0,), (0,)), ((), ())), preferred_element_type=F32)


def chunk_rows(index):
    return slice(index * CHUNK, (index + 1) * CHUNK)


def head_lanes():
    row = lax.broadcasted_iota(jnp.int32, (HL, DP), 0)
    lane = lax.broadcasted_iota(jnp.int32, (HL, DP), 1)
    offset = lane - (row & 15) * HD
    return (offset >= 0) & (offset < HD) & (lane < D)


def star_lanes(rows=ROWS, first=0):
    row = lax.broadcasted_iota(jnp.int32, (rows, HL), 0) + first
    lane = lax.broadcasted_iota(jnp.int32, (rows, HL), 1)
    return row - (lane >> 4) * SLOTS


def gelu_parts(x):
    y = jnp.abs(x)
    expo = jnp.exp(-0.5 * x * x)
    t = 1.0 / (1.0 + (0.3275911 * 0.7071067811865476) * y)
    poly = t * (
        0.5 * 0.254829592
        + t
        * (
            0.5 * -0.284496736
            + t * (0.5 * 1.421413741 + t * (0.5 * -1.453152027 + t * (0.5 * 1.061405429)))
        )
    )
    tail = poly * expo
    value = jnp.maximum(x, 0.0) - y * tail
    slope = tail - y * (expo * 0.3989422804014327)
    slope = jnp.where(x >= 0.0, 1.0 - slope, slope)
    return value, slope


def normalize(hidden):
    center = hidden - jnp.sum(hidden, -1, keepdims=True) * (1.0 / D)
    spread = jnp.sum(center * center, -1, keepdims=True) * (1.0 / D)
    root = lax.rsqrt(spread + 1e-05)
    return center * root, root


def norm_back(grad, gain, normed, root):
    scaled = grad * gain
    first = jnp.sum(scaled, -1, keepdims=True) * (1.0 / D)
    second = jnp.sum(scaled * normed, -1, keepdims=True) * (1.0 / D)
    return root * (scaled - first - normed * second)


def pad_lanes(value):
    return jnp.concatenate([value, jnp.zeros((value.shape[0], DP - D), value.dtype)], axis=1)


def put_centers(ref, value, index, mask):
    per = CHUNK // SLOTS
    for star in range(per):
        row = value[star * SLOTS : star * SLOTS + 1, :]
        at = (index * per + star) * 16
        block = jnp.where(mask[:16], jnp.broadcast_to(row, (16, DP)), 0.0)
        ref[at : at + 16, :] = block.astype(BF16)


def edge_kernel(
    cols, table, wedge, bedge, dedges, e0_out, e1_out, edges_out, back_out, dw_out, db_out, grad
):
    lane = lax.broadcasted_iota(jnp.int32, (CHUNK, NCOL), 1).astype(F32)
    for i in range(CHUNKS):
        rows = chunk_rows(i)
        one_hot = (cols[rows, 3:4] == lane).astype(BF16)
        e0 = mm(one_hot, table[...]).astype(BF16)
        e1 = (mm(e0, wedge[0]) + bedge[0:1]).astype(BF16)
        last = (mm(e1, wedge[1]) + bedge[1:2]).astype(BF16)
        e0_out[rows, :] = pad_lanes(e0)
        e1_out[rows, :] = pad_lanes(e1)
        for star in range(CHUNK // SLOTS):
            edges_out[i * (CHUNK // SLOTS) + star] = last[star * SLOTS : (star + 1) * SLOTS, :]
    for star in range(STARS):
        grad[star * SLOTS : (star + 1) * SLOTS, :] = dedges[star].astype(F32)
    db_out[...] = jnp.sum(grad[...], 0, keepdims=True)
    low = grad[...].astype(BF16)
    back_out[...] = mm_nt(low, wedge[1])
    dw_out[...] = mm_tn(e1_out[:, :D], low)


def layer_forward(x_in, weights, layer, e, keep, cols, sizes, x_out):
    w_qkv, w_out, b_out, g1, s1, w1, b1, w2, b2, g2, s2 = weights
    heads = head_lanes()
    heads_low = heads.astype(BF16)
    slot = star_lanes()
    scores = []
    for i in range(CHUNKS):
        rows = chunk_rows(i)
        low = x_in(i).astype(BF16)
        keep["xb"][rows, :] = low
        projected = mm(low, w_qkv[layer])
        edge = e[rows, :].astype(F32)
        query = projected[:, :DP]
        key_full = projected[:, DP : 2 * DP]
        value_full = projected[:, 2 * DP :]
        key = key_full * edge
        value = value_full * edge
        keep["kf"][rows, :] = key_full.astype(BF16)
        keep["vf"][rows, :] = value_full.astype(BF16)
        keep["q"][rows, :] = query.astype(BF16)
        keep["k"][rows, :] = key.astype(BF16)
        keep["v"][rows, :] = value.astype(BF16)
        put_centers(keep["q0"], query, i, heads)
        put_centers(keep["k0"], key, i, heads)
        put_centers(keep["v0"], value, i, heads)
        scores.append(mm_nt((query * key).astype(BF16), heads_low))
    inside = (slot >= 0) & (slot < SLOTS)
    leaf = (slot > 0) & (slot < SLOTS)
    key_ok = inside & (slot < sizes[...]) & ((slot == 0) | (cols[:, 2:3] > 0.0))
    center = jnp.where(key_ok, mm_nt(keep["k"][...], keep["q0"][...]) * SCALE, -1e30)
    expo = jnp.where(key_ok, jnp.exp(center - jnp.max(center, 0, keepdims=True)), 0.0)
    probs = expo / jnp.sum(expo, 0, keepdims=True)
    keep["p"][...] = probs
    gap = (mm_nt(keep["q"][...], keep["k0"][...]) - jnp.concatenate(scores, 0)) * SCALE
    ratio = jnp.exp(-jnp.abs(gap))
    large = 1.0 / (1.0 + ratio)
    small = ratio * large
    toward = jnp.where(leaf, jnp.where(gap >= 0.0, large, small), 0.0)
    itself = jnp.where(leaf, jnp.where(gap >= 0.0, small, large), 0.0)
    keep["wc"][...] = toward
    keep["ws"][...] = itself
    mixed = mm_tn(probs.astype(BF16), keep["v"][...])
    mixed = jnp.where(heads, mixed, 0.0).astype(BF16)
    is_center = (slot == 0).astype(BF16)
    left = jnp.concatenate([toward.astype(BF16), is_center], 1)
    right = jnp.concatenate([keep["v0"][...], mixed], 0)
    itself_low = itself.astype(BF16)
    for i in range(CHUNKS):
        rows = chunk_rows(i)
        out = mm(left[rows], right) + mm(itself_low[rows], heads_low) * keep["v"][rows, :].astype(
            F32
        )
        out_low = out[:, :D].astype(BF16)
        keep["ob"][rows, :] = out_low
        hidden = x_in(i) + mm(out_low, w_out[layer]) + b_out[layer : layer + 1]
        normed, root = normalize(hidden)
        keep["n1"][rows, :] = normed
        keep["r1"][rows, :] = root
        first = normed * g1[layer : layer + 1] + s1[layer : layer + 1]
        first_low = first.astype(BF16)
        keep["n1b"][rows, :] = first_low
        act, slope = gelu_parts(mm(first_low, w1[layer]) + b1[layer : layer + 1])
        act_low = act.astype(BF16)
        keep["g"][rows, :] = act_low
        keep["gp"][rows, :] = slope.astype(BF16)
        second, root = normalize(first + mm(act_low, w2[layer]) + b2[layer : layer + 1])
        keep["n2"][rows, :] = second
        keep["r2"][rows, :] = root
        result = second * g2[layer : layer + 1] + s2[layer : layer + 1]
        x_out(i, result * cols[rows, 1:2])


def ff_backward(grad_x, keep, cols, weights, layer, gf1, gf2, ga, gh1):
    w1, w2, g1, g2 = weights
    sums = None
    for i in range(CHUNKS):
        rows = chunk_rows(i)
        grad = grad_x(i) * cols[rows, 1:2]
        normed = keep["n2"][rows, :]
        back = norm_back(grad, g2[layer : layer + 1], normed, keep["r2"][rows, :])
        low = back.astype(BF16)
        gf2[rows, :] = low
        slope = keep["gp"][rows, :].astype(F32) * mm_nt(low, w2[layer])
        slope_low = slope.astype(BF16)
        gf1[rows, :] = slope_low
        back_one = back + mm_nt(slope_low, w1[layer])
        normed_one = keep["n1"][rows, :]
        hidden = norm_back(back_one, g1[layer : layer + 1], normed_one, keep["r1"][rows, :])
        gh1[rows, :] = hidden
        ga[rows, :] = hidden.astype(BF16)
        part = (
            jnp.sum(grad * normed, 0, keepdims=True),
            jnp.sum(grad, 0, keepdims=True),
            jnp.sum(back, 0, keepdims=True),
            jnp.sum(slope, 0, keepdims=True),
            jnp.sum(back_one * normed_one, 0, keepdims=True),
            jnp.sum(back_one, 0, keepdims=True),
            jnp.sum(hidden, 0, keepdims=True),
        )
        sums = part if sums is None else tuple(a + b for a, b in zip(sums, part))
    return sums


def attention_backward(ga, w_out, layer, keep, e, w_qkv, gh1, go, gqkv, x_out, e_out, go0):
    heads = head_lanes()
    heads_low = heads.astype(BF16)
    slot = star_lanes()
    leaf = (slot > 0) & (slot < SLOTS)
    selves = []
    for i in range(CHUNKS):
        rows = chunk_rows(i)
        grad = pad_lanes(mm_nt(ga[rows, :], w_out[layer]))
        go[rows, :] = grad.astype(BF16)
        put_centers(go0, grad, i, heads)
        selves.append(mm_nt((grad * keep["v"][rows, :].astype(F32)).astype(BF16), heads_low))
    probs = keep["p"][...]
    of_probs = mm_nt(keep["v"][...], go0[...])
    of_score = probs * (of_probs - jnp.sum(probs * of_probs, 0, keepdims=True)) * SCALE
    score_low = of_score.astype(BF16)
    toward = keep["wc"][...]
    itself = keep["ws"][...]
    gap = mm_nt(go[...], keep["v0"][...]) - jnp.concatenate(selves, 0)
    of_gap = jnp.where(leaf, toward * itself * gap * SCALE, 0.0)
    gap_low = of_gap.astype(BF16)
    toward_low = toward.astype(BF16)
    itself_low = itself.astype(BF16)
    probs_low = probs.astype(BF16)

    def gathered(weights, rows):
        return jnp.where(heads, mm_tn(weights, rows), 0.0).astype(BF16)

    is_center = (slot == 0).astype(BF16)
    right_q = jnp.concatenate([keep["k0"][...], gathered(score_low, keep["k"][...])], 0)
    right_k = jnp.concatenate([keep["q0"][...], gathered(gap_low, keep["q"][...])], 0)
    right_v = jnp.concatenate([go0[...], gathered(toward_low, go[...])], 0)
    for i in range(CHUNKS):
        rows = chunk_rows(i)
        gap_wide = mm(gap_low[rows], heads_low)
        self_wide = mm(itself_low[rows], heads_low)
        first = is_center[rows]
        query = keep["q"][rows, :].astype(F32)
        key = keep["k"][rows, :].astype(F32)
        edge = e[rows, :].astype(F32)
        of_q = mm(jnp.concatenate([gap_low[rows], first], 1), right_q) - gap_wide * key
        of_k = mm(jnp.concatenate([score_low[rows], first], 1), right_k) - gap_wide * query
        of_v = mm(jnp.concatenate([probs_low[rows], first], 1), right_v) + self_wide * go[
            rows, :
        ].astype(F32)
        gqkv[rows, :DP] = of_q.astype(BF16)
        gqkv[rows, DP : 2 * DP] = (of_k * edge).astype(BF16)
        gqkv[rows, 2 * DP :] = (of_v * edge).astype(BF16)
        of_edge = of_k * keep["kf"][rows, :].astype(F32) + of_v * keep["vf"][rows, :].astype(F32)
        e_out(i, of_edge[:, :D])
        x_out(i, gh1[rows, :] + mm_nt(gqkv[rows, :], w_qkv[layer]))


def pack_strips(buf, at, wide, narrow):
    for value in wide:
        for lane in range(0, value.shape[1], 128):
            part = value[:, lane : lane + 128]
            if part.shape[1] < 128:
                part = jnp.concatenate(
                    [part, jnp.zeros((part.shape[0], 128 - part.shape[1]), part.dtype)], 1
                )
            part = jnp.concatenate([part, jnp.zeros((4, 128), part.dtype)], 0)
            buf[at : at + STRIP, :] = part.astype(BF16)
            at += STRIP
    for pair in narrow:
        joined = jnp.concatenate([pair[0], jnp.zeros((D, 20), F32)], 1)
        second = pair[1] if len(pair) > 1 else jnp.zeros((D, 44), F32)
        joined = jnp.concatenate([joined, second, jnp.zeros((D, 20), F32)], 1)
        joined = jnp.concatenate([joined, jnp.zeros((4, 128), F32)], 0)
        buf[at : at + STRIP, :] = joined.astype(BF16)
        at += STRIP
    return at


def pack_vectors(buf, at, vectors, stage):
    stage[...] = jnp.zeros_like(stage)
    row = 0
    for vector in vectors:
        for lane in range(0, vector.shape[1], 128):
            part = vector[:, lane : lane + 128]
            stage[row : row + 1, : part.shape[1]] = part
            row += 1
    buf[at : at + 32, :] = stage[...].astype(BF16)


def send_halves(buf, where, mine, other, sems, half):
    core = where[0]
    first = pltpu.make_async_copy(
        buf.at[pl.ds(pl.multiple_of(core * half, 16), half), :], mine, sems.at[0]
    )
    second = pltpu.make_async_copy(
        buf.at[pl.ds(pl.multiple_of((1 - core) * half, 16), half), :], other, sems.at[1]
    )
    first.start()
    second.start()
    first.wait()
    second.wait()


KEEP = ("xb", "q", "k", "v", "kf", "vf", "q0", "k0", "v0", "p", "wc", "ws", "ob")
KEEP_FF = ("n1", "r1", "n1b", "g", "gp", "n2", "r2")
KEEP_SHAPES = {
    "xb": ((ROWS, D), BF16),
    "q": ((ROWS, DP), BF16),
    "k": ((ROWS, DP), BF16),
    "v": ((ROWS, DP), BF16),
    "kf": ((ROWS, DP), BF16),
    "vf": ((ROWS, DP), BF16),
    "q0": ((HL, DP), BF16),
    "k0": ((HL, DP), BF16),
    "v0": ((HL, DP), BF16),
    "p": ((ROWS, HL), F32),
    "wc": ((ROWS, HL), F32),
    "ws": ((ROWS, HL), F32),
    "ob": ((ROWS, D), BF16),
    "n1": ((ROWS, D), F32),
    "r1": ((ROWS, 1), F32),
    "n1b": ((ROWS, D), BF16),
    "g": ((ROWS, FF), BF16),
    "gp": ((ROWS, FF), BF16),
    "n2": ((ROWS, D), F32),
    "r2": ((ROWS, 1), F32),
}
ALL_KEPT = KEEP + KEEP_FF


def main_kernel(
    where, nodes, dnodes, cols, sizes, e0, e1, back_e, dw_edge, db_edge,
    piece_a, piece_b, piece_c0, piece_c1, piece_d0, piece_d1,
    w_out, b_out, g1, s1, w1, b1, w2, b2, g2, s2,
    nodes_out, mine, other, grad_x_out, grad_e_out, w_qkv, *rest
):
    count = len(ALL_KEPT)
    keep0 = dict(zip(ALL_KEPT, rest[:count]))
    keep1 = dict(zip(ALL_KEPT, rest[count : 2 * count]))
    x0, x1, gf1, gf2, ga, gh1, go, gqkv, go0, buf, stage, sems = rest[2 * count :]

    row = lax.broadcasted_iota(jnp.int32, (225, 3 * DP), 0)
    lane = lax.broadcasted_iota(jnp.int32, (225, 3 * DP), 1)
    part = (row >= 75).astype(jnp.int32) + (row >= 150).astype(jnp.int32)
    base = row + part * (DP - 75)
    pieces = (
        (piece_a.at[0], piece_b.at[0], piece_c0, piece_d0),
        (piece_a.at[1], piece_b.at[1], piece_c1, piece_d1),
    )
    places = [(lane == base + where[1 + n] * 75).astype(BF16) for n in range(4)]
    for layer in range(2):
        total = None
        for n in range(4):
            term = mm(pieces[layer][n][...], places[n])
            total = term if total is None else total + term
        w_qkv[layer] = total.astype(BF16)

    for star in range(STARS):
        x0[star * SLOTS : (star + 1) * SLOTS, :] = nodes[star].astype(F32)
    x0[...] = x0[...] * cols[:, 0:1]

    def store_x1(i, value):
        x1[chunk_rows(i), :] = value

    def store_x0(i, value):
        x0[chunk_rows(i), :] = value

    weights = (w_qkv, w_out, b_out, g1, s1, w1, b1, w2, b2, g2, s2)
    layer_forward(lambda i: x0[chunk_rows(i), :], weights, 0, e0, keep0, cols, sizes, store_x1)
    layer_forward(lambda i: x1[chunk_rows(i), :], weights, 1, e1, keep1, cols, sizes, store_x0)
    for star in range(STARS):
        nodes_out[star] = x0[star * SLOTS : (star + 1) * SLOTS, :].astype(BF16)
        x1[star * SLOTS : (star + 1) * SLOTS, :] = dnodes[star].astype(F32)
    sums = ff_backward(
        lambda i: x1[chunk_rows(i), :], keep1, cols, (w1, w2, g1, g2), 1, gf1, gf2, ga, gh1
    )

    def store_gx(i, value):
        grad_x_out[chunk_rows(i), :] = value

    def store_ge(i, value):
        total = value.astype(BF16).astype(F32) + back_e[chunk_rows(i), :]
        grad_e_out[chunk_rows(i), :] = total.astype(BF16)

    attention_backward(
        ga, w_out, 1, keep1, e1, w_qkv, gh1, go, gqkv, store_gx, store_ge, go0
    )
    dw1 = mm_tn(keep1["n1b"][...], gf1[...])
    dw2 = mm_tn(gf2[...], keep1["g"][...])
    at = pack_strips(buf, 0, [dw1, dw2], [])
    dwo = mm_tn(keep1["ob"][...], ga[...])
    dwe = dw_edge[...]
    dqkv = [mm_tn(keep1["xb"][...], gqkv[:, n * DP : n * DP + D]) for n in range(3)]
    full = dqkv + [dwo, dwe]
    at = pack_strips(
        buf, at, [v[:, :256] for v in full],
        [(full[0][:, 256:], full[1][:, 256:]), (full[2][:, 256:], full[3][:, 256:]),
         (full[4][:, 256:],)],
    )
    gain2, bias2, bff2, bff1, gain1, bias1, bout = sums
    pack_vectors(buf, at, [bff1, bff2, gain2, bias2, gain1, bias1, bout, db_edge[...]], stage)
    send_halves(buf, where, mine, other, sems, ROWS_L1 // 2)


def ff_kernel(where, grad_x, cols, w1, w2, g1, g2, n1, r1, n1b, g, gp, n2, r2,
              mine, other, ga, gh1, gf1, gf2, buf, stage, sems):
    keep = dict(n1=n1, r1=r1, n1b=n1b, g=g, gp=gp, n2=n2, r2=r2)
    sums = ff_backward(
        lambda i: grad_x[chunk_rows(i), :], keep, cols, (w1, w2, g1, g2), 0, gf1, gf2, ga, gh1
    )
    dw1 = mm_tn(n1b[...], gf1[...])
    dw2 = mm_tn(gf2[...], g[...])
    at = pack_strips(buf, 0, [dw1, dw2], [])
    gain2, bias2, bff2, bff1, gain1, bias1, bout = sums
    pack_vectors(buf, at, [bff1, bff2, gain2, bias2, gain1, bias1, bout], stage)
    send_halves(buf, where, mine, other, sems, ROWS_F0 // 2)


def last_kernel(where, cols, idx_row, ga, gh1, grad_e, e0, w_out, w_qkv, wedge, *rest):
    count = len(KEEP)
    keep = dict(zip(KEEP, rest[:count]))
    grad_nodes, mine, other, go, gqkv, go0, back, total_e, buf, stage, sems = rest[count:]
    low = grad_e[...]
    back[...] = mm_nt(low, wedge[0])
    dwe = mm_tn(e0[:, :D], low)
    db_edge = jnp.sum(low.astype(F32), 0, keepdims=True)
    dwo = mm_tn(keep["ob"][...], ga[...])

    def store_gx(i, value):
        value = value * cols[chunk_rows(i), 0:1]
        per = CHUNK // SLOTS
        for star in range(per):
            grad_nodes[i * per + star] = value[star * SLOTS : (star + 1) * SLOTS, :]

    def store_ge(i, value):
        total = value.astype(BF16).astype(F32) + back[chunk_rows(i), :]
        total_e[chunk_rows(i), :] = total.astype(BF16)

    attention_backward(ga, w_out, 0, keep, e0, w_qkv, gh1, go, gqkv, store_gx, store_ge, go0)
    dqkv = [mm_tn(keep["xb"][...], gqkv[:, n * DP : n * DP + D]) for n in range(3)]
    full = dqkv + [dwo, dwe]
    at = pack_strips(
        buf, 0, [v[:, :256] for v in full],
        [(full[0][:, 256:], full[1][:, 256:]), (full[2][:, 256:], full[3][:, 256:]),
         (full[4][:, 256:],)],
    )
    one_hot = (lax.broadcasted_iota(jnp.int32, (NCOL, ROWS), 0) == idx_row[...]).astype(BF16)
    dtable = pad_lanes(mm(one_hot, total_e[...])).astype(BF16)
    for lane in range(0, DP, 128):
        buf[at : at + NCOL, :] = dtable[:, lane : lane + 128]
        at += NCOL
    pack_vectors(buf, at, [db_edge], stage)
    send_halves(buf, where, mine, other, sems, ROWS_T0 // 2)


def unpack_kernel(where, l1_mine, l1_other, f0_mine, f0_other, t0_mine, t0_other,
                  table, wq, wk, wv, wo, bo, g1, s1, w1, b1, w2, b2, g2, s2, we, be,
                  l1, f0, t0, sems):
    core = where[0]
    copies = []
    for n, (mine, other, flat) in enumerate(
        ((l1_mine, l1_other, l1), (f0_mine, f0_other, f0), (t0_mine, t0_other, t0))
    ):
        half = flat.shape[0] // 2
        copies.append(pltpu.make_async_copy(
            mine, flat.at[pl.ds(pl.multiple_of(core * half, 16), half), :], sems.at[2 * n]))
        copies.append(pltpu.make_async_copy(
            other, flat.at[pl.ds(pl.multiple_of((1 - core) * half, 16), half), :],
            sems.at[2 * n + 1]))
    for copy in copies:
        copy.start()
    for copy in copies:
        copy.wait()

    def strip(buf, at, rows=D):
        return buf[at : at + STRIP, :].astype(F32)[:rows]

    def ff_parts(buf, layer):
        for n in range(10):
            width = min(128, FF - n * 128)
            w1[layer, :, n * 128 : n * 128 + width] = strip(buf, n * STRIP)[:, :width]
            part = strip(buf, (10 + n) * STRIP)
            w2[layer, n * 128 : n * 128 + width, :] = part.T[:width, :]

    row = lax.broadcasted_iota(jnp.int32, (DP, 75), 0)
    lane = lax.broadcasted_iota(jnp.int32, (DP, 75), 1)
    pick = (row == lane + where[1] * 75).astype(BF16)

    def square_parts(buf, at, layer):
        narrow = [strip(buf, at + (10 + n) * STRIP) for n in range(3)]
        lefts = [narrow[0][:, :44], narrow[0][:, 64:108], narrow[1][:, :44],
                 narrow[1][:, 64:108], narrow[2][:, :44]]
        for n, out in enumerate((wq, wk, wv, wo, we)):
            wide = jnp.concatenate(
                [strip(buf, at + 2 * n * STRIP), strip(buf, at + (2 * n + 1) * STRIP), lefts[n]], 1
            )
            if n < 3:
                out[layer] = mm(pad_lanes(wide).astype(BF16), pick)
            else:
                out[layer] = wide

    def vectors(buf, at, outs, layer):
        block = buf[at : at + 32, :].astype(F32)
        row = 0
        for out in outs:
            width = out.shape[1]
            for lane in range(0, width, 128):
                size = min(128, width - lane)
                out[layer : layer + 1, lane : lane + size] = block[row : row + 1, :size]
                row += 1

    ff_parts(l1, 1)
    square_parts(l1, 20 * STRIP, 1)
    vectors(l1, 33 * STRIP, (b1, b2, g2, s2, g1, s1, bo, be), 1)
    ff_parts(f0, 0)
    vectors(f0, 20 * STRIP, (b1, b2, g2, s2, g1, s1, bo), 0)
    square_parts(t0, 0, 0)
    at = 13 * STRIP
    table[...] = jnp.concatenate(
        [t0[at + n * NCOL : at + (n + 1) * NCOL, :].astype(F32) for n in range(3)], 1
    )[:, :D]
    vectors(t0, at + 3 * NCOL, (be,), 0)


def shape(dims, kind):
    return jax.ShapeDtypeStruct(dims, kind)


SMEM = pl.BlockSpec(memory_space=pltpu.SMEM)
VMEM = pl.BlockSpec(memory_space=pltpu.VMEM)
ANY = pl.BlockSpec(memory_space=pl.ANY)


def params(mib):
    return pltpu.CompilerParams(vmem_limit_bytes=mib * MIB)


def cost(flops, moved):
    return pl.CostEstimate(flops=int(flops), bytes_accessed=int(moved), transcendentals=0)


def half_pair(rows):
    return [shape((rows // 2, 128), BF16), shape((rows // 2, 128), BF16)]


RING_UP = [(n, (n + 1) % 4) for n in range(4)]
RING_DOWN = [(n, (n + 3) % 4) for n in range(4)]
SWAP = [(0, 1), (1, 0)]
CHIPS = ("x", "z", "yh", "yl")
ALONG_Y = ("yh", "yl")


def summed(mine, other):
    half = (mine.astype(F32) + lax.ppermute(other, "c", SWAP).astype(F32)).astype(BF16)
    rows = half.shape[0] // 64
    parts = lax.all_to_all(half, CHIPS, 0, 0, tiled=True).reshape(64, rows, 128)
    total = jnp.sum(parts.astype(F32), 0).astype(BF16)
    spread = jnp.broadcast_to(total[None], (64, rows, 128)).reshape(64 * rows, 128)
    full = lax.all_to_all(spread, CHIPS, 0, 0, tiled=True)
    return full, lax.ppermute(full, "c", SWAP)


def body(
    nodes, edge_table, edge_index, star_sizes, leaf_drop, missing, w_query, w_key, w_value, w_out,
    b_out, ln1_gain, ln1_bias, w_ff1, b_ff1, w_ff2, b_ff2, ln2_gain, ln2_bias, w_edge, b_edge,
    d_nodes_out, d_edges_out,
):
    chip = lax.axis_index("yl")
    core = lax.axis_index("c")
    own = chip * 2 + core
    joined = jnp.concatenate((w_query, w_key, w_value), 2)
    piece_c0 = lax.ppermute(joined[0], ALONG_Y, RING_UP)
    piece_c1 = lax.ppermute(joined[1], ALONG_Y, RING_DOWN)
    piece_b = lax.ppermute(joined, "c", SWAP)
    piece_d0 = lax.ppermute(piece_c0, "c", SWAP)
    piece_d1 = lax.ppermute(piece_c1, "c", SWAP)
    where = jnp.stack(
        [core, own, own + 1 - 2 * core, own + 2 - 4 * chip, own + 3 - 4 * chip - 2 * core]
    ).astype(jnp.int32)

    slot_ids = jnp.arange(SLOTS)[None, :]
    own_sizes = lax.dynamic_slice_in_dim(star_sizes, own * STARS, STARS)
    own_drop = lax.dynamic_slice_in_dim(leaf_drop, own * STARS, STARS, 0)
    present = (slot_ids == 0) | (missing == 0)
    valid = slot_ids < own_sizes[:, None]
    kept = (slot_ids == 0) | (own_drop == 0)
    cols = jnp.stack(
        [t.astype(F32).reshape(ROWS) for t in (present, valid, kept, edge_index)], axis=1
    )
    sizes = jnp.repeat(own_sizes, 16)[None, :]
    idx_row = edge_index.reshape(1, ROWS)

    e0, e1, edges_out, back_e, dw_edge, db_edge = pl.pallas_call(
        edge_kernel,
        out_shape=[
            shape((ROWS, DP), BF16), shape((ROWS, DP), BF16), shape((STARS, SLOTS, D), BF16),
            shape((ROWS, D), F32), shape((D, D), F32), shape((1, D), F32),
        ],
        in_specs=[VMEM] * 5,
        out_specs=[VMEM] * 6,
        scratch_shapes=[pltpu.VMEM((ROWS, D), F32)],
        compiler_params=params(40),
        cost_estimate=cost(1e9, 4e6),
        name="edges",
    )(cols, edge_table, w_edge, b_edge, d_edges_out)

    kept_scratch = [pltpu.VMEM(*KEEP_SHAPES[name]) for name in ALL_KEPT]
    kept_shapes = [shape(*KEEP_SHAPES[name]) for name in ALL_KEPT]
    row_scratch = dict(
        x=pltpu.VMEM((ROWS, D), F32),
        ff=pltpu.VMEM((ROWS, FF), BF16),
        low=pltpu.VMEM((ROWS, D), BF16),
        wide=pltpu.VMEM((ROWS, DP), BF16),
        qkv=pltpu.VMEM((ROWS, 3 * DP), BF16),
        center=pltpu.VMEM((HL, DP), BF16),
        stage=pltpu.VMEM((32, 128), F32),
        sems=pltpu.SemaphoreType.DMA((2,)),
    )
    main = pl.pallas_call(
        main_kernel,
        out_shape=[shape((STARS, SLOTS, D), BF16), *half_pair(ROWS_L1),
                   shape((ROWS, D), F32), shape((ROWS, D), BF16), shape((2, D, 3 * DP), BF16),
                   *kept_shapes],
        in_specs=[SMEM] + [VMEM] * 25,
        out_specs=[VMEM, ANY, ANY, VMEM, VMEM, VMEM] + [VMEM] * len(kept_shapes),
        scratch_shapes=[
            *kept_scratch,
            row_scratch["x"], row_scratch["x"], row_scratch["ff"], row_scratch["low"],
            row_scratch["low"], row_scratch["x"], row_scratch["wide"], row_scratch["qkv"],
            row_scratch["center"], pltpu.VMEM((ROWS_L1, 128), BF16), row_scratch["stage"],
            row_scratch["sems"],
        ],
        compiler_params=params(62),
        cost_estimate=cost(8e9, 3e7),
        name="forward",
    )(where, nodes, d_nodes_out, cols, sizes, e0, e1, back_e, dw_edge, db_edge,
      joined, piece_b, piece_c0, piece_c1, piece_d0, piece_d1,
      w_out, b_out, ln1_gain, ln1_bias, w_ff1, b_ff1, w_ff2, b_ff2, ln2_gain, ln2_bias)
    nodes_out, l1_mine, l1_other, grad_x, grad_e, w_qkv = main[:6]
    keep0 = dict(zip(ALL_KEPT, main[6:]))
    l1 = summed(l1_mine, l1_other)

    f0_mine, f0_other, ga, gh1 = pl.pallas_call(
        ff_kernel,
        out_shape=[*half_pair(ROWS_F0), shape((ROWS, D), BF16), shape((ROWS, D), F32)],
        in_specs=[SMEM] + [VMEM] * 13,
        out_specs=[ANY, ANY, VMEM, VMEM],
        scratch_shapes=[
            row_scratch["ff"], row_scratch["low"], pltpu.VMEM((ROWS_F0, 128), BF16),
            row_scratch["stage"], row_scratch["sems"],
        ],
        compiler_params=params(50),
        cost_estimate=cost(2.5e9, 1e7),
        name="feedforward",
    )(where, grad_x, cols, w_ff1, w_ff2, ln1_gain, ln2_gain,
      *[keep0[name] for name in KEEP_FF])
    f0 = summed(f0_mine, f0_other)

    grad_nodes, t0_mine, t0_other = pl.pallas_call(
        last_kernel,
        out_shape=[shape((STARS, SLOTS, D), F32), *half_pair(ROWS_T0)],
        in_specs=[SMEM] + [VMEM] * (9 + len(KEEP)),
        out_specs=[VMEM, ANY, ANY],
        scratch_shapes=[
            row_scratch["wide"], row_scratch["qkv"], row_scratch["center"], row_scratch["x"],
            row_scratch["low"], pltpu.VMEM((ROWS_T0, 128), BF16), row_scratch["stage"],
            row_scratch["sems"],
        ],
        compiler_params=params(50),
        cost_estimate=cost(2.5e9, 1e7),
        name="attention",
    )(where, cols, idx_row, ga, gh1, grad_e, e0, w_out, w_qkv, w_edge,
      *[keep0[name] for name in KEEP])
    t0 = summed(t0_mine, t0_other)

    grads = pl.pallas_call(
        unpack_kernel,
        out_shape=[
            shape((NCOL, D), F32), *[shape((2, D, 75), F32)] * 3, shape((2, D, D), F32),
            *[shape((2, D), F32)] * 3, shape((2, D, FF), F32), shape((2, FF), F32),
            shape((2, FF, D), F32), *[shape((2, D), F32)] * 3, shape((2, D, D), F32),
            shape((2, D), F32),
        ],
        in_specs=[SMEM] + [ANY] * 6,
        out_specs=[VMEM] * 16,
        scratch_shapes=[
            pltpu.VMEM((ROWS_L1, 128), BF16), pltpu.VMEM((ROWS_F0, 128), BF16),
            pltpu.VMEM((ROWS_T0, 128), BF16), pltpu.SemaphoreType.DMA((6,)),
        ],
        compiler_params=params(50),
        cost_estimate=cost(1e8, 1.5e7),
        name="unpack",
    )(where, *l1, *f0, *t0)
    return (nodes_out, edges_out, grad_nodes, *grads)


def solution(mesh):
    devices = mesh.devices.reshape(4, 4, 2, 2, 2)
    fine = Mesh(devices, ("x", "z", "yh", "yl", "c"))
    graphs = ("x", "z", "yh")
    heads = ("yl", "c")
    everyone = graphs + heads
    rows3 = P(everyone, None, None)
    rows2 = P(everyone, None)
    per_head = P(None, None, heads)
    return jax.shard_map(
        body,
        mesh=fine,
        in_specs=(
            rows3, P(), rows2, P(graphs), P(graphs, None), rows2, per_head, per_head, per_head,
            *[P()] * 12, rows3, rows3,
        ),
        out_specs=(rows3, rows3, rows3, P(), per_head, per_head, per_head, *[P()] * 12),
        check_vma=False,
    )
```

```python
import math

import jax
import jax.numpy as jnp
from jax import lax
from jax.experimental import pallas as pl
from jax.experimental.layout import Layout, with_layout_constraint
from jax.experimental.pallas import tpu as pltpu
from jax.sharding import Mesh, PartitionSpec as P

D = 300
DP = 384
FF = 1200
HD = 25
SLOTS = 100
STARS = 8
ROWS = STARS * SLOTS
HL = 128
NCOL = 512
SCALE = 1.0 / math.sqrt(HD)
CHUNK = 400
CHUNKS = ROWS // CHUNK
STRIP = 304
GROUP = 80
EP = 4 * GROUP
SPARE = STRIP - D
HALF = 10752
FF_ROWS = 19 * STRIP
LAYER_ROWS = FF_ROWS + 13 * EP
F32 = jnp.float32
BF16 = jnp.bfloat16
MIB = 1 << 20


def mm(left, right):
    return lax.dot_general(left, right, (((1,), (0,)), ((), ())), preferred_element_type=F32)


def mm_nt(left, right):
    return lax.dot_general(left, right, (((1,), (1,)), ((), ())), preferred_element_type=F32)


def mm_tn(left, right):
    return lax.dot_general(left, right, (((0,), (0,)), ((), ())), preferred_element_type=F32)


def chunk_rows(index):
    return slice(index * CHUNK, (index + 1) * CHUNK)


def by_slot(value):
    return value.reshape(value.shape[0] // 8, 8, value.shape[1])


def flat(value):
    return value.reshape(value.shape[0] * 8, value.shape[2])


def spread_heads():
    row = lax.broadcasted_iota(jnp.int32, (HL, 2 * DP), 0)
    lane = lax.broadcasted_iota(jnp.int32, (HL, 2 * DP), 1)
    second = lane >= DP
    lane = jnp.where(second, lane - DP, lane)
    head = jnp.where(second, row - 16, row)
    steps = sum((head >= n).astype(jnp.int32) for n in (3, 6, 9))
    offset = lane - head * HD - steps * (GROUP - 3 * HD)
    real = (head >= 0) & (head < 12)
    return ((offset >= 0) & (offset < HD) & real).astype(BF16)


def group_order():
    row = lax.broadcasted_iota(jnp.int32, (DP, D), 0)
    lane = lax.broadcasted_iota(jnp.int32, (DP, D), 1)
    steps = sum((lane >= n * 75).astype(jnp.int32) for n in (1, 2, 3))
    return (row == lane + steps * (GROUP - 75)).astype(BF16)


def lanes_from_groups(value):
    return jnp.concatenate([value[:, n * GROUP : n * GROUP + 75] for n in range(4)], 1)


def gelu_parts(x):
    share = 0.5 + 0.5 * lax.erf(x * 0.7071067811865476)
    return x * share, share + x * (jnp.exp(-0.5 * x * x) * 0.3989422804014327)


def normalize(hidden):
    center = hidden - jnp.sum(hidden, -1, keepdims=True) * (1.0 / D)
    spread = jnp.sum(center * center, -1, keepdims=True) * (1.0 / D)
    root = lax.rsqrt(spread + 1e-05)
    return center * root, root


def norm_back(grad, gain, normed, root):
    scaled = grad * gain
    first = jnp.sum(scaled, -1, keepdims=True) * (1.0 / D)
    second = jnp.sum(scaled * normed, -1, keepdims=True) * (1.0 / D)
    return root * (scaled - first - normed * second)


def own_heads():
    return lax.axis_index("yl") * 2 + lax.axis_index("c")


def pack_kernel(wq, wk, wv, first, second):
    for layer, out in enumerate((first, second)):
        for n, w in enumerate((wq, wk, wv)):
            rows = jnp.concatenate([w[:, layer, :].astype(F32), jnp.zeros((GROUP - 75, D), F32)], 0)
            out[n * GROUP : (n + 1) * GROUP, :] = rows.astype(BF16)


def edges_forward(sizes, t, bedge, edges_out):
    index, missing, drop, table, wedge = (
        t[name] for name in ("index", "missing", "drop", "table", "wedge_in")
    )
    cols_out, e0_out, e1_out, w_out_out, wedge_out, back_out, dw_out = (
        t[name] for name in ("cols", "e0", "e1", "w_out", "wedge", "back", "dw")
    )
    order = group_order()
    for layer in range(2):
        w_out_out[layer] = mm(order, t["w_out_in"][layer]).astype(BF16)
    wedge_out[...] = mm_nt(mm(order, wedge[0]).astype(BF16), order).astype(BF16)
    wedge_last = mm(order, wedge[1]).astype(BF16)
    grouped = mm(order, table[...]).astype(BF16)
    bias = bedge[0:1]
    high = bias.astype(BF16).astype(F32)
    middle = (bias - high).astype(BF16).astype(F32)
    terms = jnp.concatenate([high, middle, bias - high - middle, jnp.zeros((5, D), F32)], 0)
    bias = jnp.sum(mm_nt(terms.astype(BF16), order), 0, keepdims=True)
    slot = lax.broadcasted_iota(jnp.int32, (STARS, SLOTS), 1)
    star = lax.broadcasted_iota(jnp.int32, (STARS, SLOTS), 0)
    first = own_heads() * STARS
    size = jnp.zeros((STARS, SLOTS), jnp.int32)
    for n in range(STARS):
        size = jnp.where(star == n, sizes[first + n], size)
    dropped = drop[pl.ds(pl.multiple_of(first, 8), STARS), :]
    present = (slot == 0) | (missing[...] == 0)
    valid = slot < size
    key_ok = valid & ((slot == 0) | (dropped == 0))
    number = index[...]
    flags = jnp.concatenate(
        [t.astype(F32) for t in (present, valid, key_ok, number >> 8, number & 255)], 0
    ).astype(BF16)
    row = lax.broadcasted_iota(jnp.int32, (ROWS, SLOTS), 0)
    lane = lax.broadcasted_iota(jnp.int32, (ROWS, SLOTS), 1)
    all_stars = mm_nt(((row >> 3) == lane).astype(BF16), flags)
    row = lax.broadcasted_iota(jnp.int32, (ROWS, 5 * STARS), 0)
    lane = lax.broadcasted_iota(jnp.int32, (ROWS, 5 * STARS), 1)
    own = jnp.where((row & 7) == (lane & 7), all_stars, 0.0).astype(BF16)
    row = lax.broadcasted_iota(jnp.int32, (5 * STARS, HL), 0)
    lane = lax.broadcasted_iota(jnp.int32, (5 * STARS, HL), 1)
    cols = mm(own, ((row >> 3) == lane).astype(BF16))
    cols_out[...] = cols
    picked = cols[:, 3:4] * 256.0 + cols[:, 4:5]
    lane = lax.broadcasted_iota(jnp.int32, (CHUNK, NCOL), 1).astype(F32)
    for i in range(CHUNKS):
        rows = chunk_rows(i)
        one_hot = (picked[rows] == lane).astype(BF16)
        e0 = mm_nt(one_hot, grouped).astype(BF16)
        e1 = (mm(e0, wedge_out[...]) + bias).astype(BF16)
        edges_out[rows, :] = (mm(e1, wedge_last) + bedge[1:2]).astype(BF16)
        e0_out[rows, :] = e0
        e1_out[rows, :] = e1
    low = t["dedges"][...]
    back_out[...] = mm_nt(low, wedge_last)
    dw_out[...] = mm_tn(e1_out[:, :EP], low)
    return jnp.sum(low.astype(F32), 0, keepdims=True)


def attention_forward(x_in, layer, w_qkv, e, keep, cols):
    spread = spread_heads()
    scores = []
    center = None
    for i in range(CHUNKS):
        rows = chunk_rows(i)
        low = x_in(i).astype(BF16)
        keep["xb"][rows, :] = low
        projected = mm_nt(low, w_qkv[layer])
        edge = e[rows, :].astype(F32)
        query = projected[:, :DP]
        key_full = projected[:, DP : 2 * DP]
        value_full = projected[:, 2 * DP :]
        key = key_full * edge
        value = value_full * edge
        keep["kf"][rows, :] = key_full.astype(BF16)
        keep["vf"][rows, :] = value_full.astype(BF16)
        keep["q"][rows, :] = query.astype(BF16)
        keep["k"][rows, :] = key.astype(BF16)
        keep["v"][rows, :] = value.astype(BF16)
        if i == 0:
            center = (query[:8], key[:8])
            keep["c0"][0] = query[:8]
            keep["c0"][1] = key[:8]
            keep["c0"][2] = value[:8]
        keys = by_slot(key)
        of_center = flat(keys * center[0][None])
        of_gap = flat((center[1][None] - keys) * by_slot(query))
        products = jnp.concatenate([of_center.astype(BF16), of_gap.astype(BF16)], 1)
        scores.append(mm_nt(products, spread))
    score = jnp.concatenate(scores, 0) * SCALE
    lane = lax.broadcasted_iota(jnp.int32, (ROWS, HL), 1)
    row = lax.broadcasted_iota(jnp.int32, (ROWS, HL), 0)
    is_gap = lane >= 16
    open_ = cols[:, 2:3] > 0.0
    masked = by_slot(jnp.where(open_, score, -1e30))
    lowered = flat(masked - jnp.max(masked, 0, keepdims=True))
    expo = jnp.exp(jnp.where(is_gap, -jnp.abs(score), lowered))
    expo = jnp.where(is_gap | open_, expo, 0.0)
    total = by_slot(expo)
    probs = flat(total / jnp.sum(total, 0, keepdims=True))
    large = 1.0 / (1.0 + expo)
    toward = jnp.where(row < 8, 0.0, jnp.where(score >= 0.0, large, expo * large))
    weight = jnp.where(is_gap, toward, probs)
    keep["w"][...] = weight
    return weight.astype(BF16)


def rest_forward(x_in, layer, weights, weight, keep, cols, x_out):
    w_out, b_out, g1, s1, w1, b1, w2, b2, g2, s2 = weights
    spread = spread_heads()
    value_center = keep["c0"][2][None]
    outs = []
    total = None
    for i in range(CHUNKS):
        rows = chunk_rows(i)
        wide = mm(weight[rows], spread)
        keep["ww"][rows, :] = wide.astype(BF16)
        values = by_slot(keep["v"][rows, :].astype(F32))
        part = jnp.sum(by_slot(wide[:, :DP]) * values, 0)
        total = part if total is None else total + part
        out = flat(values + by_slot(wide[:, DP:]) * (value_center - values))
        keep["ob"][rows, :] = out.astype(BF16)
    out = keep["ob"][:16, :].astype(F32)
    keep["ob"][:16, :] = jnp.concatenate([total, out[8:]], 0).astype(BF16)
    for i in range(CHUNKS):
        rows = chunk_rows(i)
        hidden = x_in(i) + mm(keep["ob"][rows, :], w_out[layer]) + b_out[layer : layer + 1]
        normed, root = normalize(hidden)
        keep["n1"][rows, :] = normed
        keep["r"][rows, 0:1] = root
        first = normed * g1[layer : layer + 1] + s1[layer : layer + 1]
        first_low = first.astype(BF16)
        keep["n1b"][rows, :] = first_low
        act, slope = gelu_parts(mm(first_low, w1[layer]) + b1[layer : layer + 1])
        act_low = act.astype(BF16)
        keep["g"][rows, :] = act_low
        keep["gp"][rows, :] = slope.astype(BF16)
        second, root = normalize(first + mm_nt(act_low, w2[layer]) + b2[layer : layer + 1])
        keep["n2"][rows, :] = second
        keep["r"][rows, 1:2] = root
        result = second * g2[layer : layer + 1] + s2[layer : layer + 1]
        x_out(i, result * cols[rows, 1:2])


def ff_backward(grad_x, keep, cols, weights, layer, gf1, gf2, ga, gh1):
    w1, w2, g1, g2 = weights
    sums = None
    for i in range(CHUNKS):
        rows = chunk_rows(i)
        grad = grad_x(i) * cols[rows, 1:2]
        normed = keep["n2"][rows, :]
        back = norm_back(grad, g2[layer : layer + 1], normed, keep["r"][rows, 1:2])
        low = back.astype(BF16)
        gf2[rows, :] = low
        slope = keep["gp"][rows, :].astype(F32) * mm(low, w2[layer])
        slope_low = slope.astype(BF16)
        gf1[rows, :] = slope_low
        back_one = back + mm_nt(slope_low, w1[layer])
        normed_one = keep["n1"][rows, :]
        hidden = norm_back(back_one, g1[layer : layer + 1], normed_one, keep["r"][rows, 0:1])
        gh1[rows, :] = hidden
        ga[rows, :] = hidden.astype(BF16)
        part = (
            jnp.sum(slope, 0, keepdims=True),
            jnp.sum(back, 0, keepdims=True),
            jnp.sum(grad * normed, 0, keepdims=True),
            jnp.sum(grad, 0, keepdims=True),
            jnp.sum(back_one * normed_one, 0, keepdims=True),
            jnp.sum(back_one, 0, keepdims=True),
            jnp.sum(hidden, 0, keepdims=True),
        )
        sums = part if sums is None else tuple(a + b for a, b in zip(sums, part))
    return sums


def attention_backward(ga, w_out, layer, keep, e, w_qkv, gh1, go, gqkv, x_out, e_out):
    spread = spread_heads()
    query_center, key_center, value_center = (keep["c0"][n][None] for n in range(3))
    dots = []
    grad_center = None
    for i in range(CHUNKS):
        rows = chunk_rows(i)
        grad = mm_nt(ga[rows, :], w_out[layer])
        if i == 0:
            grad_center = grad[:8].astype(BF16).astype(F32)[None]
            grad = jnp.concatenate([jnp.zeros((8, DP), F32), grad[8:]], 0)
        go[rows, :] = grad.astype(BF16)
        values = by_slot(keep["v"][rows, :].astype(F32))
        of_center = flat(grad_center * values)
        of_gap = flat(by_slot(grad) * (value_center - values))
        products = jnp.concatenate([of_center.astype(BF16), of_gap.astype(BF16)], 1)
        dots.append(mm_nt(products, spread))
    dot = jnp.concatenate(dots, 0)
    weight = keep["w"][...]
    lane = lax.broadcasted_iota(jnp.int32, (ROWS, HL), 1)
    mean = jnp.sum(by_slot(weight * dot), 0, keepdims=True)
    of_probs = flat(by_slot(dot) - mean)
    grads = weight * jnp.where(lane >= 16, (1.0 - weight) * dot, of_probs) * SCALE
    grads = grads.astype(BF16)
    sums = None
    for i in reversed(range(CHUNKS)):
        rows = chunk_rows(i)
        wide = mm(grads[rows], spread)
        of_score = by_slot(wide[:, :DP])
        of_gap = by_slot(wide[:, DP:])
        query = by_slot(keep["q"][rows, :].astype(F32))
        key = by_slot(keep["k"][rows, :].astype(F32))
        grad = by_slot(go[rows, :].astype(F32))
        weights = keep["ww"][rows, :].astype(F32)
        probs = by_slot(weights[:, :DP])
        toward = by_slot(weights[:, DP:])
        edge = e[rows, :].astype(F32)
        pulled = of_gap * query
        moved = toward * grad
        part = (jnp.sum(of_score * key, 0), jnp.sum(pulled, 0), jnp.sum(moved, 0))
        sums = part if sums is None else tuple(a + b for a, b in zip(sums, part))
        of_q = of_gap * (key_center - key)
        of_k = of_score * query_center - pulled
        of_v = probs * grad_center + grad - moved
        if i == 0:
            of_q, of_k, of_v = (
                jnp.concatenate([t[:1] + s[None], t[1:]], 0)
                for t, s in zip((of_q, of_k, of_v), sums)
            )
        of_k, of_v = flat(of_k), flat(of_v)
        gqkv[rows, :DP] = flat(of_q).astype(BF16)
        gqkv[rows, DP : 2 * DP] = (of_k * edge).astype(BF16)
        gqkv[rows, 2 * DP :] = (of_v * edge).astype(BF16)
        of_edge = of_k * keep["kf"][rows, :].astype(F32) + of_v * keep["vf"][rows, :].astype(F32)
        e_out(i, of_edge)
        x_out(i, gh1[rows, :] + mm(gqkv[rows, :], w_qkv[layer]))


def pad_to(value, rows, lanes):
    if value.shape[1] < lanes:
        gap = jnp.zeros((value.shape[0], lanes - value.shape[1]), F32)
        value = jnp.concatenate([value, gap], 1)
    if value.shape[0] < rows:
        value = jnp.concatenate([value, jnp.zeros((rows - value.shape[0], lanes), F32)], 0)
    return value


class Packer:
    def __init__(self, buf, at):
        self.buf, self.at = buf, at

    def strip(self, value):
        rows = value.shape[0]
        self.buf[self.at : self.at + rows, :] = value.astype(BF16)
        self.at += rows

    def whole(self, value):
        for lane in range(0, value.shape[1] // 128 * 128, 128):
            self.strip(value[:, lane : lane + 128])

    def rests(self, values):
        values = [pad_to(v[:, v.shape[1] // 128 * 128 :], v.shape[0], 64) for v in values]
        for n in range(0, len(values), 2):
            second = values[n + 1] if n + 1 < len(values) else jnp.zeros_like(values[n])
            self.strip(jnp.concatenate([values[n], second], 1))

    def ff(self, dw1, dw2, vectors, stage):
        stage[...] = jnp.zeros_like(stage)
        row = 0
        for vector in vectors:
            for lane in range(0, vector.shape[1], 128):
                part = vector[:, lane : lane + 128]
                stage[row : row + 1, : part.shape[1]] = part
                row += 1
        for n in range(9):
            part = dw1[:, n * 128 : (n + 1) * 128]
            spare = stage[n * SPARE : (n + 1) * SPARE, :] if n < 8 else jnp.zeros((SPARE, 128), F32)
            self.strip(jnp.concatenate([part, spare], 0))
        self.whole(pad_to(dw2, STRIP, FF))
        self.rests([pad_to(dw1, STRIP, FF), pad_to(dw2, STRIP, FF)])

    def squares(self, values):
        for value in values:
            self.whole(value)
        self.rests(values)


KEEP = {
    "n2": ((ROWS, D), F32),
    "r": ((ROWS, 2), F32),
    "gp": ((ROWS, FF), BF16),
    "n1": ((ROWS, D), F32),
    "g": ((ROWS, FF), BF16),
    "n1b": ((ROWS, D), BF16),
    "c0": ((3, 8, DP), F32),
    "v": ((ROWS, DP), BF16),
    "w": ((ROWS, HL), F32),
    "ww": ((ROWS, 2 * DP), BF16),
    "q": ((ROWS, DP), BF16),
    "k": ((ROWS, DP), BF16),
    "kf": ((ROWS, DP), BF16),
    "vf": ((ROWS, DP), BF16),
    "ob": ((ROWS, DP), BF16),
    "xb": ((ROWS, D), BF16),
}
LOADS = {
    "index": ((STARS, SLOTS), jnp.int32),
    "missing": ((STARS, SLOTS), jnp.int32),
    "drop": ((4 * STARS, SLOTS), jnp.int32),
    "w_out_in": ((2, D, D), BF16),
    "wedge_in": ((2, D, D), BF16),
    "table": ((D, NCOL), BF16),
    "dedges": ((ROWS, D), BF16),
    "own0": ((3 * GROUP, D), BF16),
    "core0": ((3 * GROUP, D), BF16),
    "near0": ((3 * GROUP, D), BF16),
    "far0": ((3 * GROUP, D), BF16),
    "nodes": ((ROWS, D), BF16),
    "w1": ((2, D, FF), BF16),
    "w2": ((2, D, FF), BF16),
    "own1": ((3 * GROUP, D), BF16),
    "core1": ((3 * GROUP, D), BF16),
    "near1": ((3 * GROUP, D), BF16),
    "far1": ((3 * GROUP, D), BF16),
    "dnodes": ((ROWS, D), BF16),
}
WORK = {
    "cols": ((ROWS, HL), F32),
    "e0": ((ROWS, DP), BF16),
    "e1": ((ROWS, DP), BF16),
    "w_out": ((2, DP, D), BF16),
    "wedge": ((DP, DP), BF16),
    "back": ((ROWS, DP), F32),
    "dw": ((EP, D), F32),
    "edges": ((ROWS, D), BF16),
    "w_qkv": ((2, 3 * DP, D), BF16),
    "x": ((ROWS, D), F32),
    "gf1": ((ROWS, FF), BF16),
    "gf2": ((ROWS, D), BF16),
    "ga": ((ROWS, D), BF16),
    "gh1": ((ROWS, D), F32),
    "go": ((ROWS, DP), BF16),
    "gqkv": ((ROWS, 3 * DP), BF16),
    "ge": ((ROWS, DP), BF16),
    "last": ((ROWS, D), F32),
    "buf": ((2 * HALF, 128), BF16),
    "stage": ((32, 128), F32),
}


class Loads:
    def __init__(self, sources, targets, sems):
        self.copies = {}
        for n, name in enumerate(LOADS):
            self.copies[name] = pltpu.make_async_copy(sources[name], targets[name], sems.at[n])
            self.copies[name].start()

    def wait(self, *names):
        for name in names:
            self.copies.pop(name).wait()


def main_kernel(star_sizes, bedge, b_out, g1, s1, b1, b2, g2, s2, *rest):
    count = len(KEEP)
    sources = dict(zip(LOADS, rest))
    rest = rest[len(LOADS) :]
    nodes_out, edges_out, grad_nodes, mine, other = rest[:5]
    keep0 = dict(zip(KEEP, rest[5:]))
    keep1 = dict(zip(KEEP, rest[5 + count :]))
    rest = rest[5 + 2 * count :]
    t = dict(zip(LOADS, rest))
    rest = rest[len(LOADS) :]
    work = dict(zip(WORK, rest))
    in_sems, out_sems = rest[len(WORK) :]
    loads = Loads(sources, t, in_sems)
    core = lax.axis_index("c")
    sent = []

    def send(half, first, rows):
        n = len(sent)
        sent.append((half, first, rows))
        for is_own, to in ((True, mine), (False, other)):
            @pl.when((core == half) == is_own)
            def start():
                part = buf.at[half * HALF + first : half * HALF + first + rows, :]
                pltpu.make_async_copy(
                    part, to.at[first : first + rows, :], out_sems.at[3 + n]
                ).start()

    def sent_wait():
        for n, (half, first, rows) in enumerate(sent):
            part = buf.at[half * HALF + first : half * HALF + first + rows, :]
            pltpu.make_async_copy(
                part, mine.at[first : first + rows, :], out_sems.at[3 + n]
            ).wait()

    t.update(work)
    w_qkv, x, gf1, gf2, ga, gh1, go, gqkv, ge, last, buf, stage = list(work.values())[8:]
    cols, w_out, w1, w2 = t["cols"], t["w_out"], t["w1"], t["w2"]
    own = own_heads()

    def place(layer):
        names = [name + str(layer) for name in ("own", "core", "near", "far")]
        loads.wait(*names)
        for part in range(3):
            w_qkv[layer, part * DP + EP : (part + 1) * DP, :] = jnp.zeros((DP - EP, D), BF16)
            for n, name in enumerate(names):
                at = pl.multiple_of(part * DP + (own ^ n) * GROUP, 16)
                w_qkv[layer, pl.ds(at, GROUP), :] = t[name][part * GROUP : (part + 1) * GROUP, :]

    def x0(i):
        rows = chunk_rows(i)
        return t["nodes"][rows, :].astype(F32) * cols[rows, 0:1]

    def x1(i):
        return x[chunk_rows(i), :]

    def store_x(i, value):
        x[chunk_rows(i), :] = value

    def store_nodes(i, value):
        t["nodes"][chunk_rows(i), :] = value.astype(BF16)

    weights = (w_out, b_out, g1, s1, w1, b1, w2, b2, g2, s2)
    loads.wait("index", "missing", "drop", "w_out_in", "wedge_in", "table", "dedges")
    db_edge = edges_forward(star_sizes, t, bedge, t["edges"])
    outs = [pltpu.make_async_copy(t["edges"], edges_out, out_sems.at[0])]
    outs[0].start()
    place(0)
    loads.wait("nodes")
    weight = attention_forward(x0, 0, w_qkv, t["e0"], keep0, cols)
    loads.wait("w1", "w2")
    rest_forward(x0, 0, weights, weight, keep0, cols, store_x)
    place(1)
    weight = attention_forward(x1, 1, w_qkv, t["e1"], keep1, cols)
    rest_forward(x1, 1, weights, weight, keep1, cols, store_nodes)
    outs.append(pltpu.make_async_copy(t["nodes"], nodes_out, out_sems.at[1]))
    outs[1].start()

    loads.wait("dnodes")
    packer = Packer(buf, 0)
    sums = ff_backward(
        lambda i: t["dnodes"][chunk_rows(i), :].astype(F32),
        keep1, cols, (w1, w2, g1, g2), 1, gf1, gf2, ga, gh1,
    )
    packer.ff(
        mm_tn(keep1["n1b"][...], gf1[...]), mm_tn(gf2[...], keep1["g"][...]),
        [*sums, db_edge], stage,
    )
    dwo = mm_tn(keep1["ob"][:, :EP], ga[...])

    def store_ge(i, value):
        total = value.astype(BF16).astype(F32) + t["back"][chunk_rows(i), :]
        ge[chunk_rows(i), :] = total.astype(BF16)

    attention_backward(ga, w_out, 1, keep1, t["e1"], w_qkv, gh1, go, gqkv, store_x, store_ge)
    dqkv = [mm_tn(gqkv[:, n * DP : n * DP + EP], keep1["xb"][...]) for n in range(3)]
    packer.squares(dqkv + [dwo, t["dw"][...]])
    send(0, 0, LAYER_ROWS)
    packer.at = HALF

    sums = ff_backward(x1, keep0, cols, (w1, w2, g1, g2), 0, gf1, gf2, ga, gh1)
    t["back"][...] = mm_nt(ge[...], t["wedge"][...])
    dwe = mm_tn(t["e0"][:, :EP], ge[:, :EP])
    db_first = jnp.sum(ge[...].astype(F32), 0, keepdims=True)
    packer.ff(
        mm_tn(keep0["n1b"][...], gf1[...]), mm_tn(gf2[...], keep0["g"][...]),
        [*sums, db_first[:, :EP]], stage,
    )
    send(1, 0, FF_ROWS)
    dwo = mm_tn(keep0["ob"][:, :EP], ga[...])

    def store_last(i, value):
        rows = chunk_rows(i)
        last[rows, :] = value * cols[rows, 0:1]

    attention_backward(ga, w_out, 0, keep0, t["e0"], w_qkv, gh1, go, gqkv, store_last, store_ge)
    outs.append(pltpu.make_async_copy(last, grad_nodes, out_sems.at[2]))
    outs[2].start()
    dqkv = [mm_tn(gqkv[:, n * DP : n * DP + EP], keep0["xb"][...]) for n in range(3)]
    packer.squares(dqkv + [dwo, dwe])
    send(1, FF_ROWS, LAYER_ROWS - FF_ROWS)
    lane = lax.broadcasted_iota(jnp.int32, (ROWS, NCOL), 1).astype(F32)
    one_hot = (cols[:, 3:4] * 256.0 + cols[:, 4:5] == lane).astype(BF16)
    dtable = mm_tn(ge[:, :EP], one_hot)
    for half in range(2):
        packer.at = half * HALF + LAYER_ROWS
        packer.whole(dtable[:, half * 256 : (half + 1) * 256])
        buf[packer.at : (half + 1) * HALF, :] = jnp.zeros(
            ((half + 1) * HALF - packer.at, 128), BF16
        )
        send(half, LAYER_ROWS, HALF - LAYER_ROWS)
    for copy in outs:
        copy.wait()
    sent_wait()


BIG = ("table", "wq", "wk", "wv", "wo", "w1", "w2", "we")
SMALL = {"b1": FF, "b2": D, "g2": D, "s2": D, "g1": D, "s1": D, "bo": D, "be": D}


def unpack_half(half, layer, buf, out, vectors, ff_stage, square_stage, head_stage, table_stage,
                sems):
    stores = []

    def store(value, to):
        copy = pltpu.make_async_copy(value, to, sems.at[len(stores)])
        copy.start()
        stores.append(copy)

    def strip(at, rows):
        return buf[at : at + rows, :].astype(F32)

    def rest(at, rows, n, lanes):
        first = at + (n // 2) * rows
        return strip(first, rows)[:, 64 * (n % 2) : 64 * (n % 2) + lanes]

    for m in range(9):
        both = strip(m * STRIP, STRIP)
        ff_stage[0, :, m * 128 : (m + 1) * 128] = both[:D]
        if m < 8:
            vectors[m * SPARE : (m + 1) * SPARE, :] = both[D:]
        ff_stage[1, :, m * 128 : (m + 1) * 128] = strip((9 + m) * STRIP, STRIP)[:D]
    for n, name in enumerate(("w1", "w2")):
        ff_stage[n, :, 9 * 128 :] = rest(18 * STRIP, STRIP, n, FF - 9 * 128)[:D]
        store(ff_stage.at[n], out[name].at[:, layer, :])
    at = FF_ROWS
    rests = at + 10 * EP
    for n, name in enumerate(("wq", "wk", "wv")):
        own = pl.ds(pl.multiple_of(own_heads() * GROUP, 16), GROUP)
        first, second, last = (
            buf.at[start : start + EP, :][own, :].astype(F32)[:75]
            for start in (at + 2 * n * EP, at + (2 * n + 1) * EP, rests + (n // 2) * EP)
        )
        last = last[:, 64 * (n % 2) : 64 * (n % 2) + 44]
        head_stage[n] = jnp.concatenate([first, second, last], 1)
        store(head_stage.at[n], out[name].at[:, layer, :])
    for n, name in ((3, "wo"), (4, "we")):
        lanes = 64 if n == 4 and layer == 0 else 44
        wide = jnp.concatenate(
            [strip(at + 2 * n * EP, EP), strip(at + (2 * n + 1) * EP, EP),
             rest(rests, EP, n, lanes)], 1,
        )
        if lanes == 64:
            wide = lanes_from_groups(wide)
        for group in range(4):
            square_stage[n - 3, group * 75 : (group + 1) * 75, :] = wide[
                group * GROUP : group * GROUP + 75
            ]
        store(square_stage.at[n - 3], out[name].at[:, layer, :])
    for n in range(2):
        part = strip(LAYER_ROWS + n * EP, EP)
        for group in range(4):
            table_stage[group * 75 : (group + 1) * 75, n * 128 : (n + 1) * 128] = part[
                group * GROUP : group * GROUP + 75
            ]
    store(table_stage, out["table"].at[:, half * 256 : (half + 1) * 256])
    for copy in stores:
        copy.wait()


def unpack_own(source, *rest):
    out = dict(zip(BIG, rest))
    vectors, buf, *stages, sems, in_sem = rest[len(BIG) :]
    copy = pltpu.make_async_copy(source, buf, in_sem.at[0])
    copy.start()
    copy.wait()
    core = lax.axis_index("c")
    for half in range(2):
        @pl.when(core == half)
        def unpack():
            unpack_half(half, 1 - half, buf, out, vectors, *stages, sems)


def unpack_other(source, own_vectors, *rest):
    rest = rest[len(BIG) :]
    out = dict(zip(BIG, rest))
    small = dict(zip(SMALL, rest[len(BIG) :]))
    vectors, buf, *stages, sems, in_sem = rest[len(BIG) + len(SMALL) :]
    copy = pltpu.make_async_copy(source, buf, in_sem.at[0])
    copy.start()
    copy.wait()
    core = lax.axis_index("c")
    for half in range(2):
        @pl.when(core != half)
        def unpack():
            unpack_half(half, 1 - half, buf, out, vectors, *stages, sems)
            for layer, block in ((1 - half, vectors), (half, own_vectors)):
                row = 0
                for name in list(SMALL)[:-1]:
                    width = SMALL[name]
                    for lane in range(0, width, 128):
                        size = min(128, width - lane)
                        small[name][layer : layer + 1, lane : lane + size] = block[
                            row : row + 1, :size
                        ]
                        row += 1
                bias = jnp.concatenate([block[row + n : row + n + 1, :] for n in range(3)], 1)
                small["be"][layer : layer + 1, :] = (
                    lanes_from_groups(bias) if layer == 0 else bias[:, :D]
                )


def shape(dims, kind):
    return jax.ShapeDtypeStruct(dims, kind)


SMEM = pl.BlockSpec(memory_space=pltpu.SMEM)
VMEM = pl.BlockSpec(memory_space=pltpu.VMEM)
ANY = pl.BlockSpec(memory_space=pl.ANY)


def params(mib):
    return pltpu.CompilerParams(vmem_limit_bytes=mib * MIB)


def cost(flops, moved):
    return pl.CostEstimate(flops=int(flops), bytes_accessed=int(moved), transcendentals=0)


RING_UP = [(n, (n + 1) % 4) for n in range(4)]
RING_DOWN = [(n, (n + 3) % 4) for n in range(4)]
SWAP = [(0, 1), (1, 0)]
CHIPS = ("x", "z", "yh", "yl")
ALONG_Y = ("yh", "yl")


def add_cores(mine, other):
    return (mine.astype(F32) + lax.ppermute(other, "c", SWAP).astype(F32)).astype(BF16)


def scatter_chips(half):
    rows = half.shape[0] // 64
    parts = lax.all_to_all(half, CHIPS, 0, 0, tiled=True).reshape(64, rows, 128)
    return jnp.sum(parts.astype(F32), 0).astype(BF16)


def gather_chips(total):
    rows = total.shape[0]
    spread = jnp.broadcast_to(total[None], (64, rows, 128)).reshape(64 * rows, 128)
    return lax.all_to_all(spread, CHIPS, 0, 0, tiled=True)


def body(
    nodes, edge_table, edge_index, star_sizes, leaf_drop, missing, w_query, w_key, w_value, w_out,
    b_out, ln1_gain, ln1_bias, w_ff1, b_ff1, w_ff2, b_ff2, ln2_gain, ln2_bias, w_edge, b_edge,
    d_nodes_out, d_edges_out,
):
    def to_rows(value):
        return jnp.transpose(value, (1, 0, 2)).reshape(ROWS, D)

    def to_stars(value):
        return jnp.transpose(value.reshape(SLOTS, STARS, D), (1, 0, 2))

    w_ff2 = jnp.transpose(w_ff2, (0, 2, 1))
    own = pl.pallas_call(
        pack_kernel,
        out_shape=[shape((3 * GROUP, D), BF16)] * 2,
        in_specs=[VMEM] * 3,
        out_specs=[VMEM] * 2,
        cost_estimate=cost(1e6, 1e6),
        name="pack",
    )(*[jnp.transpose(w, (2, 0, 1)) for w in (w_query, w_key, w_value)])
    near = [
        lax.ppermute(w, ALONG_Y, ring) for w, ring in zip(own, (RING_UP, RING_DOWN))
    ]
    plain = Layout(major_to_minor=(0, 1, 2))
    moved = [with_layout_constraint(w, plain) for w in (w_ff1, w_ff2, w_out, w_edge)]
    *near, w_ff1, w_ff2, w_out, w_edge = lax.optimization_barrier((*near, *moved))
    core = [lax.ppermute(w, "c", SWAP) for w in own]
    far = [lax.ppermute(w, "c", SWAP) for w in near]

    def scratch(specs):
        return [pltpu.VMEM(*spec) for spec in specs.values()]

    loaded = dict(
        own0=own[0], core0=core[0], near0=near[0], far0=far[0],
        own1=own[1], core1=core[1], near1=near[1], far1=far[1],
        nodes=to_rows(nodes), w1=w_ff1, w2=w_ff2, dnodes=to_rows(d_nodes_out),
        dedges=to_rows(d_edges_out), table=edge_table.T, w_out_in=w_out, wedge_in=w_edge,
        index=edge_index, missing=missing, drop=leaf_drop,
    )
    nodes_out, edges_out, grad_nodes, mine, other = pl.pallas_call(
        main_kernel,
        out_shape=[
            shape((ROWS, D), BF16), shape((ROWS, D), BF16), shape((ROWS, D), F32),
            shape((HALF, 128), BF16), shape((HALF, 128), BF16),
        ],
        in_specs=[SMEM] + [VMEM] * 8 + [ANY] * len(LOADS),
        out_specs=[ANY] * 5,
        scratch_shapes=[
            *scratch(KEEP), *scratch(KEEP), *scratch(LOADS), *scratch(WORK),
            pltpu.SemaphoreType.DMA((len(LOADS),)), pltpu.SemaphoreType.DMA((8,)),
        ],
        compiler_params=params(62),
        cost_estimate=cost(1.2e10, 3e7),
        name="layers",
    )(star_sizes, b_edge, b_out, ln1_gain, ln1_bias, b_ff1, b_ff2, ln2_gain, ln2_bias,
      *[loaded[name] for name in LOADS])

    mine = gather_chips(scatter_chips(add_cores(mine, other)))
    other = lax.ppermute(mine, "c", SWAP)

    def head():
        return shape((75, 2, D), F32)

    square = shape((D, 2, D), F32)
    wide = shape((D, 2, FF), F32)
    big = [shape((D, NCOL), F32), head(), head(), head(), square, wide, wide, square]
    stages = [
        pltpu.VMEM((HALF, 128), BF16), pltpu.VMEM((2, D, FF), F32), pltpu.VMEM((2, D, D), F32),
        pltpu.VMEM((3, 75, D), F32), pltpu.VMEM((D, 256), F32), pltpu.SemaphoreType.DMA((8,)),
        pltpu.SemaphoreType.DMA((1,)),
    ]
    outs = pl.pallas_call(
        unpack_own,
        out_shape=[*big, shape((32, 128), F32)],
        in_specs=[ANY],
        out_specs=[ANY] * len(BIG) + [VMEM],
        scratch_shapes=stages,
        compiler_params=params(30),
        cost_estimate=cost(1e8, 1e7),
        name="unpack_own",
    )(mine)
    outs = pl.pallas_call(
        unpack_other,
        out_shape=[*big, *[shape((2, n), F32) for n in SMALL.values()]],
        in_specs=[ANY, VMEM] + [ANY] * len(BIG),
        out_specs=[ANY] * len(BIG) + [VMEM] * len(SMALL),
        scratch_shapes=[pltpu.VMEM((32, 128), F32), *stages],
        input_output_aliases={n + 2: n for n in range(len(BIG))},
        compiler_params=params(30),
        cost_estimate=cost(1e8, 1e7),
        name="unpack_other",
    )(other, outs[-1], *outs[:-1])
    table, wq, wk, wv, wo, w1, w2, we, b1, b2, g2, s2, g1, s1, bo, be = outs
    wq, wk, wv = (jnp.transpose(t, (1, 2, 0)) for t in (wq, wk, wv))
    wo, w1, we = (jnp.transpose(t, (1, 0, 2)) for t in (wo, w1, we))
    w2 = jnp.transpose(w2, (1, 2, 0))
    return (
        to_stars(nodes_out), to_stars(edges_out), to_stars(grad_nodes), table.T,
        wq, wk, wv, wo, bo, g1, s1, w1, b1, w2, b2, g2, s2, we, be,
    )


def solution(mesh):
    devices = mesh.devices.reshape(4, 4, 2, 2, 2)
    fine = Mesh(devices, ("x", "z", "yh", "yl", "c"))
    graphs = ("x", "z", "yh")
    heads = ("yl", "c")
    everyone = graphs + heads
    rows3 = P(everyone, None, None)
    rows2 = P(everyone, None)
    per_head = P(None, None, heads)
    return jax.shard_map(
        body,
        mesh=fine,
        in_specs=(
            rows3, P(), rows2, P(graphs), P(graphs, None), rows2, per_head, per_head, per_head,
            *[P()] * 12, rows3, rows3,
        ),
        out_specs=(rows3, rows3, rows3, P(), per_head, per_head, per_head, *[P()] * 12),
        check_vma=False,
    )
```

```python
import math

import jax
import jax.numpy as jnp
from jax import lax
from jax.experimental import pallas as pl
from jax.experimental.layout import Layout, with_layout_constraint
from jax.experimental.pallas import tpu as pltpu
from jax.sharding import Mesh, PartitionSpec as P

D = 300
DP = 384
FF = 1200
HD = 25
SLOTS = 100
STARS = 8
ROWS = STARS * SLOTS
HL = 128
NCOL = 512
SCALE = 1.0 / math.sqrt(HD)
CHUNK = 800
CHUNKS = ROWS // CHUNK
STRIP = 304
GROUP = 80
EP = 4 * GROUP
SPARE = STRIP - D
COMMON = 8192
HEADS = 1024
LEFT = 640
MAIN_ROWS = 22 * STRIP
LAST_CUT = COMMON - 26 * STRIP
F32 = jnp.float32
BF16 = jnp.bfloat16
MIB = 1 << 20


def mm(left, right):
    return lax.dot_general(left, right, (((1,), (0,)), ((), ())), preferred_element_type=F32)


def mm_nt(left, right):
    return lax.dot_general(left, right, (((1,), (1,)), ((), ())), preferred_element_type=F32)


def mm_tn(left, right):
    return lax.dot_general(left, right, (((0,), (0,)), ((), ())), preferred_element_type=F32)


def chunk_rows(index):
    return slice(index * CHUNK, (index + 1) * CHUNK)


def by_slot(value):
    return value.reshape(value.shape[0] // 8, 8, value.shape[1])


def flat(value):
    return value.reshape(value.shape[0] * 8, value.shape[2])


def spread_heads():
    row = lax.broadcasted_iota(jnp.int32, (HL, 2 * DP), 0)
    lane = lax.broadcasted_iota(jnp.int32, (HL, 2 * DP), 1)
    second = lane >= DP
    lane = jnp.where(second, lane - DP, lane)
    head = jnp.where(second, row - 16, row)
    steps = sum((head >= n).astype(jnp.int32) for n in (3, 6, 9))
    offset = lane - head * HD - steps * (GROUP - 3 * HD)
    real = (head >= 0) & (head < 12)
    return ((offset >= 0) & (offset < HD) & real).astype(BF16)


def group_order():
    row = lax.broadcasted_iota(jnp.int32, (DP, D), 0)
    lane = lax.broadcasted_iota(jnp.int32, (DP, D), 1)
    steps = sum((lane >= n * 75).astype(jnp.int32) for n in (1, 2, 3))
    return (row == lane + steps * (GROUP - 75)).astype(BF16)


def lanes_from_groups(value):
    return jnp.concatenate([value[:, n * GROUP : n * GROUP + 75] for n in range(4)], 1)


def gelu_parts(x):
    share = 0.5 + 0.5 * lax.erf(x * 0.7071067811865476)
    return x * share, share + x * (jnp.exp(-0.5 * x * x) * 0.3989422804014327)


def normalize(hidden):
    center = hidden - jnp.sum(hidden, -1, keepdims=True) * (1.0 / D)
    spread = jnp.sum(center * center, -1, keepdims=True) * (1.0 / D)
    root = lax.rsqrt(spread + 1e-05)
    return center * root, root


def norm_back(grad, gain, normed, root):
    scaled = grad * gain
    first = jnp.sum(scaled, -1, keepdims=True) * (1.0 / D)
    second = jnp.sum(scaled * normed, -1, keepdims=True) * (1.0 / D)
    return root * (scaled - first - normed * second)


def own_heads():
    return lax.axis_index("yl") * 2 + lax.axis_index("c")


def pack_kernel(wq, wk, wv, first, second):
    for layer, out in enumerate((first, second)):
        for n, w in enumerate((wq, wk, wv)):
            rows = jnp.concatenate([w[:, layer, :].astype(F32), jnp.zeros((GROUP - 75, D), F32)], 0)
            out[n * GROUP : (n + 1) * GROUP, :] = rows.astype(BF16)


def edges_forward(sizes, t, bedge):
    index, missing, drop, table, wedge = (
        t[name] for name in ("index", "missing", "drop", "table", "wedge_in")
    )
    cols_out, e0_out, e1_out, w_out_out, wedge_out, back_out, dw_out = (
        t[name] for name in ("cols", "e0", "e1", "w_out", "wedge", "back", "dw")
    )
    order = group_order()
    for layer in range(2):
        w_out_out[layer] = mm(order, t["w_out_in"][layer]).astype(BF16)
    wedge_out[...] = mm_nt(mm(order, wedge[0]).astype(BF16), order).astype(BF16)
    wedge_last = mm(order, wedge[1]).astype(BF16)
    grouped = mm(order, table[...]).astype(BF16)
    bias = bedge[0:1]
    high = bias.astype(BF16).astype(F32)
    middle = (bias - high).astype(BF16).astype(F32)
    terms = jnp.concatenate([high, middle, bias - high - middle, jnp.zeros((5, D), F32)], 0)
    bias = jnp.sum(mm_nt(terms.astype(BF16), order), 0, keepdims=True)
    slot = lax.broadcasted_iota(jnp.int32, (STARS, SLOTS), 1)
    star = lax.broadcasted_iota(jnp.int32, (STARS, SLOTS), 0)
    first = own_heads() * STARS
    size = jnp.zeros((STARS, SLOTS), jnp.int32)
    for n in range(STARS):
        size = jnp.where(star == n, sizes[first + n], size)
    dropped = drop[pl.ds(pl.multiple_of(first, 8), STARS), :]
    present = (slot == 0) | (missing[...] == 0)
    valid = slot < size
    key_ok = valid & ((slot == 0) | (dropped == 0))
    number = index[...]
    flags = jnp.concatenate(
        [t.astype(F32) for t in (present, valid, key_ok, number >> 8, number & 255)], 0
    ).astype(BF16)
    row = lax.broadcasted_iota(jnp.int32, (ROWS, SLOTS), 0)
    lane = lax.broadcasted_iota(jnp.int32, (ROWS, SLOTS), 1)
    all_stars = mm_nt(((row >> 3) == lane).astype(BF16), flags)
    row = lax.broadcasted_iota(jnp.int32, (ROWS, 5 * STARS), 0)
    lane = lax.broadcasted_iota(jnp.int32, (ROWS, 5 * STARS), 1)
    own = jnp.where((row & 7) == (lane & 7), all_stars, 0.0).astype(BF16)
    row = lax.broadcasted_iota(jnp.int32, (5 * STARS, HL), 0)
    lane = lax.broadcasted_iota(jnp.int32, (5 * STARS, HL), 1)
    cols = mm(own, ((row >> 3) == lane).astype(BF16))
    cols_out[...] = cols
    picked = cols[:, 3:4] * 256.0 + cols[:, 4:5]
    lane = lax.broadcasted_iota(jnp.int32, (CHUNK, NCOL), 1).astype(F32)
    for i in range(CHUNKS):
        rows = chunk_rows(i)
        one_hot = (picked[rows] == lane).astype(BF16)
        e0 = mm_nt(one_hot, grouped).astype(BF16)
        e1 = (mm(e0, wedge_out[...]) + bias).astype(BF16)
        e0_out[rows, :] = e0
        e1_out[rows, :] = e1

    def others():
        t["edges"][...] = (mm(e1_out[...], wedge_last) + bedge[1:2]).astype(BF16)
        low = t["dedges"][...]
        back_out[...] = mm_nt(low, wedge_last)
        dw_out[...] = mm_tn(e1_out[:, :EP], low)

    return others


def attention_forward(x_in, layer, w_qkv, e, keep, cols, beside=None):
    spread = spread_heads()
    scores = []
    center = None
    for i in range(CHUNKS):
        rows = chunk_rows(i)
        low = x_in(i).astype(BF16)
        keep["xb"][rows, :] = low
        projected = mm_nt(low, w_qkv[layer])
        edge = e[rows, :].astype(F32)
        query = projected[:, :DP]
        key_full = projected[:, DP : 2 * DP]
        value_full = projected[:, 2 * DP :]
        key = key_full * edge
        value = value_full * edge
        keep["kf"][rows, :] = key_full.astype(BF16)
        keep["vf"][rows, :] = value_full.astype(BF16)
        keep["q"][rows, :] = query.astype(BF16)
        keep["k"][rows, :] = key.astype(BF16)
        keep["v"][rows, :] = value.astype(BF16)
        if i == 0:
            center = (query[:8], key[:8])
            keep["c0"][0] = query[:8]
            keep["c0"][1] = key[:8]
            keep["c0"][2] = value[:8]
        keys = by_slot(key)
        of_center = flat(keys * center[0][None])
        of_gap = flat((center[1][None] - keys) * by_slot(query))
        products = jnp.concatenate([of_center.astype(BF16), of_gap.astype(BF16)], 1)
        scores.append(mm_nt(products, spread))
    if beside is not None:
        beside()
    score = jnp.concatenate(scores, 0) * SCALE
    lane = lax.broadcasted_iota(jnp.int32, (ROWS, HL), 1)
    row = lax.broadcasted_iota(jnp.int32, (ROWS, HL), 0)
    is_gap = lane >= 16
    open_ = cols[:, 2:3] > 0.0
    masked = by_slot(jnp.where(open_, score, -1e30))
    lowered = flat(masked - jnp.max(masked, 0, keepdims=True))
    expo = jnp.exp(jnp.where(is_gap, -jnp.abs(score), lowered))
    expo = jnp.where(is_gap | open_, expo, 0.0)
    total = by_slot(expo)
    probs = flat(total / jnp.sum(total, 0, keepdims=True))
    large = 1.0 / (1.0 + expo)
    toward = jnp.where(row < 8, 0.0, jnp.where(score >= 0.0, large, expo * large))
    weight = jnp.where(is_gap, toward, probs)
    keep["w"][...] = weight
    return weight.astype(BF16)


def rest_forward(x_in, layer, weights, weight, keep, cols, x_out):
    w_out, b_out, g1, s1, w1, b1, w2, b2, g2, s2 = weights
    spread = spread_heads()
    value_center = keep["c0"][2][None]
    outs = []
    total = None
    for i in range(CHUNKS):
        rows = chunk_rows(i)
        wide = mm(weight[rows], spread)
        keep["ww"][rows, :] = wide.astype(BF16)
        values = by_slot(keep["v"][rows, :].astype(F32))
        part = jnp.sum(by_slot(wide[:, :DP]) * values, 0)
        total = part if total is None else total + part
        out = flat(values + by_slot(wide[:, DP:]) * (value_center - values))
        keep["ob"][rows, :] = out.astype(BF16)
    out = keep["ob"][:16, :].astype(F32)
    keep["ob"][:16, :] = jnp.concatenate([total, out[8:]], 0).astype(BF16)
    for i in range(CHUNKS):
        rows = chunk_rows(i)
        hidden = x_in(i) + mm(keep["ob"][rows, :], w_out[layer]) + b_out[layer : layer + 1]
        normed, root = normalize(hidden)
        keep["n1"][rows, :] = normed
        keep["r"][rows, 0:1] = root
        first = normed * g1[layer : layer + 1] + s1[layer : layer + 1]
        first_low = first.astype(BF16)
        keep["n1b"][rows, :] = first_low
        act, slope = gelu_parts(mm(first_low, w1[layer]) + b1[layer : layer + 1])
        act_low = act.astype(BF16)
        keep["g"][rows, :] = act_low
        keep["gp"][rows, :] = slope.astype(BF16)
        second, root = normalize(first + mm_nt(act_low, w2[layer]) + b2[layer : layer + 1])
        keep["n2"][rows, :] = second
        keep["r"][rows, 1:2] = root
        result = second * g2[layer : layer + 1] + s2[layer : layer + 1]
        x_out(i, result * cols[rows, 1:2])


def ff_backward(grad_x, keep, cols, weights, layer, gf1, gf2, ga, gh1, beside=None):
    w1, w2, g1, g2 = weights
    sums = None
    for i in range(CHUNKS):
        rows = chunk_rows(i)
        grad = grad_x(i) * cols[rows, 1:2]
        normed = keep["n2"][rows, :]
        back = norm_back(grad, g2[layer : layer + 1], normed, keep["r"][rows, 1:2])
        if i == 0 and beside is not None:
            beside()
        low = back.astype(BF16)
        gf2[rows, :] = low
        slope = keep["gp"][rows, :].astype(F32) * mm(low, w2[layer])
        slope_low = slope.astype(BF16)
        gf1[rows, :] = slope_low
        back_one = back + mm_nt(slope_low, w1[layer])
        normed_one = keep["n1"][rows, :]
        hidden = norm_back(back_one, g1[layer : layer + 1], normed_one, keep["r"][rows, 0:1])
        gh1[rows, :] = hidden
        ga[rows, :] = hidden.astype(BF16)
        part = (
            jnp.sum(slope, 0, keepdims=True),
            jnp.sum(back, 0, keepdims=True),
            jnp.sum(grad * normed, 0, keepdims=True),
            jnp.sum(grad, 0, keepdims=True),
            jnp.sum(back_one * normed_one, 0, keepdims=True),
            jnp.sum(back_one, 0, keepdims=True),
            jnp.sum(hidden, 0, keepdims=True),
        )
        sums = part if sums is None else tuple(a + b for a, b in zip(sums, part))
    return sums


def attention_backward(ga, w_out, layer, keep, e, w_qkv, gh1, go, gqkv, x_out, e_out, beside):
    spread = spread_heads()
    query_center, key_center, value_center = (keep["c0"][n][None] for n in range(3))
    dots = []
    grad_center = None
    for i in range(CHUNKS):
        rows = chunk_rows(i)
        grad = mm_nt(ga[rows, :], w_out[layer])
        if i == 0:
            grad_center = grad[:8].astype(BF16).astype(F32)[None]
            grad = jnp.concatenate([jnp.zeros((8, DP), F32), grad[8:]], 0)
        go[rows, :] = grad.astype(BF16)
        values = by_slot(keep["v"][rows, :].astype(F32))
        of_center = flat(grad_center * values)
        of_gap = flat(by_slot(grad) * (value_center - values))
        products = jnp.concatenate([of_center.astype(BF16), of_gap.astype(BF16)], 1)
        dots.append(mm_nt(products, spread))
    beside[0]()
    dot = jnp.concatenate(dots, 0)
    weight = keep["w"][...]
    lane = lax.broadcasted_iota(jnp.int32, (ROWS, HL), 1)
    mean = jnp.sum(by_slot(weight * dot), 0, keepdims=True)
    of_probs = flat(by_slot(dot) - mean)
    grads = weight * jnp.where(lane >= 16, (1.0 - weight) * dot, of_probs) * SCALE
    grads = grads.astype(BF16)
    beside[1]()
    sums = None
    for i in reversed(range(CHUNKS)):
        rows = chunk_rows(i)
        wide = mm(grads[rows], spread)
        of_score = by_slot(wide[:, :DP])
        of_gap = by_slot(wide[:, DP:])
        query = by_slot(keep["q"][rows, :].astype(F32))
        key = by_slot(keep["k"][rows, :].astype(F32))
        grad = by_slot(go[rows, :].astype(F32))
        weights = keep["ww"][rows, :].astype(F32)
        probs = by_slot(weights[:, :DP])
        toward = by_slot(weights[:, DP:])
        edge = e[rows, :].astype(F32)
        pulled = of_gap * query
        moved = toward * grad
        part = (jnp.sum(of_score * key, 0), jnp.sum(pulled, 0), jnp.sum(moved, 0))
        sums = part if sums is None else tuple(a + b for a, b in zip(sums, part))
        of_q = of_gap * (key_center - key)
        of_k = of_score * query_center - pulled
        of_v = probs * grad_center + grad - moved
        if i == 0:
            of_q, of_k, of_v = (
                jnp.concatenate([t[:1] + s[None], t[1:]], 0)
                for t, s in zip((of_q, of_k, of_v), sums)
            )
        of_k, of_v = flat(of_k), flat(of_v)
        gqkv[rows, :DP] = flat(of_q).astype(BF16)
        gqkv[rows, DP : 2 * DP] = (of_k * edge).astype(BF16)
        gqkv[rows, 2 * DP :] = (of_v * edge).astype(BF16)
        of_edge = of_k * keep["kf"][rows, :].astype(F32) + of_v * keep["vf"][rows, :].astype(F32)
        e_out(i, of_edge)
        x_out(i, gh1[rows, :] + mm(gqkv[rows, :], w_qkv[layer]))


def rows_from_groups(value):
    return jnp.concatenate([value[n * GROUP : n * GROUP + 75] for n in range(4)], 0)


class Packer:
    def __init__(self, common, heads, left):
        self.common, self.heads, self.left = common, heads, left
        self.at = self.lane = 0

    def strip(self, value, spare=None):
        if value.shape[0] < STRIP:
            spare = jnp.zeros((SPARE, 128), F32) if spare is None else spare
            value = jnp.concatenate([value, spare], 0)
        self.common[self.at : self.at + STRIP, :] = value.astype(BF16)
        self.at += STRIP

    def whole(self, value, spares=()):
        lanes = value.shape[1] // 128 * 128
        for lane in range(0, lanes, 128):
            n = lane // 128
            self.strip(value[:, lane : lane + 128], spares[n] if n < len(spares) else None)
        self.leave(value[:, lanes:])

    def leave(self, value):
        width = value.shape[1]
        if width:
            self.left[:D, self.lane : self.lane + width] = value
            self.lane += width

    def ff(self, dw1, dw2, vectors, stage):
        stage[...] = jnp.zeros_like(stage)
        row = 0
        for vector in vectors:
            for lane in range(0, vector.shape[1], 128):
                part = vector[:, lane : lane + 128]
                stage[row : row + 1, : part.shape[1]] = part
                row += 1
        self.whole(dw1, [stage[n * SPARE : (n + 1) * SPARE, :] for n in range(8)])
        self.whole(dw2)

    def projections(self, values, layer):
        for part, value in enumerate(values):
            low = value.astype(BF16)
            for group in range(4):
                for n in range(2):
                    at = (group // 2) * HEADS + ((layer * 3 + part) * 2 + n) * GROUP
                    self.heads[group % 2, at : at + GROUP, :] = low[
                        group * GROUP : (group + 1) * GROUP, n * 128 : (n + 1) * 128
                    ]
            self.leave(rows_from_groups(value[:, 256:]))


KEEP = {
    "n2": ((ROWS, D), F32),
    "r": ((ROWS, 2), F32),
    "gp": ((ROWS, FF), BF16),
    "n1": ((ROWS, D), F32),
    "g": ((ROWS, FF), BF16),
    "n1b": ((ROWS, D), BF16),
    "c0": ((3, 8, DP), F32),
    "v": ((ROWS, DP), BF16),
    "w": ((ROWS, HL), F32),
    "ww": ((ROWS, 2 * DP), BF16),
    "q": ((ROWS, DP), BF16),
    "k": ((ROWS, DP), BF16),
    "kf": ((ROWS, DP), BF16),
    "vf": ((ROWS, DP), BF16),
    "ob": ((ROWS, DP), BF16),
    "xb": ((ROWS, D), BF16),
}
LOADS = {
    "index": ((STARS, SLOTS), jnp.int32),
    "missing": ((STARS, SLOTS), jnp.int32),
    "drop": ((4 * STARS, SLOTS), jnp.int32),
    "w_out_in": ((2, D, D), BF16),
    "wedge_in": ((2, D, D), BF16),
    "table": ((D, NCOL), BF16),
    "dedges": ((ROWS, D), BF16),
    "own0": ((3 * GROUP, D), BF16),
    "core0": ((3 * GROUP, D), BF16),
    "near0": ((3 * GROUP, D), BF16),
    "far0": ((3 * GROUP, D), BF16),
    "nodes": ((ROWS, D), BF16),
    "w1": ((2, D, FF), BF16),
    "w2": ((2, D, FF), BF16),
    "own1": ((3 * GROUP, D), BF16),
    "core1": ((3 * GROUP, D), BF16),
    "near1": ((3 * GROUP, D), BF16),
    "far1": ((3 * GROUP, D), BF16),
    "dnodes": ((ROWS, D), BF16),
}
WORK = {
    "cols": ((ROWS, HL), F32),
    "e0": ((ROWS, DP), BF16),
    "e1": ((ROWS, DP), BF16),
    "w_out": ((2, DP, D), BF16),
    "wedge": ((DP, DP), BF16),
    "back": ((ROWS, DP), F32),
    "dw": ((EP, D), F32),
    "edges": ((ROWS, D), BF16),
    "w_qkv": ((2, 3 * DP, D), BF16),
    "x": ((ROWS, D), F32),
    "gf1": ((ROWS, FF), BF16),
    "gf2": ((ROWS, D), BF16),
    "ga": ((ROWS, D), BF16),
    "gh1": ((ROWS, D), F32),
    "go": ((ROWS, DP), BF16),
    "gqkv": ((ROWS, 3 * DP), BF16),
    "ge": ((ROWS, DP), BF16),
    "last": ((ROWS, D), F32),
    "common": ((2 * COMMON, 128), BF16),
    "heads": ((2, 2 * HEADS, 128), BF16),
    "left": ((STRIP, LEFT), F32),
    "stage": ((32, 128), F32),
}


def chunk_copy(rows, chunks, sem, out):
    rows = rows.reshape(*chunks.shape)
    return pltpu.make_async_copy(*((rows, chunks) if out else (chunks, rows)), sem)


class Loads:
    def __init__(self, sources, targets, sems):
        self.copies = {}
        for n, name in enumerate(LOADS):
            self.copies[name] = pltpu.make_async_copy(sources[name], targets[name], sems.at[n])
            self.copies[name].start()

    def wait(self, *names):
        for name in names:
            self.copies.pop(name).wait()


def main_kernel(star_sizes, bedge, b_out, g1, s1, b1, b2, g2, s2, *rest):
    count = len(KEEP)
    sources = dict(zip(LOADS, rest))
    rest = rest[len(LOADS) :]
    nodes_out, edges_out, grad_nodes, mine, other = rest[:5]
    keep0 = dict(zip(KEEP, rest[5:]))
    keep1 = dict(zip(KEEP, rest[5 + count :]))
    rest = rest[5 + 2 * count :]
    t = dict(zip(LOADS, rest))
    rest = rest[len(LOADS) :]
    work = dict(zip(WORK, rest))
    in_sems, out_sems = rest[len(WORK) :]
    loads = Loads(sources, t, in_sems)
    core = lax.axis_index("c")
    sent = []

    def send(which, part, first, chunks, at, rows):
        n = len(sent)
        for is_own, to in ((True, mine), (False, other)):
            place = to.at[first : first + chunks, at : at + rows, :]

            @pl.when((core == which) == is_own)
            def start():
                chunk_copy(part, place, out_sems.at[3 + n], True).start()

        sent.append((part, mine.at[first : first + chunks, at : at + rows, :]))

    def send_common(half, first, end):
        rows = common.at[half * COMMON + first * 128 : half * COMMON + end * 128, :]
        send(half, rows, first, end - first, 0, 128)

    def sent_wait():
        for n, (part, place) in enumerate(sent):
            chunk_copy(part, place, out_sems.at[3 + n], True).wait()

    t.update(work)
    w_qkv, x, gf1, gf2, ga, gh1, go, gqkv, ge, last, common, heads, left, stage = list(
        work.values()
    )[8:]
    cols, w_out, w1, w2 = t["cols"], t["w_out"], t["w1"], t["w2"]
    own = own_heads()

    def place(layer):
        names = [name + str(layer) for name in ("own", "core", "near", "far")]
        loads.wait(*names)
        for part in range(3):
            w_qkv[layer, part * DP + EP : (part + 1) * DP, :] = jnp.zeros((DP - EP, D), BF16)
            for n, name in enumerate(names):
                at = pl.multiple_of(part * DP + (own ^ n) * GROUP, 16)
                w_qkv[layer, pl.ds(at, GROUP), :] = t[name][part * GROUP : (part + 1) * GROUP, :]

    def x0(i):
        rows = chunk_rows(i)
        return t["nodes"][rows, :].astype(F32) * cols[rows, 0:1]

    def x1(i):
        return x[chunk_rows(i), :]

    def store_x(i, value):
        x[chunk_rows(i), :] = value

    def store_nodes(i, value):
        t["nodes"][chunk_rows(i), :] = value.astype(BF16)

    weights = (w_out, b_out, g1, s1, w1, b1, w2, b2, g2, s2)
    left[...] = jnp.zeros_like(left)
    loads.wait("index", "missing", "drop", "w_out_in", "wedge_in", "table", "dedges")
    edges_others = edges_forward(star_sizes, t, bedge)
    place(0)
    loads.wait("nodes")
    weight = attention_forward(x0, 0, w_qkv, t["e0"], keep0, cols, edges_others)
    outs = [pltpu.make_async_copy(t["edges"], edges_out, out_sems.at[0])]
    outs[0].start()
    loads.wait("w1", "w2")
    rest_forward(x0, 0, weights, weight, keep0, cols, store_x)
    place(1)
    weight = attention_forward(x1, 1, w_qkv, t["e1"], keep1, cols)
    rest_forward(x1, 1, weights, weight, keep1, cols, store_nodes)
    outs.append(pltpu.make_async_copy(t["nodes"], nodes_out, out_sems.at[1]))
    outs[1].start()

    loads.wait("dnodes")
    packer = Packer(common, heads, left)
    sums = ff_backward(
        lambda i: t["dnodes"][chunk_rows(i), :].astype(F32),
        keep1, cols, (w1, w2, g1, g2), 1, gf1, gf2, ga, gh1,
    )
    low = t["dedges"][...].astype(F32)
    vectors = [*sums, jnp.sum(low, 0, keepdims=True)]

    def store_ge(i, value):
        total = value.astype(BF16).astype(F32) + t["back"][chunk_rows(i), :]
        ge[chunk_rows(i), :] = total.astype(BF16)

    def ff_gradients(keep, vectors):
        packer.ff(
            mm_tn(keep["n1b"][...], gf1[...]), mm_tn(gf2[...], keep["g"][...]), vectors, stage
        )

    def out_gradient(keep):
        packer.whole(rows_from_groups(mm_tn(keep["ob"][:, :EP], ga[...])))

    def projection_gradients(keep, layer):
        packer.projections(
            [mm_tn(gqkv[:, n * DP : n * DP + EP], keep["xb"][...]) for n in range(3)], layer
        )

    def edge_gradient_one():
        out_gradient(keep1)
        packer.whole(rows_from_groups(t["dw"][...]))

    attention_backward(
        ga, w_out, 1, keep1, t["e1"], w_qkv, gh1, go, gqkv, store_x, store_ge,
        (lambda: ff_gradients(keep1, vectors), edge_gradient_one),
    )

    sums = ff_backward(
        x1, keep0, cols, (w1, w2, g1, g2), 0, gf1, gf2, ga, gh1,
        lambda: projection_gradients(keep1, 1),
    )
    send_common(0, 0, 52)
    packer.at = COMMON
    db_first = jnp.sum(ge[...].astype(F32), 0, keepdims=True)

    def store_last(i, value):
        rows = chunk_rows(i)
        last[rows, :] = value * cols[rows, 0:1]

    def edge_gradient_zero():
        out_gradient(keep0)
        dwe = mm_tn(t["e0"][:, :EP], ge[:, :EP])
        packer.whole(lanes_from_groups(rows_from_groups(dwe)))
        t["back"][...] = mm_nt(ge[...], t["wedge"][...])

    attention_backward(
        ga, w_out, 0, keep0, t["e0"], w_qkv, gh1, go, gqkv, store_last, store_ge,
        (lambda: ff_gradients(keep0, [*sums, db_first[:, :EP]]), edge_gradient_zero),
    )
    outs.append(pltpu.make_async_copy(last, grad_nodes, out_sems.at[2]))
    outs[2].start()
    send_common(1, 0, 52)
    projection_gradients(keep0, 0)
    zeros = jnp.zeros((HEADS - 12 * GROUP, 128), BF16)
    for n in range(2):
        for m in range(2):
            heads[n, m * HEADS + 12 * GROUP : (m + 1) * HEADS, :] = zeros
            part = heads.at[n, m * HEADS : (m + 1) * HEADS, :]
            send(n, part, 0, 64, 128 + 16 * m, 16)
    lane = lax.broadcasted_iota(jnp.int32, (ROWS, NCOL), 1).astype(F32)
    one_hot = (cols[:, 3:4] * 256.0 + cols[:, 4:5] == lane).astype(BF16)
    dtable = rows_from_groups(mm_tn(ge[:, :EP], one_hot))
    packer.at = MAIN_ROWS
    packer.whole(dtable[:, :384])
    packer.strip(left[:, :128])
    final = left[:, 512:].astype(BF16)
    common[packer.at : COMMON, :] = final[:LAST_CUT]
    packer.at = COMMON + MAIN_ROWS
    packer.whole(dtable[:, 384:])
    for n in range(1, 4):
        packer.strip(left[:, n * 128 : (n + 1) * 128])
    common[packer.at : packer.at + STRIP - LAST_CUT, :] = final[LAST_CUT:]
    packer.at += STRIP - LAST_CUT
    common[packer.at :, :] = jnp.zeros((2 * COMMON - packer.at, 128), BF16)
    send_common(0, 52, 64)
    send_common(1, 52, 64)
    for copy in outs:
        copy.wait()
    sent_wait()


BIG = ("table", "wq", "wk", "wv", "wo", "w1", "w2", "we")
SMALL = {"b1": FF, "b2": D, "g2": D, "s2": D, "g1": D, "s1": D, "bo": D, "be": D}
LEFT_ROWS = 3 * STRIP + STRIP - LAST_CUT


class Stores:
    def __init__(self, sems):
        self.sems, self.copies = sems, []

    def start(self, value, to):
        copy = pltpu.make_async_copy(value, to, self.sems.at[len(self.copies)])
        copy.start()
        self.copies.append(copy)

    def wait(self):
        for copy in self.copies:
            copy.wait()


def unpack_half(half, common, out, vectors, ff_stage, square_stage, table_stage, stores):
    layer = 1 - half

    def strip(n):
        return common[n * STRIP : (n + 1) * STRIP, :].astype(F32)

    for m in range(9):
        both = strip(m)
        ff_stage[0, :, m * 128 : (m + 1) * 128] = both[:D]
        if m < 8:
            vectors[m * SPARE : (m + 1) * SPARE, :] = both[D:]
    stores.start(ff_stage.at[0], out["w1"].at[:, layer, 0:1152])
    for m in range(9):
        ff_stage[1, :, m * 128 : (m + 1) * 128] = strip(9 + m)[:D]
    stores.start(ff_stage.at[1], out["w2"].at[:, layer, 0:1152])
    for n, name in enumerate(("wo", "we")):
        for m in range(2):
            square_stage[n, :, m * 128 : (m + 1) * 128] = strip(18 + 2 * n + m)[:D]
        stores.start(square_stage.at[n], out[name].at[:, layer, 0:256])
    first, count = ((0, 3), (3, 1))[half]
    for n in range(count):
        table_stage[:, n * 128 : (n + 1) * 128] = strip(22 + n)[:D]
    stores.start(
        table_stage.at[:, 0 : count * 128],
        out["table"].at[:, first * 128 : (first + count) * 128],
    )


def left_parts(half):
    if half == 0:
        return ((0, 0, STRIP), (4, 0, LAST_CUT))
    return tuple((n, 0, STRIP) for n in (1, 2, 3)) + ((4, LAST_CUT, STRIP - LAST_CUT),)


def left_first(half):
    return (25, 23)[half] * STRIP


def unpack_own(source, *rest):
    out = dict(zip(BIG, rest))
    vectors, left_out, common, *stages, heads, head_stage, sems, in_sems = rest[len(BIG) :]
    loads = [
        chunk_copy(common, source.at[:, 0:128, :], in_sems.at[0], False),
        chunk_copy(heads, source.at[:, 128:144, :], in_sems.at[1], False),
    ]
    for copy in loads:
        copy.start()
    for copy in loads:
        copy.wait()
    stores = Stores(sems)
    for layer in range(2):
        for part, name in enumerate(("wq", "wk", "wv")):
            n = layer * 3 + part
            for m in range(2):
                at = (2 * n + m) * GROUP
                head_stage[n, :, m * 128 : (m + 1) * 128] = heads[at : at + GROUP, :].astype(F32)[
                    :75
                ]
            stores.start(head_stage.at[n], out[name].at[:, layer, 0:256])
    core = lax.axis_index("c")
    for half in range(2):
        @pl.when(core == half)
        def unpack():
            mine = Stores(sems.at[pl.ds(6, 5)])
            unpack_half(half, common, out, vectors, *stages, mine)
            at, to = left_first(half), 0
            for _, _, rows in left_parts(half):
                left_out[to : to + rows, :] = common[at : at + rows, :]
                at += rows
                to += rows
            mine.wait()
    stores.wait()


def unpack_other(source, own_vectors, own_left, *rest):
    rest = rest[len(BIG) :]
    out = dict(zip(BIG, rest))
    small = dict(zip(SMALL, rest[len(BIG) :]))
    common, *stages, vectors, left, ff_rest, square_rest, head_rest, sems, in_sems = rest[
        len(BIG) + len(SMALL) :
    ]
    copy = chunk_copy(common, source.at[:, 0:128, :], in_sems.at[0], False)
    copy.start()
    copy.wait()
    core = lax.axis_index("c")
    for half in range(2):
        @pl.when(core != half)
        def unpack():
            theirs = Stores(sems.at[pl.ds(14, 5)])
            unpack_half(half, common, out, vectors, *stages, theirs)
            for which, rows_of, at in (
                (half, common, left_first(half)), (1 - half, own_left, 0),
            ):
                for n, row, rows in left_parts(which):
                    left[row : row + rows, n * 128 : (n + 1) * 128] = rows_of[
                        at : at + rows, :
                    ].astype(F32)
                    at += rows
            for layer, block in ((1 - half, vectors), (half, own_vectors)):
                row = 0
                for name in list(SMALL)[:-1]:
                    width = SMALL[name]
                    for lane in range(0, width, 128):
                        size = min(128, width - lane)
                        small[name][layer : layer + 1, lane : lane + size] = block[
                            row : row + 1, :size
                        ]
                        row += 1
                bias = jnp.concatenate([block[row + n : row + n + 1, :] for n in range(3)], 1)
                small["be"][layer : layer + 1, :] = (
                    lanes_from_groups(bias) if layer == 0 else bias[:, :D]
                )
            theirs.wait()
    stores = Stores(sems)
    row = lax.broadcasted_iota(jnp.int32, (75, STRIP), 0)
    lane = lax.broadcasted_iota(jnp.int32, (75, STRIP), 1)
    picked = mm((lane == row + own_heads() * 75).astype(BF16), left[...].astype(BF16))
    for layer in range(2):
        at = (1 - layer) * (LEFT // 2 - 4)
        for n, name in enumerate(("w1", "w2")):
            ff_rest[2 * layer + n] = left[:D, at : at + 48]
            stores.start(ff_rest.at[2 * layer + n], out[name].at[:, layer, 1152:1200])
            at += 48
        for n, name in enumerate(("wo", "we")):
            square_rest[2 * layer + n] = left[:D, at : at + 44]
            stores.start(square_rest.at[2 * layer + n], out[name].at[:, layer, 256:300])
            at += 44
        for n, name in enumerate(("wq", "wk", "wv")):
            head_rest[3 * layer + n] = picked[:, at : at + 44]
            stores.start(head_rest.at[3 * layer + n], out[name].at[:, layer, 256:300])
            at += 44
    stores.wait()


def shape(dims, kind):
    return jax.ShapeDtypeStruct(dims, kind)


SMEM = pl.BlockSpec(memory_space=pltpu.SMEM)
VMEM = pl.BlockSpec(memory_space=pltpu.VMEM)
ANY = pl.BlockSpec(memory_space=pl.ANY)


def params(mib):
    return pltpu.CompilerParams(vmem_limit_bytes=mib * MIB)


def cost(flops, moved):
    return pl.CostEstimate(flops=int(flops), bytes_accessed=int(moved), transcendentals=0)


RING_UP = [(n, (n + 1) % 4) for n in range(4)]
RING_DOWN = [(n, (n + 3) % 4) for n in range(4)]
SWAP = [(0, 1), (1, 0)]
CHIPS = ("x", "z", "yh", "yl")
ALONG_Y = ("yh", "yl")


def add_cores(mine, other):
    return (mine.astype(F32) + lax.ppermute(other, "c", SWAP).astype(F32)).astype(BF16)


def scatter_chips(half):
    parts = lax.all_to_all(half, CHIPS, 0, 0, tiled=True)
    return jnp.sum(parts.astype(F32), 0).astype(BF16)


def gather_chips(total):
    shares = [jnp.concatenate([total[:128], total[at : at + 16]], 0) for at in (128, 144)]
    spread = jnp.broadcast_to(jnp.stack(shares)[None], (32, 2, 144, 128))
    return lax.all_to_all(spread.reshape(64, 144, 128), CHIPS, 0, 0, tiled=True)


def body(
    nodes, edge_table, edge_index, star_sizes, leaf_drop, missing, w_query, w_key, w_value, w_out,
    b_out, ln1_gain, ln1_bias, w_ff1, b_ff1, w_ff2, b_ff2, ln2_gain, ln2_bias, w_edge, b_edge,
    d_nodes_out, d_edges_out,
):
    def to_rows(value):
        return jnp.transpose(value, (1, 0, 2)).reshape(ROWS, D)

    def to_stars(value):
        return jnp.transpose(value.reshape(SLOTS, STARS, D), (1, 0, 2))

    w_ff2 = jnp.transpose(w_ff2, (0, 2, 1))
    own = pl.pallas_call(
        pack_kernel,
        out_shape=[shape((3 * GROUP, D), BF16)] * 2,
        in_specs=[VMEM] * 3,
        out_specs=[VMEM] * 2,
        cost_estimate=cost(1e6, 1e6),
        name="pack",
    )(*[jnp.transpose(w, (2, 0, 1)) for w in (w_query, w_key, w_value)])
    near = [
        lax.ppermute(w, ALONG_Y, ring) for w, ring in zip(own, (RING_UP, RING_DOWN))
    ]
    plain = Layout(major_to_minor=(0, 1, 2))
    moved = [with_layout_constraint(w, plain) for w in (w_ff1, w_ff2)]
    *near, w_ff1, w_ff2 = lax.optimization_barrier((*near, *moved))
    core = [lax.ppermute(w, "c", SWAP) for w in own]
    far = [lax.ppermute(w, "c", SWAP) for w in near]

    def scratch(specs):
        return [pltpu.VMEM(*spec) for spec in specs.values()]

    loaded = dict(
        own0=own[0], core0=core[0], near0=near[0], far0=far[0],
        own1=own[1], core1=core[1], near1=near[1], far1=far[1],
        nodes=to_rows(nodes), w1=w_ff1, w2=w_ff2, dnodes=to_rows(d_nodes_out),
        dedges=to_rows(d_edges_out), table=edge_table.T, w_out_in=w_out, wedge_in=w_edge,
        index=edge_index, missing=missing, drop=leaf_drop,
    )
    nodes_out, edges_out, grad_nodes, mine, other = pl.pallas_call(
        main_kernel,
        out_shape=[
            shape((ROWS, D), BF16), shape((ROWS, D), BF16), shape((ROWS, D), F32),
            shape((64, 160, 128), BF16), shape((64, 160, 128), BF16),
        ],
        in_specs=[SMEM] + [VMEM] * 8 + [ANY] * len(LOADS),
        out_specs=[ANY] * 5,
        scratch_shapes=[
            *scratch(KEEP), *scratch(KEEP), *scratch(LOADS), *scratch(WORK),
            pltpu.SemaphoreType.DMA((len(LOADS),)), pltpu.SemaphoreType.DMA((12,)),
        ],
        compiler_params=params(62),
        cost_estimate=cost(1.2e10, 3e7),
        name="layers",
    )(star_sizes, b_edge, b_out, ln1_gain, ln1_bias, b_ff1, b_ff2, ln2_gain, ln2_bias,
      *[loaded[name] for name in LOADS])

    mine = gather_chips(scatter_chips(add_cores(mine, other)))
    other = lax.ppermute(mine, "c", SWAP)

    def head():
        return shape((75, 2, D), F32)

    square = shape((D, 2, D), F32)
    wide = shape((D, 2, FF), F32)
    big = [shape((D, NCOL), F32), head(), head(), head(), square, wide, wide, square]
    stages = [
        pltpu.VMEM((COMMON, 128), BF16), pltpu.VMEM((2, D, 1152), F32),
        pltpu.VMEM((2, D, 256), F32), pltpu.VMEM((D, 384), F32),
    ]
    outs = pl.pallas_call(
        unpack_own,
        out_shape=[*big, shape((32, 128), F32), shape((LEFT_ROWS, 128), BF16)],
        in_specs=[ANY],
        out_specs=[ANY] * len(BIG) + [VMEM] * 2,
        scratch_shapes=[
            *stages, pltpu.VMEM((HEADS, 128), BF16), pltpu.VMEM((6, 75, 256), F32),
            pltpu.SemaphoreType.DMA((11,)), pltpu.SemaphoreType.DMA((2,)),
        ],
        compiler_params=params(30),
        cost_estimate=cost(1e8, 1e7),
        name="unpack_own",
    )(mine)
    outs = pl.pallas_call(
        unpack_other,
        out_shape=[*big, *[shape((2, n), F32) for n in SMALL.values()]],
        in_specs=[ANY, VMEM, VMEM] + [ANY] * len(BIG),
        out_specs=[ANY] * len(BIG) + [VMEM] * len(SMALL),
        scratch_shapes=[
            *stages, pltpu.VMEM((32, 128), F32), pltpu.VMEM((STRIP, LEFT), F32),
            pltpu.VMEM((4, D, 48), F32), pltpu.VMEM((4, D, 44), F32), pltpu.VMEM((6, 75, 44), F32),
            pltpu.SemaphoreType.DMA((19,)), pltpu.SemaphoreType.DMA((1,)),
        ],
        input_output_aliases={n + 3: n for n in range(len(BIG))},
        compiler_params=params(30),
        cost_estimate=cost(1e8, 1e7),
        name="unpack_other",
    )(other, outs[-2], outs[-1], *outs[:-2])
    table, wq, wk, wv, wo, w1, w2, we, b1, b2, g2, s2, g1, s1, bo, be = outs
    wq, wk, wv = (jnp.transpose(t, (1, 2, 0)) for t in (wq, wk, wv))
    wo, w1, we = (jnp.transpose(t, (1, 0, 2)) for t in (wo, w1, we))
    w2 = jnp.transpose(w2, (1, 2, 0))
    return (
        to_stars(nodes_out), to_stars(edges_out), to_stars(grad_nodes), table.T,
        wq, wk, wv, wo, bo, g1, s1, w1, b1, w2, b2, g2, s2, we, be,
    )


def solution(mesh):
    devices = mesh.devices.reshape(4, 4, 2, 2, 2)
    fine = Mesh(devices, ("x", "z", "yh", "yl", "c"))
    graphs = ("x", "z", "yh")
    heads = ("yl", "c")
    everyone = graphs + heads
    rows3 = P(everyone, None, None)
    rows2 = P(everyone, None)
    per_head = P(None, None, heads)
    return jax.shard_map(
        body,
        mesh=fine,
        in_specs=(
            rows3, P(), rows2, P(graphs), P(graphs, None), rows2, per_head, per_head, per_head,
            *[P()] * 12, rows3, rows3,
        ),
        out_specs=(rows3, rows3, rows3, P(), per_head, per_head, per_head, *[P()] * 12),
        check_vma=False,
    )
```

```python
import math

import jax
import jax.numpy as jnp
from jax import lax
from jax.experimental import pallas as pl
from jax.experimental.layout import Layout, with_layout_constraint
from jax.experimental.pallas import tpu as pltpu
from jax.sharding import Mesh, PartitionSpec as P

D = 300
DP = 384
FF = 1200
HD = 25
SLOTS = 100
STARS = 8
ROWS = STARS * SLOTS
HL = 128
NCOL = 512
SCALE = 1.0 / math.sqrt(HD)
CHUNK = 800
CHUNKS = ROWS // CHUNK
STRIP = 304
GROUP = 80
EP = 4 * GROUP
QKV = 1024
SPARE = STRIP - D
COMMON = 8192
HEADS = 1024
LEFT = 640
MAIN_ROWS = 22 * STRIP
LAST_CUT = COMMON - 26 * STRIP
F32 = jnp.float32
BF16 = jnp.bfloat16
MIB = 1 << 20


def mm(left, right):
    return lax.dot_general(left, right, (((1,), (0,)), ((), ())), preferred_element_type=F32)


def mm_nt(left, right):
    return lax.dot_general(left, right, (((1,), (1,)), ((), ())), preferred_element_type=F32)


def mm_tn(left, right):
    return lax.dot_general(left, right, (((0,), (0,)), ((), ())), preferred_element_type=F32)


def chunk_rows(index):
    return slice(index * CHUNK, (index + 1) * CHUNK)


def by_slot(value):
    return value.reshape(value.shape[0] // 8, 8, value.shape[1])


def flat(value):
    return value.reshape(value.shape[0] * 8, value.shape[2])


def spread_heads():
    row = lax.broadcasted_iota(jnp.int32, (HL, 2 * DP), 0)
    lane = lax.broadcasted_iota(jnp.int32, (HL, 2 * DP), 1)
    second = lane >= DP
    lane = jnp.where(second, lane - DP, lane)
    head = jnp.where(second, row - 16, row)
    steps = sum((head >= n).astype(jnp.int32) for n in (3, 6, 9))
    offset = lane - head * HD - steps * (GROUP - 3 * HD)
    real = (head >= 0) & (head < 12)
    return ((offset >= 0) & (offset < HD) & real).astype(BF16)


def rows_to_groups(value):
    gap = jnp.zeros((GROUP - 75, value.shape[1]), F32)
    parts = [part for n in range(4) for part in (value[n * 75 : (n + 1) * 75], gap)]
    return jnp.concatenate([*parts, jnp.zeros((DP - EP, value.shape[1]), F32)], 0)


def lanes_to_groups(value):
    gap = jnp.zeros((value.shape[0], GROUP - 75), F32)
    parts = [part for n in range(4) for part in (value[:, n * 75 : (n + 1) * 75], gap)]
    return jnp.concatenate([*parts, jnp.zeros((value.shape[0], DP - EP), F32)], 1)


def lanes_from_groups(value):
    return jnp.concatenate([value[:, n * GROUP : n * GROUP + 75] for n in range(4)], 1)


def gelu_parts(x):
    share = 0.5 + 0.5 * lax.erf(x * 0.7071067811865476)
    return x * share, share + (x * 0.3989422804014327) * jnp.exp2((x * -0.7213475204444817) * x)


def normalize(hidden):
    center = hidden - jnp.sum(hidden, -1, keepdims=True) * (1.0 / D)
    spread = jnp.sum(center * center, -1, keepdims=True) * (1.0 / D)
    root = lax.rsqrt(spread + 1e-05)
    return center * root, root


def norm_back(grad, gain, normed, root):
    scaled = grad * gain
    first = jnp.sum(scaled, -1, keepdims=True) * (1.0 / D)
    second = jnp.sum(scaled * normed, -1, keepdims=True) * (1.0 / D)
    return root * (scaled - first - normed * second)


def own_heads():
    return lax.axis_index("yl") * 2 + lax.axis_index("c")


def pack_kernel(wq, wk, wv, first, second):
    for layer, out in enumerate((first, second)):
        for n, w in enumerate((wq, wk, wv)):
            rows = jnp.concatenate([w[:, layer, :].astype(F32), jnp.zeros((GROUP - 75, D), F32)], 0)
            out[n * GROUP : (n + 1) * GROUP, :] = rows.astype(BF16)


def edges_forward(sizes, t, bedge):
    index, missing, drop, table, wedge = (
        t[name] for name in ("index", "missing", "drop", "table", "wedge_in")
    )
    cols_out, e0_out, e1_out, w_out_out, wedge_out, back_out, dw_out = (
        t[name] for name in ("cols", "e0", "e1", "w_out", "wedge", "back", "dw")
    )
    for layer in range(2):
        w_out_out[layer] = rows_to_groups(t["w_out_in"][layer].astype(F32)).astype(BF16)
    wedge_out[...] = lanes_to_groups(rows_to_groups(wedge[0].astype(F32))).astype(BF16)
    wedge_last = rows_to_groups(wedge[1].astype(F32)).astype(BF16)
    grouped = rows_to_groups(table[...].astype(F32)).astype(BF16)
    bias = lanes_to_groups(bedge[0:1])
    slot = lax.broadcasted_iota(jnp.int32, (STARS, SLOTS), 1)
    star = lax.broadcasted_iota(jnp.int32, (STARS, SLOTS), 0)
    first = own_heads() * STARS
    size = jnp.zeros((STARS, SLOTS), jnp.int32)
    for n in range(STARS):
        size = jnp.where(star == n, sizes[first + n], size)
    dropped = drop[pl.ds(pl.multiple_of(first, 8), STARS), :]
    present = (slot == 0) | (missing[...] == 0)
    valid = slot < size
    key_ok = valid & ((slot == 0) | (dropped == 0))
    number = index[...]
    flags = jnp.concatenate(
        [t.astype(F32) for t in (present, valid, key_ok, number >> 8, number & 255)], 0
    ).astype(BF16)
    row = lax.broadcasted_iota(jnp.int32, (ROWS, SLOTS), 0)
    lane = lax.broadcasted_iota(jnp.int32, (ROWS, SLOTS), 1)
    all_stars = mm_nt(((row >> 3) == lane).astype(BF16), flags)
    row = lax.broadcasted_iota(jnp.int32, (ROWS, 5 * STARS), 0)
    lane = lax.broadcasted_iota(jnp.int32, (ROWS, 5 * STARS), 1)
    own = jnp.where((row & 7) == (lane & 7), all_stars, 0.0).astype(BF16)
    row = lax.broadcasted_iota(jnp.int32, (5 * STARS, HL), 0)
    lane = lax.broadcasted_iota(jnp.int32, (5 * STARS, HL), 1)
    cols = mm(own, ((row >> 3) == lane).astype(BF16))
    cols_out[...] = cols
    picked = cols[:, 3:4] * 256.0 + cols[:, 4:5]
    lane = lax.broadcasted_iota(jnp.int32, (CHUNK, NCOL), 1).astype(F32)
    for i in range(CHUNKS):
        rows = chunk_rows(i)
        one_hot = (picked[rows] == lane).astype(BF16)
        e0 = mm_nt(one_hot, grouped).astype(BF16)
        e1 = (mm(e0, wedge_out[...]) + bias).astype(BF16)
        e0_out[rows, :] = e0
        e1_out[rows, :] = e1

    def others():
        t["edges"][...] = (mm(e1_out[...], wedge_last) + bedge[1:2]).astype(BF16)
        low = t["dedges"][...]
        back_out[...] = mm_nt(low, wedge_last)
        dw_out[...] = mm_tn(e1_out[:, :EP], low)

    return others


def attention_forward(x_in, layer, w_qkv, e, keep, cols, beside=None):
    spread = spread_heads()
    scores = []
    center = None
    for i in range(CHUNKS):
        rows = chunk_rows(i)
        low = x_in(i).astype(BF16)
        keep["xb"][rows, :] = low
        projected = mm_nt(low, w_qkv[layer])
        edge = e[rows, :].astype(F32)
        last = projected[:, 768:896]
        query = jnp.concatenate([projected[:, :256], last], 1)
        key_full = jnp.concatenate([projected[:, 256:512], pltpu.roll(last, 64, 1)], 1)
        value_full = jnp.concatenate([projected[:, 512:768], projected[:, 896:]], 1)
        key = key_full * edge
        value = value_full * edge
        keep["kf"][rows, :] = key_full.astype(BF16)
        keep["vf"][rows, :] = value_full.astype(BF16)
        keep["q"][rows, :] = query.astype(BF16)
        keep["k"][rows, :] = key.astype(BF16)
        keep["v"][rows, :] = value.astype(BF16)
        if i == 0:
            center = (query[:8], key[:8])
            keep["c0"][0] = query[:8]
            keep["c0"][1] = key[:8]
            keep["c0"][2] = value[:8]
        keys = by_slot(key)
        of_center = flat(keys * center[0][None])
        of_gap = flat((center[1][None] - keys) * by_slot(query))
        products = jnp.concatenate([of_center.astype(BF16), of_gap.astype(BF16)], 1)
        scores.append(mm_nt(products, spread))
    if beside is not None:
        beside()
    score = jnp.concatenate(scores, 0) * SCALE
    lane = lax.broadcasted_iota(jnp.int32, (ROWS, HL), 1)
    row = lax.broadcasted_iota(jnp.int32, (ROWS, HL), 0)
    is_gap = lane >= 16
    open_ = cols[:, 2:3] > 0.0
    masked = by_slot(jnp.where(open_, score, -1e30))
    lowered = flat(masked - jnp.max(masked, 0, keepdims=True))
    expo = jnp.exp(jnp.where(is_gap, -jnp.abs(score), lowered))
    expo = jnp.where(is_gap | open_, expo, 0.0)
    total = by_slot(expo)
    probs = flat(total / jnp.sum(total, 0, keepdims=True))
    large = 1.0 / (1.0 + expo)
    toward = jnp.where(row < 8, 0.0, jnp.where(score >= 0.0, large, expo * large))
    weight = jnp.where(is_gap, toward, probs)
    keep["w"][...] = weight
    return weight.astype(BF16)


def rest_forward(x_in, layer, weights, weight, keep, cols, x_out):
    w_out, b_out, g1, s1, w1, b1, w2, b2, g2, s2 = weights
    spread = spread_heads()
    value_center = keep["c0"][2][None]
    outs = []
    total = None
    for i in range(CHUNKS):
        rows = chunk_rows(i)
        wide = mm(weight[rows], spread)
        keep["ww"][rows, :] = wide.astype(BF16)
        values = by_slot(keep["v"][rows, :].astype(F32))
        part = jnp.sum(by_slot(wide[:, :DP]) * values, 0)
        total = part if total is None else total + part
        out = flat(values + by_slot(wide[:, DP:]) * (value_center - values))
        keep["ob"][rows, :] = out.astype(BF16)
    out = keep["ob"][:16, :].astype(F32)
    keep["ob"][:16, :] = jnp.concatenate([total, out[8:]], 0).astype(BF16)
    for i in range(CHUNKS):
        rows = chunk_rows(i)
        hidden = x_in(i) + mm(keep["ob"][rows, :], w_out[layer]) + b_out[layer : layer + 1]
        normed, root = normalize(hidden)
        keep["n1"][rows, :] = normed
        keep["r"][rows, 0:1] = root
        first = normed * g1[layer : layer + 1] + s1[layer : layer + 1]
        first_low = first.astype(BF16)
        keep["n1b"][rows, :] = first_low
        act, slope = gelu_parts(mm(first_low, w1[layer]) + b1[layer : layer + 1])
        act_low = act.astype(BF16)
        keep["g"][rows, :] = act_low
        keep["gp"][rows, :] = slope.astype(BF16)
        second, root = normalize(first + mm_nt(act_low, w2[layer]) + b2[layer : layer + 1])
        keep["n2"][rows, :] = second
        keep["r"][rows, 1:2] = root
        result = second * g2[layer : layer + 1] + s2[layer : layer + 1]
        x_out(i, result * cols[rows, 1:2])


def ff_backward(grad_x, keep, cols, weights, layer, gf1, gf2, ga, gh1, beside=None):
    w1, w2, g1, g2 = weights
    sums = None
    for i in range(CHUNKS):
        rows = chunk_rows(i)
        grad = grad_x(i) * cols[rows, 1:2]
        normed = keep["n2"][rows, :]
        back = norm_back(grad, g2[layer : layer + 1], normed, keep["r"][rows, 1:2])
        if i == 0 and beside is not None:
            beside()
        low = back.astype(BF16)
        gf2[rows, :] = low
        slope = keep["gp"][rows, :].astype(F32) * mm(low, w2[layer])
        slope_low = slope.astype(BF16)
        gf1[rows, :] = slope_low
        back_one = back + mm_nt(slope_low, w1[layer])
        normed_one = keep["n1"][rows, :]
        hidden = norm_back(back_one, g1[layer : layer + 1], normed_one, keep["r"][rows, 0:1])
        gh1[rows, :] = hidden
        ga[rows, :] = hidden.astype(BF16)
        part = (
            jnp.sum(slope, 0, keepdims=True),
            jnp.sum(back, 0, keepdims=True),
            jnp.sum(grad * normed, 0, keepdims=True),
            jnp.sum(grad, 0, keepdims=True),
            jnp.sum(back_one * normed_one, 0, keepdims=True),
            jnp.sum(back_one, 0, keepdims=True),
            jnp.sum(hidden, 0, keepdims=True),
        )
        sums = part if sums is None else tuple(a + b for a, b in zip(sums, part))
    return sums


def attention_backward(ga, w_out, layer, keep, e, w_qkv, gh1, go, gqkv, x_out, e_out, beside):
    spread = spread_heads()
    query_center, key_center, value_center = (keep["c0"][n][None] for n in range(3))
    dots = []
    grad_center = None
    for i in range(CHUNKS):
        rows = chunk_rows(i)
        grad = mm_nt(ga[rows, :], w_out[layer])
        if i == 0:
            grad_center = grad[:8].astype(BF16).astype(F32)[None]
            grad = jnp.concatenate([jnp.zeros((8, DP), F32), grad[8:]], 0)
        go[rows, :] = grad.astype(BF16)
        values = by_slot(keep["v"][rows, :].astype(F32))
        of_center = flat(grad_center * values)
        of_gap = flat(by_slot(grad) * (value_center - values))
        products = jnp.concatenate([of_center.astype(BF16), of_gap.astype(BF16)], 1)
        dots.append(mm_nt(products, spread))
    beside[0]()
    dot = jnp.concatenate(dots, 0)
    weight = keep["w"][...]
    lane = lax.broadcasted_iota(jnp.int32, (ROWS, HL), 1)
    mean = jnp.sum(by_slot(weight * dot), 0, keepdims=True)
    of_probs = flat(by_slot(dot) - mean)
    grads = weight * jnp.where(lane >= 16, (1.0 - weight) * dot, of_probs) * SCALE
    grads = grads.astype(BF16)
    beside[1]()
    sums = None
    for i in reversed(range(CHUNKS)):
        rows = chunk_rows(i)
        wide = mm(grads[rows], spread)
        of_score = by_slot(wide[:, :DP])
        of_gap = by_slot(wide[:, DP:])
        query = by_slot(keep["q"][rows, :].astype(F32))
        key = by_slot(keep["k"][rows, :].astype(F32))
        grad = by_slot(go[rows, :].astype(F32))
        weights = keep["ww"][rows, :].astype(F32)
        probs = by_slot(weights[:, :DP])
        toward = by_slot(weights[:, DP:])
        edge = e[rows, :].astype(F32)
        pulled = of_gap * query
        moved = toward * grad
        part = (jnp.sum(of_score * key, 0), jnp.sum(pulled, 0), jnp.sum(moved, 0))
        sums = part if sums is None else tuple(a + b for a, b in zip(sums, part))
        of_q = of_gap * (key_center - key)
        of_k = of_score * query_center - pulled
        of_v = probs * grad_center + grad - moved
        if i == 0:
            of_q, of_k, of_v = (
                jnp.concatenate([t[:1] + s[None], t[1:]], 0)
                for t, s in zip((of_q, of_k, of_v), sums)
            )
        of_k, of_v = flat(of_k), flat(of_v)
        to_q, to_k, to_v = flat(of_q), of_k * edge, of_v * edge
        for n, value in enumerate((to_q, to_k, to_v)):
            gqkv[rows, n * 256 : (n + 1) * 256] = value[:, :256].astype(BF16)
        last = to_q[:, 256:] + pltpu.roll(to_k[:, 256:], 64, 1)
        gqkv[rows, 768:896] = last.astype(BF16)
        gqkv[rows, 896:] = to_v[:, 256:].astype(BF16)
        of_edge = of_k * keep["kf"][rows, :].astype(F32) + of_v * keep["vf"][rows, :].astype(F32)
        e_out(i, of_edge)
        x_out(i, gh1[rows, :] + mm(gqkv[rows, :], w_qkv[layer]))


def rows_from_groups(value):
    return jnp.concatenate([value[n * GROUP : n * GROUP + 75] for n in range(4)], 0)


class Packer:
    def __init__(self, common, heads, left):
        self.common, self.heads, self.left = common, heads, left
        self.at = self.lane = 0

    def strip(self, value, spare=None):
        if value.shape[0] < STRIP:
            spare = jnp.zeros((SPARE, 128), F32) if spare is None else spare
            value = jnp.concatenate([value, spare], 0)
        self.common[self.at : self.at + STRIP, :] = value.astype(BF16)
        self.at += STRIP

    def whole(self, value, spares=()):
        lanes = value.shape[1] // 128 * 128
        for lane in range(0, lanes, 128):
            n = lane // 128
            self.strip(value[:, lane : lane + 128], spares[n] if n < len(spares) else None)
        self.leave(value[:, lanes:])

    def leave(self, value):
        width = value.shape[1]
        if width:
            self.left[:D, self.lane : self.lane + width] = value
            self.lane += width

    def ff(self, dw1, dw2, vectors, stage):
        stage[...] = jnp.zeros_like(stage)
        row = 0
        for vector in vectors:
            for lane in range(0, vector.shape[1], 128):
                part = vector[:, lane : lane + 128]
                stage[row : row + 1, : part.shape[1]] = part
                row += 1
        self.whole(dw1, [stage[n * SPARE : (n + 1) * SPARE, :] for n in range(8)])
        self.whole(dw2)

    def projections(self, values, layer):
        for part, value in enumerate(values):
            low = value.astype(BF16)
            for group in range(4):
                for n in range(2):
                    at = (group // 2) * HEADS + ((layer * 3 + part) * 2 + n) * GROUP
                    self.heads[group % 2, at : at + GROUP, :] = low[
                        group * GROUP : (group + 1) * GROUP, n * 128 : (n + 1) * 128
                    ]
            self.leave(rows_from_groups(value[:, 256:]))


KEEP = {
    "n2": ((ROWS, D), F32),
    "r": ((ROWS, 2), F32),
    "gp": ((ROWS, FF), BF16),
    "n1": ((ROWS, D), F32),
    "g": ((ROWS, FF), BF16),
    "n1b": ((ROWS, D), BF16),
    "c0": ((3, 8, DP), F32),
    "v": ((ROWS, DP), BF16),
    "w": ((ROWS, HL), F32),
    "ww": ((ROWS, 2 * DP), BF16),
    "q": ((ROWS, DP), BF16),
    "k": ((ROWS, DP), BF16),
    "kf": ((ROWS, DP), BF16),
    "vf": ((ROWS, DP), BF16),
    "ob": ((ROWS, DP), BF16),
    "xb": ((ROWS, D), BF16),
}
LOADS = {
    "index": ((STARS, SLOTS), jnp.int32),
    "missing": ((STARS, SLOTS), jnp.int32),
    "drop": ((4 * STARS, SLOTS), jnp.int32),
    "w_out_in": ((2, D, D), BF16),
    "wedge_in": ((2, D, D), BF16),
    "table": ((D, NCOL), BF16),
    "dedges": ((ROWS, D), BF16),
    "own0": ((3 * GROUP, D), BF16),
    "core0": ((3 * GROUP, D), BF16),
    "near0": ((3 * GROUP, D), BF16),
    "far0": ((3 * GROUP, D), BF16),
    "nodes": ((ROWS, D), BF16),
    "w1": ((2, D, FF), BF16),
    "w2": ((2, D, FF), BF16),
    "own1": ((3 * GROUP, D), BF16),
    "core1": ((3 * GROUP, D), BF16),
    "near1": ((3 * GROUP, D), BF16),
    "far1": ((3 * GROUP, D), BF16),
    "dnodes": ((ROWS, D), BF16),
}
WORK = {
    "cols": ((ROWS, HL), F32),
    "e0": ((ROWS, DP), BF16),
    "e1": ((ROWS, DP), BF16),
    "w_out": ((2, DP, D), BF16),
    "wedge": ((DP, DP), BF16),
    "back": ((ROWS, DP), F32),
    "dw": ((EP, D), F32),
    "edges": ((ROWS, D), BF16),
    "w_qkv": ((2, QKV, D), BF16),
    "x": ((ROWS, D), F32),
    "gf1": ((ROWS, FF), BF16),
    "gf2": ((ROWS, D), BF16),
    "ga": ((ROWS, D), BF16),
    "gh1": ((ROWS, D), F32),
    "go": ((ROWS, DP), BF16),
    "gqkv": ((ROWS, QKV), BF16),
    "ge": ((ROWS, DP), BF16),
    "last": ((ROWS, D), F32),
    "common": ((2 * COMMON, 128), BF16),
    "heads": ((2, 2 * HEADS, 128), BF16),
    "left": ((STRIP, LEFT), F32),
    "stage": ((32, 128), F32),
}


def chunk_copy(rows, chunks, sem, out):
    rows = rows.reshape(*chunks.shape)
    return pltpu.make_async_copy(*((rows, chunks) if out else (chunks, rows)), sem)


class Loads:
    def __init__(self, sources, targets, sems):
        self.copies = {}
        for n, name in enumerate(LOADS):
            self.copies[name] = pltpu.make_async_copy(sources[name], targets[name], sems.at[n])
            self.copies[name].start()

    def wait(self, *names):
        for name in names:
            self.copies.pop(name).wait()


def main_kernel(star_sizes, bedge, b_out, g1, s1, b1, b2, g2, s2, *rest):
    count = len(KEEP)
    sources = dict(zip(LOADS, rest))
    rest = rest[len(LOADS) :]
    nodes_out, edges_out, grad_nodes, mine, other = rest[:5]
    keep0 = dict(zip(KEEP, rest[5:]))
    keep1 = dict(zip(KEEP, rest[5 + count :]))
    rest = rest[5 + 2 * count :]
    t = dict(zip(LOADS, rest))
    rest = rest[len(LOADS) :]
    work = dict(zip(WORK, rest))
    in_sems, out_sems = rest[len(WORK) :]
    loads = Loads(sources, t, in_sems)
    core = lax.axis_index("c")
    sent = []

    def send(which, part, first, chunks, at, rows):
        n = len(sent)
        for is_own, to in ((True, mine), (False, other)):
            place = to.at[first : first + chunks, at : at + rows, :]

            @pl.when((core == which) == is_own)
            def start():
                chunk_copy(part, place, out_sems.at[3 + n], True).start()

        sent.append((part, mine.at[first : first + chunks, at : at + rows, :]))

    def send_common(half, first, end):
        rows = common.at[half * COMMON + first * 128 : half * COMMON + end * 128, :]
        send(half, rows, first, end - first, 0, 128)

    def sent_wait():
        for n, (part, place) in enumerate(sent):
            chunk_copy(part, place, out_sems.at[3 + n], True).wait()

    t.update(work)
    w_qkv, x, gf1, gf2, ga, gh1, go, gqkv, ge, last, common, heads, left, stage = list(
        work.values()
    )[8:]
    cols, w_out, w1, w2 = t["cols"], t["w_out"], t["w1"], t["w2"]
    own = own_heads()

    def place(layer):
        names = [name + str(layer) for name in ("own", "core", "near", "far")]
        loads.wait(*names)
        for part in range(3):
            for n, name in enumerate(names):
                group = own ^ n
                at = pl.multiple_of(part * 256 + group * GROUP, 16)
                w_qkv[layer, pl.ds(at, 16), :] = t[name][part * GROUP : part * GROUP + 16, :]
                at = jnp.where(group == 3, 768 + part * 64, at + 16)
                w_qkv[layer, pl.ds(pl.multiple_of(at, 16), 64), :] = t[name][
                    part * GROUP + 16 : (part + 1) * GROUP, :
                ]
        w_qkv[layer, QKV - 64 :, :] = jnp.zeros((64, D), BF16)

    def x0(i):
        rows = chunk_rows(i)
        return t["nodes"][rows, :].astype(F32) * cols[rows, 0:1]

    def x1(i):
        return x[chunk_rows(i), :]

    def store_x(i, value):
        x[chunk_rows(i), :] = value

    def store_nodes(i, value):
        t["nodes"][chunk_rows(i), :] = value.astype(BF16)

    weights = (w_out, b_out, g1, s1, w1, b1, w2, b2, g2, s2)
    left[...] = jnp.zeros_like(left)
    loads.wait("index", "missing", "drop", "w_out_in", "wedge_in", "table")
    edges_others = edges_forward(star_sizes, t, bedge)
    loads.wait("dedges")
    place(0)
    loads.wait("nodes")
    weight = attention_forward(x0, 0, w_qkv, t["e0"], keep0, cols, edges_others)
    outs = [pltpu.make_async_copy(t["edges"], edges_out, out_sems.at[0])]
    outs[0].start()
    loads.wait("w1", "w2")
    rest_forward(x0, 0, weights, weight, keep0, cols, store_x)
    place(1)
    weight = attention_forward(x1, 1, w_qkv, t["e1"], keep1, cols)
    rest_forward(x1, 1, weights, weight, keep1, cols, store_nodes)
    outs.append(pltpu.make_async_copy(t["nodes"], nodes_out, out_sems.at[1]))
    outs[1].start()

    loads.wait("dnodes")
    packer = Packer(common, heads, left)
    sums = ff_backward(
        lambda i: t["dnodes"][chunk_rows(i), :].astype(F32),
        keep1, cols, (w1, w2, g1, g2), 1, gf1, gf2, ga, gh1,
    )
    low = t["dedges"][...].astype(F32)
    vectors = [*sums, jnp.sum(low, 0, keepdims=True)]

    def store_ge(i, value):
        total = value.astype(BF16).astype(F32) + t["back"][chunk_rows(i), :]
        ge[chunk_rows(i), :] = total.astype(BF16)

    def ff_gradients(keep, vectors):
        packer.ff(
            mm_tn(keep["n1b"][...], gf1[...]), mm_tn(gf2[...], keep["g"][...]), vectors, stage
        )

    def out_gradient(keep):
        packer.whole(rows_from_groups(mm_tn(keep["ob"][:, :EP], ga[...])))

    def projection_gradients(keep, layer):
        whole = mm_tn(gqkv[...], keep["xb"][...])
        packer.projections(
            [
                jnp.concatenate(
                    [whole[n * 256 : (n + 1) * 256], whole[768 + n * 64 : 832 + n * 64]], 0
                )
                for n in range(3)
            ],
            layer,
        )

    def edge_gradient_one():
        out_gradient(keep1)
        packer.whole(rows_from_groups(t["dw"][...]))

    attention_backward(
        ga, w_out, 1, keep1, t["e1"], w_qkv, gh1, go, gqkv, store_x, store_ge,
        (lambda: ff_gradients(keep1, vectors), edge_gradient_one),
    )

    sums = ff_backward(
        x1, keep0, cols, (w1, w2, g1, g2), 0, gf1, gf2, ga, gh1,
        lambda: projection_gradients(keep1, 1),
    )
    send_common(0, 0, 52)
    packer.at = COMMON
    db_first = jnp.sum(ge[...].astype(F32), 0, keepdims=True)

    def store_last(i, value):
        rows = chunk_rows(i)
        last[rows, :] = value * cols[rows, 0:1]

    def edge_gradient_zero():
        out_gradient(keep0)
        dwe = mm_tn(t["e0"][:, :EP], ge[:, :EP])
        packer.whole(lanes_from_groups(rows_from_groups(dwe)))
        t["back"][...] = mm_nt(ge[...], t["wedge"][...])

    attention_backward(
        ga, w_out, 0, keep0, t["e0"], w_qkv, gh1, go, gqkv, store_last, store_ge,
        (lambda: ff_gradients(keep0, [*sums, db_first[:, :EP]]), edge_gradient_zero),
    )
    outs.append(pltpu.make_async_copy(last, grad_nodes, out_sems.at[2]))
    outs[2].start()
    send_common(1, 0, 52)
    projection_gradients(keep0, 0)
    zeros = jnp.zeros((HEADS - 12 * GROUP, 128), BF16)
    for n in range(2):
        for m in range(2):
            heads[n, m * HEADS + 12 * GROUP : (m + 1) * HEADS, :] = zeros
            part = heads.at[n, m * HEADS : (m + 1) * HEADS, :]
            send(n, part, 0, 64, 128 + 16 * m, 16)
    lane = lax.broadcasted_iota(jnp.int32, (ROWS, NCOL), 1).astype(F32)
    one_hot = (cols[:, 3:4] * 256.0 + cols[:, 4:5] == lane).astype(BF16)
    dtable = rows_from_groups(mm_tn(ge[:, :EP], one_hot))
    packer.at = MAIN_ROWS
    packer.whole(dtable[:, :256])
    for n in range(2):
        packer.strip(left[:, n * 128 : (n + 1) * 128])
    final = left[:, 512:].astype(BF16)
    common[packer.at : COMMON, :] = final[:LAST_CUT]
    packer.at = COMMON + MAIN_ROWS
    packer.whole(dtable[:, 256:])
    for n in range(2, 4):
        packer.strip(left[:, n * 128 : (n + 1) * 128])
    common[packer.at : packer.at + STRIP - LAST_CUT, :] = final[LAST_CUT:]
    packer.at += STRIP - LAST_CUT
    common[packer.at :, :] = jnp.zeros((2 * COMMON - packer.at, 128), BF16)
    send_common(0, 52, 64)
    send_common(1, 52, 64)
    for copy in outs:
        copy.wait()
    sent_wait()


BIG = ("table", "wq", "wk", "wv", "wo", "w1", "w2", "we")
SMALL = {"b1": FF, "b2": D, "g2": D, "s2": D, "g1": D, "s1": D, "bo": D, "be": D}
LEFT_ROWS = 2 * STRIP + LAST_CUT


class Stores:
    def __init__(self, sems):
        self.sems, self.copies = sems, []

    def start(self, value, to):
        copy = pltpu.make_async_copy(value, to, self.sems.at[len(self.copies)])
        copy.start()
        self.copies.append(copy)

    def wait(self):
        for copy in self.copies:
            copy.wait()


class Parts:
    def __init__(self, source, common, sems):
        self.copies = [
            chunk_copy(
                common.at[n * 2048 : (n + 1) * 2048, :],
                source.at[n * 16 : (n + 1) * 16, 0:128, :],
                sems.at[n],
                False,
            )
            for n in range(4)
        ]

    def start(self):
        for copy in self.copies:
            copy.start()

    def until(self, row, done):
        while done < 4 and done * 2048 < row:
            self.copies[done].wait()
            done += 1
        return done


def unpack_half(
    half, parts, common, out, vectors, ff_stage, square_stage, table_stage, stores
):
    layer = 1 - half
    done = 0

    def strip(n):
        nonlocal done
        done = parts.until((n + 1) * STRIP, done)
        return common[n * STRIP : (n + 1) * STRIP, :].astype(F32)

    for m in range(9):
        both = strip(m)
        ff_stage[0, :, m * 128 : (m + 1) * 128] = both[:D]
        if m < 8:
            vectors[m * SPARE : (m + 1) * SPARE, :] = both[D:]
    stores.start(ff_stage.at[0], out["w1"].at[:, layer, 0:1152])
    for m in range(9):
        ff_stage[1, :, m * 128 : (m + 1) * 128] = strip(9 + m)[:D]
    stores.start(ff_stage.at[1], out["w2"].at[:, layer, 0:1152])
    for n, name in enumerate(("wo", "we")):
        for m in range(2):
            square_stage[n, :, m * 128 : (m + 1) * 128] = strip(18 + 2 * n + m)[:D]
        stores.start(square_stage.at[n], out[name].at[:, layer, 0:256])
    for n in range(2):
        table_stage[:, n * 128 : (n + 1) * 128] = strip(22 + n)[:D]
    stores.start(
        table_stage, out["table"].at[:, half * 256 : (half + 1) * 256]
    )
    parts.until(COMMON, done)


def left_parts(half):
    last = ((4, 0, LAST_CUT), (4, LAST_CUT, STRIP - LAST_CUT))[half]
    return ((2 * half, 0, STRIP), (2 * half + 1, 0, STRIP), last)


def left_first():
    return 24 * STRIP


def left_items():
    at, items = 0, []
    for layer in (1, 0):
        for name in ("w1", "w2", "wo", "we", "wq", "wk", "wv"):
            width = 48 if name in ("w1", "w2") else 44
            items.append((layer, name, at, width))
            at += width
    return items


def alone(half):
    return [
        item
        for item in left_items()
        if item[2] >= half * 256 and item[2] + item[3] <= (half + 1) * 256
    ]


def store_left(items, left, out, ff_rest, square_rest, head_rest, stores):
    row = lax.broadcasted_iota(jnp.int32, (75, STRIP), 0)
    lane = lax.broadcasted_iota(jnp.int32, (75, STRIP), 1)
    picked = mm((lane == row + own_heads() * 75).astype(BF16), left[...].astype(BF16))
    for layer, name, at, width in items:
        if name in ("w1", "w2"):
            n = 2 * layer + ("w1", "w2").index(name)
            ff_rest[n] = left[:D, at : at + width]
            stores.start(ff_rest.at[n], out[name].at[:, layer, 1152:1200])
        elif name in ("wo", "we"):
            n = 2 * layer + ("wo", "we").index(name)
            square_rest[n] = left[:D, at : at + width]
            stores.start(square_rest.at[n], out[name].at[:, layer, 256:300])
        else:
            n = 3 * layer + ("wq", "wk", "wv").index(name)
            head_rest[n] = picked[:, at : at + width]
            stores.start(head_rest.at[n], out[name].at[:, layer, 256:300])


def unpack_own(source, *rest):
    out = dict(zip(BIG, rest))
    (vectors, left_out, common, ff_stage, square_stage, table_stage, left, *rests, heads,
     head_stage, sems, in_sems) = rest[len(BIG) :]
    stages = (ff_stage, square_stage, table_stage)
    parts = Parts(source, common, in_sems)
    parts.start()
    copy = chunk_copy(heads, source.at[:, 128:144, :], in_sems.at[4], False)
    copy.start()
    copy.wait()
    stores = Stores(sems)
    for layer in range(2):
        for part, name in enumerate(("wq", "wk", "wv")):
            n = layer * 3 + part
            for m in range(2):
                at = (2 * n + m) * GROUP
                head_stage[n, :, m * 128 : (m + 1) * 128] = heads[at : at + GROUP, :].astype(F32)[
                    :75
                ]
            stores.start(head_stage.at[n], out[name].at[:, layer, 0:256])
    core = lax.axis_index("c")
    for half in range(2):
        @pl.when(core == half)
        def unpack():
            mine = Stores(sems.at[pl.ds(6, 11)])
            unpack_half(half, parts, common, out, vectors, *stages, mine)
            at, to = left_first(), 0
            for _, _, rows in left_parts(half):
                left_out[to : to + rows, :] = common[at : at + rows, :]
                at += rows
                to += rows
            left[...] = jnp.zeros_like(left)
            for n in range(2):
                at = left_first() + n * STRIP
                strip = 2 * half + n
                left[:, strip * 128 : (strip + 1) * 128] = common[at : at + STRIP, :].astype(F32)
            store_left(alone(half), left, out, *rests, mine)
            mine.wait()
    stores.wait()


def unpack_other(source, own_vectors, own_left, *rest):
    rest = rest[len(BIG) :]
    out = dict(zip(BIG, rest))
    small = dict(zip(SMALL, rest[len(BIG) :]))
    common, ff_stage, square_stage, table_stage, left, *rests, vectors, sems, in_sems = rest[
        len(BIG) + len(SMALL) :
    ]
    stages = (ff_stage, square_stage, table_stage)
    parts = Parts(source, common, in_sems)
    parts.start()
    core = lax.axis_index("c")
    for half in range(2):
        @pl.when(core != half)
        def unpack():
            theirs = Stores(sems)
            unpack_half(half, parts, common, out, vectors, *stages, theirs)
            for which, rows_of, at in (
                (half, common, left_first()), (1 - half, own_left, 0),
            ):
                for n, row, rows in left_parts(which):
                    left[row : row + rows, n * 128 : (n + 1) * 128] = rows_of[
                        at : at + rows, :
                    ].astype(F32)
                    at += rows
            done = alone(1 - half)
            items = [item for item in left_items() if item not in done]
            store_left(items, left, out, *rests, theirs)
            for layer, block in ((1 - half, vectors), (half, own_vectors)):
                row = 0
                for name in list(SMALL)[:-1]:
                    width = SMALL[name]
                    for lane in range(0, width, 128):
                        size = min(128, width - lane)
                        small[name][layer : layer + 1, lane : lane + size] = block[
                            row : row + 1, :size
                        ]
                        row += 1
                bias = jnp.concatenate([block[row + n : row + n + 1, :] for n in range(3)], 1)
                small["be"][layer : layer + 1, :] = (
                    lanes_from_groups(bias) if layer == 0 else bias[:, :D]
                )
            theirs.wait()


def shape(dims, kind):
    return jax.ShapeDtypeStruct(dims, kind)


SMEM = pl.BlockSpec(memory_space=pltpu.SMEM)
VMEM = pl.BlockSpec(memory_space=pltpu.VMEM)
ANY = pl.BlockSpec(memory_space=pl.ANY)


def params(mib):
    return pltpu.CompilerParams(vmem_limit_bytes=mib * MIB)


def cost(flops, moved):
    return pl.CostEstimate(flops=int(flops), bytes_accessed=int(moved), transcendentals=0)


RING_UP = [(n, (n + 1) % 4) for n in range(4)]
RING_DOWN = [(n, (n + 3) % 4) for n in range(4)]
SWAP = [(0, 1), (1, 0)]
CHIPS = ("x", "z", "yh", "yl")
ALONG_Y = ("yh", "yl")


def add_cores(mine, other):
    return (mine.astype(F32) + lax.ppermute(other, "c", SWAP).astype(F32)).astype(BF16)


def scatter_chips(half):
    parts = lax.all_to_all(half, CHIPS, 0, 0, tiled=True)
    return jnp.sum(parts.astype(F32), 0).astype(BF16)


def gather_chips(total):
    shares = [jnp.concatenate([total[:128], total[at : at + 16]], 0) for at in (128, 144)]
    spread = jnp.broadcast_to(jnp.stack(shares)[None], (32, 2, 144, 128))
    return lax.all_to_all(spread.reshape(64, 144, 128), CHIPS, 0, 0, tiled=True)


def body(
    nodes, edge_table, edge_index, star_sizes, leaf_drop, missing, w_query, w_key, w_value, w_out,
    b_out, ln1_gain, ln1_bias, w_ff1, b_ff1, w_ff2, b_ff2, ln2_gain, ln2_bias, w_edge, b_edge,
    d_nodes_out, d_edges_out,
):
    def to_rows(value):
        return jnp.transpose(value, (1, 0, 2)).reshape(ROWS, D)

    def to_stars(value):
        return jnp.transpose(value.reshape(SLOTS, STARS, D), (1, 0, 2))

    w_ff2 = jnp.transpose(w_ff2, (0, 2, 1))
    own = pl.pallas_call(
        pack_kernel,
        out_shape=[shape((3 * GROUP, D), BF16)] * 2,
        in_specs=[VMEM] * 3,
        out_specs=[VMEM] * 2,
        cost_estimate=cost(1e6, 1e6),
        name="pack",
    )(*[jnp.transpose(w, (2, 0, 1)) for w in (w_query, w_key, w_value)])
    near = [
        lax.ppermute(w, ALONG_Y, ring) for w, ring in zip(own, (RING_UP, RING_DOWN))
    ]
    plain = Layout(major_to_minor=(0, 1, 2))
    moved = [with_layout_constraint(w, plain) for w in (w_ff1, w_ff2)]
    *near, w_ff1, w_ff2 = lax.optimization_barrier((*near, *moved))
    core = [lax.ppermute(w, "c", SWAP) for w in own]
    far = [lax.ppermute(w, "c", SWAP) for w in near]

    def scratch(specs):
        return [pltpu.VMEM(*spec) for spec in specs.values()]

    loaded = dict(
        own0=own[0], core0=core[0], near0=near[0], far0=far[0],
        own1=own[1], core1=core[1], near1=near[1], far1=far[1],
        nodes=to_rows(nodes), w1=w_ff1, w2=w_ff2, dnodes=to_rows(d_nodes_out),
        dedges=to_rows(d_edges_out), table=edge_table.T, w_out_in=w_out, wedge_in=w_edge,
        index=edge_index, missing=missing, drop=leaf_drop,
    )
    nodes_out, edges_out, grad_nodes, mine, other = pl.pallas_call(
        main_kernel,
        out_shape=[
            shape((ROWS, D), BF16), shape((ROWS, D), BF16), shape((ROWS, D), F32),
            shape((64, 160, 128), BF16), shape((64, 160, 128), BF16),
        ],
        in_specs=[SMEM] + [VMEM] * 8 + [ANY] * len(LOADS),
        out_specs=[ANY] * 5,
        scratch_shapes=[
            *scratch(KEEP), *scratch(KEEP), *scratch(LOADS), *scratch(WORK),
            pltpu.SemaphoreType.DMA((len(LOADS),)), pltpu.SemaphoreType.DMA((12,)),
        ],
        compiler_params=params(62),
        cost_estimate=cost(1.2e10, 3e7),
        name="layers",
    )(star_sizes, b_edge, b_out, ln1_gain, ln1_bias, b_ff1, b_ff2, ln2_gain, ln2_bias,
      *[loaded[name] for name in LOADS])

    mine = gather_chips(scatter_chips(add_cores(mine, other)))
    other = lax.ppermute(mine, "c", SWAP)

    def head():
        return shape((75, 2, D), F32)

    square = shape((D, 2, D), F32)
    wide = shape((D, 2, FF), F32)
    big = [shape((D, NCOL), F32), head(), head(), head(), square, wide, wide, square]
    stages = [
        pltpu.VMEM((COMMON, 128), BF16), pltpu.VMEM((2, D, 1152), F32),
        pltpu.VMEM((2, D, 256), F32), pltpu.VMEM((D, 256), F32),
        pltpu.VMEM((STRIP, LEFT), F32), pltpu.VMEM((4, D, 48), F32), pltpu.VMEM((4, D, 44), F32),
        pltpu.VMEM((6, 75, 44), F32),
    ]
    outs = pl.pallas_call(
        unpack_own,
        out_shape=[*big, shape((32, 128), F32), shape((LEFT_ROWS, 128), BF16)],
        in_specs=[ANY],
        out_specs=[ANY] * len(BIG) + [VMEM] * 2,
        scratch_shapes=[
            *stages, pltpu.VMEM((HEADS, 128), BF16), pltpu.VMEM((6, 75, 256), F32),
            pltpu.SemaphoreType.DMA((17,)), pltpu.SemaphoreType.DMA((5,)),
        ],
        compiler_params=params(30),
        cost_estimate=cost(1e8, 1e7),
        name="unpack_own",
    )(mine)
    outs = pl.pallas_call(
        unpack_other,
        out_shape=[*big, *[shape((2, n), F32) for n in SMALL.values()]],
        in_specs=[ANY, VMEM, VMEM] + [ANY] * len(BIG),
        out_specs=[ANY] * len(BIG) + [VMEM] * len(SMALL),
        scratch_shapes=[
            *stages, pltpu.VMEM((32, 128), F32), pltpu.SemaphoreType.DMA((19,)), pltpu.SemaphoreType.DMA((4,)),
        ],
        input_output_aliases={n + 3: n for n in range(len(BIG))},
        compiler_params=params(30),
        cost_estimate=cost(1e8, 1e7),
        name="unpack_other",
    )(other, outs[-2], outs[-1], *outs[:-2])
    table, wq, wk, wv, wo, w1, w2, we, b1, b2, g2, s2, g1, s1, bo, be = outs
    wq, wk, wv = (jnp.transpose(t, (1, 2, 0)) for t in (wq, wk, wv))
    wo, w1, we = (jnp.transpose(t, (1, 0, 2)) for t in (wo, w1, we))
    w2 = jnp.transpose(w2, (1, 2, 0))
    return (
        to_stars(nodes_out), to_stars(edges_out), to_stars(grad_nodes), table.T,
        wq, wk, wv, wo, bo, g1, s1, w1, b1, w2, b2, g2, s2, we, be,
    )


def solution(mesh):
    devices = mesh.devices.reshape(4, 4, 2, 2, 2)
    fine = Mesh(devices, ("x", "z", "yh", "yl", "c"))
    graphs = ("x", "z", "yh")
    heads = ("yl", "c")
    everyone = graphs + heads
    rows3 = P(everyone, None, None)
    rows2 = P(everyone, None)
    per_head = P(None, None, heads)
    return jax.shard_map(
        body,
        mesh=fine,
        in_specs=(
            rows3, P(), rows2, P(graphs), P(graphs, None), rows2, per_head, per_head, per_head,
            *[P()] * 12, rows3, rows3,
        ),
        out_specs=(rows3, rows3, rows3, P(), per_head, per_head, per_head, *[P()] * 12),
        check_vma=False,
    )
```

```python
import math

import jax
import jax.numpy as jnp
from jax import lax
from jax.experimental import pallas as pl
from jax.experimental.layout import Layout, with_layout_constraint
from jax.experimental.pallas import tpu as pltpu
from jax.sharding import Mesh, PartitionSpec as P

D = 300
DP = 384
FF = 1200
HD = 25
SLOTS = 100
STARS = 8
ROWS = STARS * SLOTS
HL = 128
NCOL = 512
SCALE = 1.0 / math.sqrt(HD)
CHUNK = 800
CHUNKS = ROWS // CHUNK
STRIP = 304
GROUP = 80
EP = 4 * GROUP
QKV = 1024
SPARE = STRIP - D
COMMON = 8192
HEADS = 1024
LEFT = 640
MAIN_ROWS = 22 * STRIP
LAST_CUT = COMMON - 26 * STRIP
F32 = jnp.float32
BF16 = jnp.bfloat16
MIB = 1 << 20


def mm(left, right):
    return lax.dot_general(left, right, (((1,), (0,)), ((), ())), preferred_element_type=F32)


def mm_nt(left, right):
    return lax.dot_general(left, right, (((1,), (1,)), ((), ())), preferred_element_type=F32)


def mm_tn(left, right):
    return lax.dot_general(left, right, (((0,), (0,)), ((), ())), preferred_element_type=F32)


def chunk_rows(index):
    return slice(index * CHUNK, (index + 1) * CHUNK)


def by_slot(value):
    return value.reshape(value.shape[0] // 8, 8, value.shape[1])


def flat(value):
    return value.reshape(value.shape[0] * 8, value.shape[2])


def spread_heads():
    row = lax.broadcasted_iota(jnp.int32, (HL, 2 * DP), 0)
    lane = lax.broadcasted_iota(jnp.int32, (HL, 2 * DP), 1)
    second = lane >= DP
    lane = jnp.where(second, lane - DP, lane)
    head = jnp.where(second, row - 16, row)
    steps = sum((head >= n).astype(jnp.int32) for n in (3, 6, 9))
    offset = lane - head * HD - steps * (GROUP - 3 * HD)
    real = (head >= 0) & (head < 12)
    return ((offset >= 0) & (offset < HD) & real).astype(BF16)


def rows_to_groups(value):
    gap = jnp.zeros((GROUP - 75, value.shape[1]), F32)
    parts = [part for n in range(4) for part in (value[n * 75 : (n + 1) * 75], gap)]
    return jnp.concatenate([*parts, jnp.zeros((DP - EP, value.shape[1]), F32)], 0)


def lanes_to_groups(value):
    gap = jnp.zeros((value.shape[0], GROUP - 75), F32)
    parts = [part for n in range(4) for part in (value[:, n * 75 : (n + 1) * 75], gap)]
    return jnp.concatenate([*parts, jnp.zeros((value.shape[0], DP - EP), F32)], 1)


def lanes_from_groups(value):
    return jnp.concatenate([value[:, n * GROUP : n * GROUP + 75] for n in range(4)], 1)


def gelu_parts(x):
    share = 0.5 + 0.5 * lax.erf(x * 0.7071067811865476)
    bell = jnp.exp2((x * -0.7213475204444817) * x)
    return x * share, share + (x * 0.3989422804014327) * bell


def normalize(hidden):
    center = hidden - jnp.sum(hidden, -1, keepdims=True) * (1.0 / D)
    spread = jnp.sum(center * center, -1, keepdims=True) * (1.0 / D)
    root = lax.rsqrt(spread + 1e-05)
    return center * root, root


def norm_back(grad, gain, normed, root):
    scaled = grad * gain
    first = jnp.sum(scaled, -1, keepdims=True) * (1.0 / D)
    second = jnp.sum(scaled * normed, -1, keepdims=True) * (1.0 / D)
    return root * (scaled - first - normed * second)


def own_heads():
    return lax.axis_index("yl") * 2 + lax.axis_index("c")


def pack_kernel(wq, wk, wv, first, second, both):
    for layer, out in enumerate((first, second)):
        for n, w in enumerate((wq, wk, wv)):
            rows = jnp.concatenate([w[:, layer, :].astype(F32), jnp.zeros((GROUP - 75, D), F32)], 0)
            at = (3 * layer + n) * GROUP
            out[n * GROUP : (n + 1) * GROUP, :] = rows.astype(BF16)
            both[at : at + GROUP, :] = rows.astype(BF16)


def edges_forward(sizes, t, bedge):
    index, missing, drop, table, wedge = (
        t[name] for name in ("index", "missing", "drop", "table", "wedge_in")
    )
    cols_out, e0_out, e1_out, w_out_out, wedge_out, back_out, dw_out = (
        t[name] for name in ("cols", "e0", "e1", "w_out", "wedge", "back", "dw")
    )
    for layer in range(2):
        w_out_out[layer] = rows_to_groups(t["w_out_in"][layer].astype(F32)).astype(BF16)
    wedge_out[...] = lanes_to_groups(rows_to_groups(wedge[0].astype(F32))).astype(BF16)
    wedge_last = rows_to_groups(wedge[1].astype(F32)).astype(BF16)
    grouped = rows_to_groups(table[...].astype(F32)).astype(BF16)
    bias = lanes_to_groups(bedge[0:1])
    slot = lax.broadcasted_iota(jnp.int32, (STARS, SLOTS), 1)
    star = lax.broadcasted_iota(jnp.int32, (STARS, SLOTS), 0)
    first = own_heads() * STARS
    size = jnp.zeros((STARS, SLOTS), jnp.int32)
    for n in range(STARS):
        size = jnp.where(star == n, sizes[first + n], size)
    dropped = drop[pl.ds(pl.multiple_of(first, 8), STARS), :]
    present = (slot == 0) | (missing[...] == 0)
    valid = slot < size
    key_ok = valid & ((slot == 0) | (dropped == 0))
    number = index[...]
    flags = jnp.concatenate(
        [t.astype(F32) for t in (present, valid, key_ok, number >> 8, number & 255)], 0
    ).astype(BF16)
    row = lax.broadcasted_iota(jnp.int32, (ROWS, SLOTS), 0)
    lane = lax.broadcasted_iota(jnp.int32, (ROWS, SLOTS), 1)
    all_stars = mm_nt(((row >> 3) == lane).astype(BF16), flags)
    row = lax.broadcasted_iota(jnp.int32, (ROWS, 5 * STARS), 0)
    lane = lax.broadcasted_iota(jnp.int32, (ROWS, 5 * STARS), 1)
    own = jnp.where((row & 7) == (lane & 7), all_stars, 0.0).astype(BF16)
    row = lax.broadcasted_iota(jnp.int32, (5 * STARS, HL), 0)
    lane = lax.broadcasted_iota(jnp.int32, (5 * STARS, HL), 1)
    cols = mm(own, ((row >> 3) == lane).astype(BF16))
    cols_out[...] = cols
    picked = cols[:, 3:4] * 256.0 + cols[:, 4:5]
    lane = lax.broadcasted_iota(jnp.int32, (CHUNK, NCOL), 1).astype(F32)
    for i in range(CHUNKS):
        rows = chunk_rows(i)
        one_hot = (picked[rows] == lane).astype(BF16)
        e0 = mm_nt(one_hot, grouped).astype(BF16)
        e1 = (mm(e0, wedge_out[...]) + bias).astype(BF16)
        e0_out[rows, :] = e0
        e1_out[rows, :] = e1

    def others():
        t["edges"][...] = (mm(e1_out[...], wedge_last) + bedge[1:2]).astype(BF16)
        low = t["dedges"][...]
        back_out[...] = mm_nt(low, wedge_last)
        dw_out[...] = mm_tn(e1_out[:, :EP], low)

    return others


def attention_forward(x_in, layer, w_qkv, e, keep, cols, beside=None):
    spread = spread_heads()
    scores = []
    center = None
    for i in range(CHUNKS):
        rows = chunk_rows(i)
        low = x_in(i).astype(BF16)
        keep["xb"][rows, :] = low
        projected = mm_nt(low, w_qkv[layer])
        edge = e[rows, :].astype(F32)
        last = projected[:, 768:896]
        query = jnp.concatenate([projected[:, :256], last], 1)
        key_full = jnp.concatenate([projected[:, 256:512], pltpu.roll(last, 64, 1)], 1)
        value_full = jnp.concatenate([projected[:, 512:768], projected[:, 896:]], 1)
        key = key_full * edge
        value = value_full * edge
        keep["kf"][rows, :] = key_full.astype(BF16)
        keep["vf"][rows, :] = value_full.astype(BF16)
        keep["q"][rows, :] = query.astype(BF16)
        keep["k"][rows, :] = key.astype(BF16)
        keep["v"][rows, :] = value.astype(BF16)
        if i == 0:
            center = (query[:8], key[:8])
            keep["c0"][0] = query[:8]
            keep["c0"][1] = key[:8]
            keep["c0"][2] = value[:8]
        keys = by_slot(key)
        of_center = flat(keys * center[0][None])
        of_gap = flat((center[1][None] - keys) * by_slot(query))
        products = jnp.concatenate([of_center.astype(BF16), of_gap.astype(BF16)], 1)
        scores.append(mm_nt(products, spread))
    if beside is not None:
        beside()
    score = jnp.concatenate(scores, 0) * SCALE
    lane = lax.broadcasted_iota(jnp.int32, (ROWS, HL), 1)
    row = lax.broadcasted_iota(jnp.int32, (ROWS, HL), 0)
    is_gap = lane >= 16
    open_ = cols[:, 2:3] > 0.0
    masked = by_slot(jnp.where(open_, score, -1e30))
    lowered = flat(masked - jnp.max(masked, 0, keepdims=True))
    expo = jnp.exp(jnp.where(is_gap, -jnp.abs(score), lowered))
    expo = jnp.where(is_gap | open_, expo, 0.0)
    total = by_slot(expo)
    probs = flat(total / jnp.sum(total, 0, keepdims=True))
    large = 1.0 / (1.0 + expo)
    toward = jnp.where(row < 8, 0.0, jnp.where(score >= 0.0, large, expo * large))
    weight = jnp.where(is_gap, toward, probs)
    keep["w"][...] = weight
    return weight.astype(BF16)


def rest_forward(x_in, layer, weights, weight, keep, cols, x_out):
    w_out, b_out, g1, s1, w1, b1, w2, b2, g2, s2 = weights
    spread = spread_heads()
    value_center = keep["c0"][2][None]
    outs = []
    total = None
    for i in range(CHUNKS):
        rows = chunk_rows(i)
        wide = mm(weight[rows], spread)
        keep["ww"][rows, :] = wide.astype(BF16)
        values = by_slot(keep["v"][rows, :].astype(F32))
        part = jnp.sum(by_slot(wide[:, :DP]) * values, 0)
        total = part if total is None else total + part
        out = flat(values + by_slot(wide[:, DP:]) * (value_center - values))
        keep["ob"][rows, :] = out.astype(BF16)
    out = keep["ob"][:16, :].astype(F32)
    keep["ob"][:16, :] = jnp.concatenate([total, out[8:]], 0).astype(BF16)
    for i in range(CHUNKS):
        rows = chunk_rows(i)
        hidden = x_in(i) + mm(keep["ob"][rows, :], w_out[layer]) + b_out[layer : layer + 1]
        normed, root = normalize(hidden)
        keep["n1"][rows, :] = normed
        keep["r"][rows, 0:1] = root
        first = normed * g1[layer : layer + 1] + s1[layer : layer + 1]
        first_low = first.astype(BF16)
        keep["n1b"][rows, :] = first_low
        act, slope = gelu_parts(mm(first_low, w1[layer]) + b1[layer : layer + 1])
        act_low = act.astype(BF16)
        keep["g"][rows, :] = act_low
        keep["gp"][rows, :] = slope.astype(BF16)
        second, root = normalize(first + mm_nt(act_low, w2[layer]) + b2[layer : layer + 1])
        keep["n2"][rows, :] = second
        keep["r"][rows, 1:2] = root
        result = second * g2[layer : layer + 1] + s2[layer : layer + 1]
        x_out(i, result * cols[rows, 1:2])


def ff_backward(grad_x, keep, cols, weights, layer, gf1, gf2, ga, gh1, beside=None):
    w1, w2, g1, g2 = weights
    sums = None
    for i in range(CHUNKS):
        rows = chunk_rows(i)
        grad = grad_x(i) * cols[rows, 1:2]
        normed = keep["n2"][rows, :]
        back = norm_back(grad, g2[layer : layer + 1], normed, keep["r"][rows, 1:2])
        if i == 0 and beside is not None:
            beside()
        low = back.astype(BF16)
        gf2[rows, :] = low
        slope = keep["gp"][rows, :].astype(F32) * mm(low, w2[layer])
        slope_low = slope.astype(BF16)
        gf1[rows, :] = slope_low
        back_one = back + mm_nt(slope_low, w1[layer])
        normed_one = keep["n1"][rows, :]
        hidden = norm_back(back_one, g1[layer : layer + 1], normed_one, keep["r"][rows, 0:1])
        gh1[rows, :] = hidden
        ga[rows, :] = hidden.astype(BF16)
        part = (
            jnp.sum(slope, 0, keepdims=True),
            jnp.sum(back, 0, keepdims=True),
            jnp.sum(grad * normed, 0, keepdims=True),
            jnp.sum(grad, 0, keepdims=True),
            jnp.sum(back_one * normed_one, 0, keepdims=True),
            jnp.sum(back_one, 0, keepdims=True),
            jnp.sum(hidden, 0, keepdims=True),
        )
        sums = part if sums is None else tuple(a + b for a, b in zip(sums, part))
    return sums


def attention_backward(ga, w_out, layer, keep, e, w_qkv, gh1, go, gqkv, x_out, e_out, beside):
    spread = spread_heads()
    query_center, key_center, value_center = (keep["c0"][n][None] for n in range(3))
    dots = []
    grad_center = None
    for i in range(CHUNKS):
        rows = chunk_rows(i)
        grad = mm_nt(ga[rows, :], w_out[layer])
        if i == 0:
            grad_center = grad[:8].astype(BF16).astype(F32)[None]
            grad = jnp.concatenate([jnp.zeros((8, DP), F32), grad[8:]], 0)
        go[rows, :] = grad.astype(BF16)
        values = by_slot(keep["v"][rows, :].astype(F32))
        of_center = flat(grad_center * values)
        of_gap = flat(by_slot(grad) * (value_center - values))
        products = jnp.concatenate([of_center.astype(BF16), of_gap.astype(BF16)], 1)
        dots.append(mm_nt(products, spread))
    beside[0]()
    dot = jnp.concatenate(dots, 0)
    weight = keep["w"][...]
    lane = lax.broadcasted_iota(jnp.int32, (ROWS, HL), 1)
    mean = jnp.sum(by_slot(weight * dot), 0, keepdims=True)
    of_probs = flat(by_slot(dot) - mean)
    grads = weight * jnp.where(lane >= 16, (1.0 - weight) * dot, of_probs) * SCALE
    grads = grads.astype(BF16)
    beside[1]()
    sums = None
    for i in reversed(range(CHUNKS)):
        rows = chunk_rows(i)
        wide = mm(grads[rows], spread)
        of_score = by_slot(wide[:, :DP])
        of_gap = by_slot(wide[:, DP:])
        query = by_slot(keep["q"][rows, :].astype(F32))
        key = by_slot(keep["k"][rows, :].astype(F32))
        grad = by_slot(go[rows, :].astype(F32))
        weights = keep["ww"][rows, :].astype(F32)
        probs = by_slot(weights[:, :DP])
        toward = by_slot(weights[:, DP:])
        edge = e[rows, :].astype(F32)
        pulled = of_gap * query
        moved = toward * grad
        part = (jnp.sum(of_score * key, 0), jnp.sum(pulled, 0), jnp.sum(moved, 0))
        sums = part if sums is None else tuple(a + b for a, b in zip(sums, part))
        of_q = of_gap * (key_center - key)
        of_k = of_score * query_center - pulled
        of_v = probs * grad_center + grad - moved
        if i == 0:
            of_q, of_k, of_v = (
                jnp.concatenate([t[:1] + s[None], t[1:]], 0)
                for t, s in zip((of_q, of_k, of_v), sums)
            )
        of_k, of_v = flat(of_k), flat(of_v)
        to_q, to_k, to_v = flat(of_q), of_k * edge, of_v * edge
        for n, value in enumerate((to_q, to_k, to_v)):
            gqkv[rows, n * 256 : (n + 1) * 256] = value[:, :256].astype(BF16)
        last = to_q[:, 256:] + pltpu.roll(to_k[:, 256:], 64, 1)
        gqkv[rows, 768:896] = last.astype(BF16)
        gqkv[rows, 896:] = to_v[:, 256:].astype(BF16)
        of_edge = of_k * keep["kf"][rows, :].astype(F32) + of_v * keep["vf"][rows, :].astype(F32)
        e_out(i, of_edge)
        x_out(i, gh1[rows, :] + mm(gqkv[rows, :], w_qkv[layer]))


def rows_from_groups(value):
    return jnp.concatenate([value[n * GROUP : n * GROUP + 75] for n in range(4)], 0)


class Packer:
    def __init__(self, common, heads, left):
        self.common, self.heads, self.left = common, heads, left
        self.at = self.lane = 0

    def strip(self, value, spare=None):
        if value.shape[0] < STRIP:
            spare = jnp.zeros((SPARE, 128), F32) if spare is None else spare
            value = jnp.concatenate([value, spare], 0)
        self.common[self.at : self.at + STRIP, :] = value.astype(BF16)
        self.at += STRIP

    def whole(self, value, spares=()):
        lanes = value.shape[1] // 128 * 128
        for lane in range(0, lanes, 128):
            n = lane // 128
            self.strip(value[:, lane : lane + 128], spares[n] if n < len(spares) else None)
        self.leave(value[:, lanes:])

    def leave(self, value):
        width = value.shape[1]
        if width:
            self.left[:D, self.lane : self.lane + width] = value
            self.lane += width

    def ff(self, dw1, dw2, vectors, stage):
        stage[...] = jnp.zeros_like(stage)
        row = 0
        for vector in vectors:
            for lane in range(0, vector.shape[1], 128):
                part = vector[:, lane : lane + 128]
                stage[row : row + 1, : part.shape[1]] = part
                row += 1
        self.whole(dw1, [stage[n * SPARE : (n + 1) * SPARE, :] for n in range(8)])
        self.whole(dw2)

    def projections(self, values, layer):
        for part, value in enumerate(values):
            low = value.astype(BF16)
            for group in range(4):
                for n in range(2):
                    at = (group // 2) * HEADS + ((layer * 3 + part) * 2 + n) * GROUP
                    self.heads[group % 2, at : at + GROUP, :] = low[
                        group * GROUP : (group + 1) * GROUP, n * 128 : (n + 1) * 128
                    ]
            self.leave(rows_from_groups(value[:, 256:]))


KEEP = {
    "n2": ((ROWS, D), F32),
    "r": ((ROWS, 2), F32),
    "gp": ((ROWS, FF), BF16),
    "n1": ((ROWS, D), F32),
    "g": ((ROWS, FF), BF16),
    "n1b": ((ROWS, D), BF16),
    "c0": ((3, 8, DP), F32),
    "v": ((ROWS, DP), BF16),
    "w": ((ROWS, HL), F32),
    "ww": ((ROWS, 2 * DP), BF16),
    "q": ((ROWS, DP), BF16),
    "k": ((ROWS, DP), BF16),
    "kf": ((ROWS, DP), BF16),
    "vf": ((ROWS, DP), BF16),
    "ob": ((ROWS, DP), BF16),
    "xb": ((ROWS, D), BF16),
}
LOADS = {
    "index": ((STARS, SLOTS), jnp.int32),
    "missing": ((STARS, SLOTS), jnp.int32),
    "drop": ((4 * STARS, SLOTS), jnp.int32),
    "w_out_in": ((2, D, D), BF16),
    "wedge_in": ((2, D, D), BF16),
    "table": ((D, NCOL), BF16),
    "dedges": ((ROWS, D), BF16),
    "own0": ((3 * GROUP, D), BF16),
    "core0": ((3 * GROUP, D), BF16),
    "near0": ((3 * GROUP, D), BF16),
    "far0": ((3 * GROUP, D), BF16),
    "nodes": ((ROWS, D), BF16),
    "w1": ((2, D, FF), BF16),
    "w2": ((2, D, FF), BF16),
    "own1": ((3 * GROUP, D), BF16),
    "core1": ((3 * GROUP, D), BF16),
    "near1": ((3 * GROUP, D), BF16),
    "far1": ((3 * GROUP, D), BF16),
    "dnodes": ((ROWS, D), BF16),
}
WORK = {
    "cols": ((ROWS, HL), F32),
    "e0": ((ROWS, DP), BF16),
    "e1": ((ROWS, DP), BF16),
    "w_out": ((2, DP, D), BF16),
    "wedge": ((DP, DP), BF16),
    "back": ((ROWS, DP), F32),
    "dw": ((EP, D), F32),
    "edges": ((ROWS, D), BF16),
    "w_qkv": ((2, QKV, D), BF16),
    "x": ((ROWS, D), F32),
    "gf1": ((ROWS, FF), BF16),
    "gf2": ((ROWS, D), BF16),
    "ga": ((ROWS, D), BF16),
    "gh1": ((ROWS, D), F32),
    "go": ((ROWS, DP), BF16),
    "gqkv": ((ROWS, QKV), BF16),
    "ge": ((ROWS, DP), BF16),
    "last": ((ROWS, D), F32),
    "common": ((2 * COMMON, 128), BF16),
    "heads": ((2, 2 * HEADS, 128), BF16),
    "left": ((STRIP, LEFT), F32),
    "stage": ((32, 128), F32),
}


def chunk_copy(rows, chunks, sem, out):
    rows = rows.reshape(*chunks.shape)
    return pltpu.make_async_copy(*((rows, chunks) if out else (chunks, rows)), sem)


class Loads:
    def __init__(self, sources, targets, sems):
        self.copies = {}
        for n, name in enumerate(LOADS):
            source = sources[name]
            if name in ("core0", "core1"):
                at = int(name[-1]) * 3 * GROUP
                source = source.at[at : at + 3 * GROUP, :]
            self.copies[name] = pltpu.make_async_copy(source, targets[name], sems.at[n])
            self.copies[name].start()

    def wait(self, *names):
        for name in names:
            self.copies.pop(name).wait()


def main_kernel(star_sizes, bedge, b_out, g1, s1, b1, b2, g2, s2, *rest):
    count = len(KEEP)
    sources = dict(zip(LOADS, rest))
    rest = rest[len(LOADS) :]
    nodes_out, edges_out, grad_nodes, mine, other = rest[:5]
    keep0 = dict(zip(KEEP, rest[5:]))
    keep1 = dict(zip(KEEP, rest[5 + count :]))
    rest = rest[5 + 2 * count :]
    t = dict(zip(LOADS, rest))
    rest = rest[len(LOADS) :]
    work = dict(zip(WORK, rest))
    in_sems, out_sems = rest[len(WORK) :]
    loads = Loads(sources, t, in_sems)
    core = lax.axis_index("c")
    sent = []

    def send(which, part, first, chunks, at, rows):
        n = len(sent)
        for is_own, to in ((True, mine), (False, other)):
            place = to.at[first : first + chunks, at : at + rows, :]

            @pl.when((core == which) == is_own)
            def start():
                chunk_copy(part, place, out_sems.at[3 + n], True).start()

        sent.append((part, mine.at[first : first + chunks, at : at + rows, :]))

    def send_common(half, first, end):
        rows = common.at[half * COMMON + first * 128 : half * COMMON + end * 128, :]
        send(half, rows, first, end - first, 0, 128)

    def sent_wait():
        for n, (part, place) in enumerate(sent):
            chunk_copy(part, place, out_sems.at[3 + n], True).wait()

    t.update(work)
    w_qkv, x, gf1, gf2, ga, gh1, go, gqkv, ge, last, common, heads, left, stage = list(
        work.values()
    )[8:]
    cols, w_out, w1, w2 = t["cols"], t["w_out"], t["w1"], t["w2"]
    own = own_heads()

    def place(layer):
        names = [name + str(layer) for name in ("own", "core", "near", "far")]
        loads.wait(*names)
        for part in range(3):
            for n, name in enumerate(names):
                group = own ^ n
                at = pl.multiple_of(part * 256 + group * GROUP, 16)
                w_qkv[layer, pl.ds(at, 16), :] = t[name][part * GROUP : part * GROUP + 16, :]
                at = jnp.where(group == 3, 768 + part * 64, at + 16)
                w_qkv[layer, pl.ds(pl.multiple_of(at, 16), 64), :] = t[name][
                    part * GROUP + 16 : (part + 1) * GROUP, :
                ]
        w_qkv[layer, QKV - 64 :, :] = jnp.zeros((64, D), BF16)

    def x0(i):
        rows = chunk_rows(i)
        return t["nodes"][rows, :].astype(F32) * cols[rows, 0:1]

    def x1(i):
        return x[chunk_rows(i), :]

    def store_x(i, value):
        x[chunk_rows(i), :] = value

    def store_nodes(i, value):
        t["nodes"][chunk_rows(i), :] = value.astype(BF16)

    weights = (w_out, b_out, g1, s1, w1, b1, w2, b2, g2, s2)
    left[...] = jnp.zeros_like(left)
    loads.wait("index", "missing", "drop", "w_out_in", "wedge_in", "table")
    edges_others = edges_forward(star_sizes, t, bedge)
    loads.wait("dedges")
    place(0)
    loads.wait("nodes")
    weight = attention_forward(x0, 0, w_qkv, t["e0"], keep0, cols, edges_others)
    outs = [pltpu.make_async_copy(t["edges"], edges_out, out_sems.at[0])]
    outs[0].start()
    loads.wait("w1", "w2")
    rest_forward(x0, 0, weights, weight, keep0, cols, store_x)
    place(1)
    weight = attention_forward(x1, 1, w_qkv, t["e1"], keep1, cols)
    rest_forward(x1, 1, weights, weight, keep1, cols, store_nodes)
    outs.append(pltpu.make_async_copy(t["nodes"], nodes_out, out_sems.at[1]))
    outs[1].start()

    loads.wait("dnodes")
    packer = Packer(common, heads, left)
    sums = ff_backward(
        lambda i: t["dnodes"][chunk_rows(i), :].astype(F32),
        keep1, cols, (w1, w2, g1, g2), 1, gf1, gf2, ga, gh1,
    )
    low = t["dedges"][...].astype(F32)
    vectors = [*sums, jnp.sum(low, 0, keepdims=True)]

    def store_ge(i, value):
        total = value.astype(BF16).astype(F32) + t["back"][chunk_rows(i), :]
        ge[chunk_rows(i), :] = total.astype(BF16)

    def ff_gradients(keep, vectors):
        packer.ff(
            mm_tn(keep["n1b"][...], gf1[...]), mm_tn(gf2[...], keep["g"][...]), vectors, stage
        )

    def out_gradient(keep):
        packer.whole(rows_from_groups(mm_tn(keep["ob"][:, :EP], ga[...])))

    def projection_gradients(keep, layer):
        whole = mm_tn(gqkv[...], keep["xb"][...])
        packer.projections(
            [
                jnp.concatenate(
                    [whole[n * 256 : (n + 1) * 256], whole[768 + n * 64 : 832 + n * 64]], 0
                )
                for n in range(3)
            ],
            layer,
        )

    def edge_gradient_one():
        out_gradient(keep1)
        packer.whole(rows_from_groups(t["dw"][...]))

    attention_backward(
        ga, w_out, 1, keep1, t["e1"], w_qkv, gh1, go, gqkv, store_x, store_ge,
        (lambda: ff_gradients(keep1, vectors), edge_gradient_one),
    )

    sums = ff_backward(
        x1, keep0, cols, (w1, w2, g1, g2), 0, gf1, gf2, ga, gh1,
        lambda: projection_gradients(keep1, 1),
    )
    send_common(0, 0, 52)
    packer.at = COMMON
    db_first = jnp.sum(ge[...].astype(F32), 0, keepdims=True)

    def store_last(i, value):
        rows = chunk_rows(i)
        last[rows, :] = value * cols[rows, 0:1]

    def edge_gradient_zero():
        out_gradient(keep0)
        dwe = mm_tn(t["e0"][:, :EP], ge[:, :EP])
        packer.whole(lanes_from_groups(rows_from_groups(dwe)))
        t["back"][...] = mm_nt(ge[...], t["wedge"][...])

    attention_backward(
        ga, w_out, 0, keep0, t["e0"], w_qkv, gh1, go, gqkv, store_last, store_ge,
        (lambda: ff_gradients(keep0, [*sums, db_first[:, :EP]]), edge_gradient_zero),
    )
    outs.append(pltpu.make_async_copy(last, grad_nodes, out_sems.at[2]))
    outs[2].start()
    send_common(1, 0, 52)
    lane = lax.broadcasted_iota(jnp.int32, (ROWS, NCOL), 1).astype(F32)
    one_hot = (cols[:, 3:4] * 256.0 + cols[:, 4:5] == lane).astype(BF16)
    dtable = rows_from_groups(mm_tn(ge[:, :EP], one_hot))
    for half in range(2):
        packer.at = half * COMMON + MAIN_ROWS
        packer.whole(dtable[:, half * 256 : (half + 1) * 256])
    projection_gradients(keep0, 0)
    zeros = jnp.zeros((HEADS - 12 * GROUP, 128), BF16)
    for n in range(2):
        for m in range(2):
            heads[n, m * HEADS + 12 * GROUP : (m + 1) * HEADS, :] = zeros
            part = heads.at[n, m * HEADS : (m + 1) * HEADS, :]
            send(n, part, 0, 64, 128 + 16 * m, 16)
    final = left[:, 512:].astype(BF16)
    for half, first, count in ((0, 0, LAST_CUT), (1, LAST_CUT, STRIP - LAST_CUT)):
        packer.at = half * COMMON + 24 * STRIP
        for n in range(2):
            packer.strip(left[:, half * 256 + n * 128 : half * 256 + (n + 1) * 128])
        end = packer.at + count
        common[packer.at : end, :] = final[first : first + count]
        if end < (half + 1) * COMMON:
            common[end : (half + 1) * COMMON, :] = jnp.zeros(
                ((half + 1) * COMMON - end, 128), BF16
            )
    send_common(0, 52, 64)
    send_common(1, 52, 64)
    for copy in outs:
        copy.wait()
    sent_wait()


BIG = ("table", "wq", "wk", "wv", "wo", "w1", "w2", "we")
SMALL = {"b1": FF, "b2": D, "g2": D, "s2": D, "g1": D, "s1": D, "bo": D, "be": D}
LEFT_ROWS = 2 * STRIP + LAST_CUT


class Stores:
    def __init__(self, sems):
        self.sems, self.copies = sems, []

    def start(self, value, to):
        copy = pltpu.make_async_copy(value, to, self.sems.at[len(self.copies)])
        copy.start()
        self.copies.append(copy)

    def wait(self):
        for copy in self.copies:
            copy.wait()


class Parts:
    def __init__(self, source, common, sems):
        self.copies = [
            chunk_copy(
                common.at[n * 2048 : (n + 1) * 2048, :],
                source.at[n * 16 : (n + 1) * 16, 0:128, :],
                sems.at[n],
                False,
            )
            for n in range(4)
        ]

    def start(self):
        for copy in self.copies:
            copy.start()

    def until(self, row, done):
        while done < 4 and done * 2048 < row:
            self.copies[done].wait()
            done += 1
        return done


def unpack_half(
    half, parts, common, out, vectors, ff_stage, square_stage, table_stage, stores
):
    layer = 1 - half
    done = 0

    def strip(n):
        nonlocal done
        done = parts.until((n + 1) * STRIP, done)
        return common[n * STRIP : (n + 1) * STRIP, :].astype(F32)

    for m in range(9):
        both = strip(m)
        ff_stage[0, :, m * 128 : (m + 1) * 128] = both[:D]
        if m < 8:
            vectors[m * SPARE : (m + 1) * SPARE, :] = both[D:]
    stores.start(ff_stage.at[0], out["w1"].at[:, layer, 0:1152])
    for m in range(9):
        ff_stage[1, :, m * 128 : (m + 1) * 128] = strip(9 + m)[:D]
    stores.start(ff_stage.at[1], out["w2"].at[:, layer, 0:1152])
    for n, name in enumerate(("wo", "we")):
        for m in range(2):
            square_stage[n, :, m * 128 : (m + 1) * 128] = strip(18 + 2 * n + m)[:D]
        stores.start(square_stage.at[n], out[name].at[:, layer, 0:256])
    for n in range(2):
        table_stage[:, n * 128 : (n + 1) * 128] = strip(22 + n)[:D]
    stores.start(
        table_stage, out["table"].at[:, half * 256 : (half + 1) * 256]
    )
    parts.until(COMMON, done)


def left_parts(half):
    last = ((4, 0, LAST_CUT), (4, LAST_CUT, STRIP - LAST_CUT))[half]
    return ((2 * half, 0, STRIP), (2 * half + 1, 0, STRIP), last)


def left_first():
    return 24 * STRIP


def left_items():
    at, items = 0, []
    for layer in (1, 0):
        for name in ("w1", "w2", "wo", "we", "wq", "wk", "wv"):
            width = 48 if name in ("w1", "w2") else 44
            items.append((layer, name, at, width))
            at += width
    return items


def alone(half):
    return [
        item
        for item in left_items()
        if item[2] >= half * 256 and item[2] + item[3] <= (half + 1) * 256
    ]


def store_left(items, left, out, ff_rest, square_rest, head_rest, stores):
    row = lax.broadcasted_iota(jnp.int32, (75, STRIP), 0)
    lane = lax.broadcasted_iota(jnp.int32, (75, STRIP), 1)
    picked = mm((lane == row + own_heads() * 75).astype(BF16), left[...].astype(BF16))
    for layer, name, at, width in items:
        if name in ("w1", "w2"):
            n = 2 * layer + ("w1", "w2").index(name)
            ff_rest[n] = left[:D, at : at + width]
            stores.start(ff_rest.at[n], out[name].at[:, layer, 1152:1200])
        elif name in ("wo", "we"):
            n = 2 * layer + ("wo", "we").index(name)
            square_rest[n] = left[:D, at : at + width]
            stores.start(square_rest.at[n], out[name].at[:, layer, 256:300])
        else:
            n = 3 * layer + ("wq", "wk", "wv").index(name)
            head_rest[n] = picked[:, at : at + width]
            stores.start(head_rest.at[n], out[name].at[:, layer, 256:300])


def unpack_own(source, *rest):
    out = dict(zip(BIG, rest))
    (vectors, left_out, common, ff_stage, square_stage, table_stage, left, *rests, heads,
     head_stage, sems, in_sems) = rest[len(BIG) :]
    stages = (ff_stage, square_stage, table_stage)
    parts = Parts(source, common, in_sems)
    parts.start()
    copy = chunk_copy(heads, source.at[:, 128:144, :], in_sems.at[4], False)
    copy.start()
    copy.wait()
    stores = Stores(sems)
    for layer in range(2):
        for part, name in enumerate(("wq", "wk", "wv")):
            n = layer * 3 + part
            for m in range(2):
                at = (2 * n + m) * GROUP
                head_stage[n, :, m * 128 : (m + 1) * 128] = heads[at : at + GROUP, :].astype(F32)[
                    :75
                ]
            stores.start(head_stage.at[n], out[name].at[:, layer, 0:256])
    core = lax.axis_index("c")
    for half in range(2):
        @pl.when(core == half)
        def unpack():
            mine = Stores(sems.at[pl.ds(6, 11)])
            unpack_half(half, parts, common, out, vectors, *stages, mine)
            at, to = left_first(), 0
            for _, _, rows in left_parts(half):
                left_out[to : to + rows, :] = common[at : at + rows, :]
                at += rows
                to += rows
            left[...] = jnp.zeros_like(left)
            for n in range(2):
                at = left_first() + n * STRIP
                strip = 2 * half + n
                left[:, strip * 128 : (strip + 1) * 128] = common[at : at + STRIP, :].astype(F32)
            store_left(alone(half), left, out, *rests, mine)
            mine.wait()
    stores.wait()


def unpack_other(source, own_vectors, own_left, *rest):
    rest = rest[len(BIG) :]
    out = dict(zip(BIG, rest))
    small = dict(zip(SMALL, rest[len(BIG) :]))
    common, ff_stage, square_stage, table_stage, left, *rests, vectors, sems, in_sems = rest[
        len(BIG) + len(SMALL) :
    ]
    stages = (ff_stage, square_stage, table_stage)
    parts = Parts(source, common, in_sems)
    parts.start()
    core = lax.axis_index("c")
    for half in range(2):
        @pl.when(core != half)
        def unpack():
            theirs = Stores(sems)
            unpack_half(half, parts, common, out, vectors, *stages, theirs)
            for which, rows_of, at in (
                (half, common, left_first()), (1 - half, own_left, 0),
            ):
                for n, row, rows in left_parts(which):
                    left[row : row + rows, n * 128 : (n + 1) * 128] = rows_of[
                        at : at + rows, :
                    ].astype(F32)
                    at += rows
            done = alone(1 - half)
            items = [item for item in left_items() if item not in done]
            store_left(items, left, out, *rests, theirs)
            for layer, block in ((1 - half, vectors), (half, own_vectors)):
                row = 0
                for name in list(SMALL)[:-1]:
                    width = SMALL[name]
                    for lane in range(0, width, 128):
                        size = min(128, width - lane)
                        small[name][layer : layer + 1, lane : lane + size] = block[
                            row : row + 1, :size
                        ]
                        row += 1
                bias = jnp.concatenate([block[row + n : row + n + 1, :] for n in range(3)], 1)
                small["be"][layer : layer + 1, :] = (
                    lanes_from_groups(bias) if layer == 0 else bias[:, :D]
                )
            theirs.wait()


def shape(dims, kind):
    return jax.ShapeDtypeStruct(dims, kind)


SMEM = pl.BlockSpec(memory_space=pltpu.SMEM)
VMEM = pl.BlockSpec(memory_space=pltpu.VMEM)
ANY = pl.BlockSpec(memory_space=pl.ANY)


def params(mib):
    return pltpu.CompilerParams(vmem_limit_bytes=mib * MIB)


def cost(flops, moved):
    return pl.CostEstimate(flops=int(flops), bytes_accessed=int(moved), transcendentals=0)


RING_UP = [(n, (n + 1) % 4) for n in range(4)]
RING_DOWN = [(n, (n + 3) % 4) for n in range(4)]
SWAP = [(0, 1), (1, 0)]
CHIPS = ("x", "z", "yh", "yl")
ALONG_Y = ("yh", "yl")


def add_cores(mine, other):
    return (mine.astype(F32) + lax.ppermute(other, "c", SWAP).astype(F32)).astype(BF16)


def scatter_chips(half):
    parts = lax.all_to_all(half, CHIPS, 0, 0, tiled=True)
    return jnp.sum(parts.astype(F32), 0).astype(BF16)


def gather_chips(total):
    shares = [jnp.concatenate([total[:128], total[at : at + 16]], 0) for at in (128, 144)]
    spread = jnp.broadcast_to(jnp.stack(shares)[None], (32, 2, 144, 128))
    return lax.all_to_all(spread.reshape(64, 144, 128), CHIPS, 0, 0, tiled=True)


def body(
    nodes, edge_table, edge_index, star_sizes, leaf_drop, missing, w_query, w_key, w_value, w_out,
    b_out, ln1_gain, ln1_bias, w_ff1, b_ff1, w_ff2, b_ff2, ln2_gain, ln2_bias, w_edge, b_edge,
    d_nodes_out, d_edges_out,
):
    def to_rows(value):
        return jnp.transpose(value, (1, 0, 2)).reshape(ROWS, D)

    def to_stars(value):
        return jnp.transpose(value.reshape(SLOTS, STARS, D), (1, 0, 2))

    w_ff2 = jnp.transpose(w_ff2, (0, 2, 1))
    *own, both = pl.pallas_call(
        pack_kernel,
        out_shape=[shape((3 * GROUP, D), BF16)] * 2 + [shape((6 * GROUP, D), BF16)],
        in_specs=[VMEM] * 3,
        out_specs=[VMEM] * 3,
        cost_estimate=cost(1e6, 1e6),
        name="pack",
    )(*[jnp.transpose(w, (2, 0, 1)) for w in (w_query, w_key, w_value)])
    near = [
        lax.ppermute(w, ALONG_Y, ring) for w, ring in zip(own, (RING_UP, RING_DOWN))
    ]
    plain = Layout(major_to_minor=(0, 1, 2))
    moved = [with_layout_constraint(w, plain) for w in (w_ff1, w_ff2)]
    *near, w_ff1, w_ff2 = lax.optimization_barrier((*near, *moved))
    core = lax.ppermute(both, "c", SWAP)
    far = [lax.ppermute(w, "c", SWAP) for w in near]

    def scratch(specs):
        return [pltpu.VMEM(*spec) for spec in specs.values()]

    loaded = dict(
        own0=own[0], core0=core, near0=near[0], far0=far[0],
        own1=own[1], core1=core, near1=near[1], far1=far[1],
        nodes=to_rows(nodes), w1=w_ff1, w2=w_ff2, dnodes=to_rows(d_nodes_out),
        dedges=to_rows(d_edges_out), table=edge_table.T, w_out_in=w_out, wedge_in=w_edge,
        index=edge_index, missing=missing, drop=leaf_drop,
    )
    nodes_out, edges_out, grad_nodes, mine, other = pl.pallas_call(
        main_kernel,
        out_shape=[
            shape((ROWS, D), BF16), shape((ROWS, D), BF16), shape((ROWS, D), F32),
            shape((64, 160, 128), BF16), shape((64, 160, 128), BF16),
        ],
        in_specs=[SMEM] + [VMEM] * 8 + [ANY] * len(LOADS),
        out_specs=[ANY] * 5,
        scratch_shapes=[
            *scratch(KEEP), *scratch(KEEP), *scratch(LOADS), *scratch(WORK),
            pltpu.SemaphoreType.DMA((len(LOADS),)), pltpu.SemaphoreType.DMA((12,)),
        ],
        compiler_params=params(62),
        cost_estimate=cost(1.2e10, 3e7),
        name="layers",
    )(star_sizes, b_edge, b_out, ln1_gain, ln1_bias, b_ff1, b_ff2, ln2_gain, ln2_bias,
      *[loaded[name] for name in LOADS])

    mine = gather_chips(scatter_chips(add_cores(mine, other)))
    other = lax.ppermute(mine, "c", SWAP)

    def head():
        return shape((75, 2, D), F32)

    square = shape((D, 2, D), F32)
    wide = shape((D, 2, FF), F32)
    big = [shape((D, NCOL), F32), head(), head(), head(), square, wide, wide, square]
    stages = [
        pltpu.VMEM((COMMON, 128), BF16), pltpu.VMEM((2, D, 1152), F32),
        pltpu.VMEM((2, D, 256), F32), pltpu.VMEM((D, 256), F32),
        pltpu.VMEM((STRIP, LEFT), F32), pltpu.VMEM((4, D, 48), F32), pltpu.VMEM((4, D, 44), F32),
        pltpu.VMEM((6, 75, 44), F32),
    ]
    outs = pl.pallas_call(
        unpack_own,
        out_shape=[*big, shape((32, 128), F32), shape((LEFT_ROWS, 128), BF16)],
        in_specs=[ANY],
        out_specs=[ANY] * len(BIG) + [VMEM] * 2,
        scratch_shapes=[
            *stages, pltpu.VMEM((HEADS, 128), BF16), pltpu.VMEM((6, 75, 256), F32),
            pltpu.SemaphoreType.DMA((17,)), pltpu.SemaphoreType.DMA((5,)),
        ],
        compiler_params=params(30),
        cost_estimate=cost(1e8, 1e7),
        name="unpack_own",
    )(mine)
    outs = pl.pallas_call(
        unpack_other,
        out_shape=[*big, *[shape((2, n), F32) for n in SMALL.values()]],
        in_specs=[ANY, VMEM, VMEM] + [ANY] * len(BIG),
        out_specs=[ANY] * len(BIG) + [VMEM] * len(SMALL),
        scratch_shapes=[
            *stages, pltpu.VMEM((32, 128), F32), pltpu.SemaphoreType.DMA((19,)), pltpu.SemaphoreType.DMA((4,)),
        ],
        input_output_aliases={n + 3: n for n in range(len(BIG))},
        compiler_params=params(30),
        cost_estimate=cost(1e8, 1e7),
        name="unpack_other",
    )(other, outs[-2], outs[-1], *outs[:-2])
    table, wq, wk, wv, wo, w1, w2, we, b1, b2, g2, s2, g1, s1, bo, be = outs
    wq, wk, wv = (jnp.transpose(t, (1, 2, 0)) for t in (wq, wk, wv))
    wo, w1, we = (jnp.transpose(t, (1, 0, 2)) for t in (wo, w1, we))
    w2 = jnp.transpose(w2, (1, 2, 0))
    return (
        to_stars(nodes_out), to_stars(edges_out), to_stars(grad_nodes), table.T,
        wq, wk, wv, wo, bo, g1, s1, w1, b1, w2, b2, g2, s2, we, be,
    )


def solution(mesh):
    devices = mesh.devices.reshape(4, 4, 2, 2, 2)
    fine = Mesh(devices, ("x", "z", "yh", "yl", "c"))
    graphs = ("x", "z", "yh")
    heads = ("yl", "c")
    everyone = graphs + heads
    rows3 = P(everyone, None, None)
    rows2 = P(everyone, None)
    per_head = P(None, None, heads)
    return jax.shard_map(
        body,
        mesh=fine,
        in_specs=(
            rows3, P(), rows2, P(graphs), P(graphs, None), rows2, per_head, per_head, per_head,
            *[P()] * 12, rows3, rows3,
        ),
        out_specs=(rows3, rows3, rows3, P(), per_head, per_head, per_head, *[P()] * 12),
        check_vma=False,
    )
```
